32 devices in a mesh: sky: 8 (over z, x), band: 4 (over y, core).
Axes of the slice: x: 2, y: 2, z: 4, core: 2. Of those that a mesh axis runs over, the one named last changes fastest.
Arguments:
- raw_blocks: bfloat16 [168, 172032], P(None, ('sky', 'band')), may hold values from -6 to 6
- patch_of_block: int32 [1024, 1], P(('sky', 'band')), may hold values from 0 to 7; in each aligned block of 32 rows (0 to 31, 32 to 63, ...) at most 8 rows name the same one
- cell_of_block: int32 [1024], P(('sky', 'band')), may hold values from 0 to 15
- band_of_block: int32 [1024], P(('sky', 'band')), may hold values from 0 to 5
- block_weight: bfloat16 [1024], P(('sky', 'band')), may hold values from 0.25 to 4
- basis_coef: bfloat16 [1024, 3], P(('sky', 'band')), may hold values from 0.25 to 1
- row_basis: float32 [3, 41], replicated, may hold values from -1 to 1
- col_basis: float32 [3, 41], replicated, may hold values from -1 to 1
- band_gain: float32 [6], replicated, may hold values from 0.5 to 2
- filter_taps: float32 [41], replicated, may hold values from -1 to 1
Outputs:
- detection: float32 [8, 512, 512], P('sky', 'band')
The draws below stay inside these ranges and needn't reach their ends.
Inputs may be any that keep to these rules, and one draw needn't show every extreme that they name: `patch_of_block`: of the 32 blocks of one device at most 8 intersect one patch, and on some device exactly 8 do.
All inputs are finite; a program needn't handle non-finite values.
Results may differ from the reference program's by a relative error of at most 0.015.
Values may be sent and summed in bfloat16 or wider, within the bound.
No kernel may reach another device: no remote copies, remote signals or barrier semaphores. Data moves between devices by JAX's collectives and lax.ppermute only.
A program may use at most 128 MiB of HBM per device.

```python
import math
import jax
import jax.numpy as jnp
import numpy as np
from jax import lax

B = 128
KT = 41
R = 20
P_SIZE = 168
NBASIS = 3
BANDS = 6
CR = 4
CC = 4
CELLS = 16
BLK_DEV = 32
CAP = 8
BLOCKS = 1024
NPATCH = 8


def plant(result, own_key, smallest, high):
    longest = result.shape.index(max(result.shape))
    spots = []
    for shift in (0, 1):
        where = [jax.random.randint(jax.random.fold_in(own_key, axis), (), 0, length) for axis, length in enumerate(result.shape)]
        where[longest] = (where[longest] + shift) % result.shape[longest]
        spots.append(tuple(where))
    return result.at[spots[0]].set(smallest).at[spots[1]].set(high)


def levels(key, dims, split, least, top_value):
    def one(position, parts):
        draws = jax.random.uniform(jax.random.fold_in(jax.random.fold_in(key, 6), position), (parts,), jnp.float32, least / len(split), top_value / len(split))
        return jnp.repeat(jnp.exp(draws), dims[position] // parts).reshape((-1,) + (1,) * (len(dims) - position - 1))

    gain = one(*split[0])
    for cut in split[1:]:
        gain = gain * one(*cut)
    return gain


def shared_out(rng, own, number, rows, amount, top, reach, lean):
    ranking = jax.random.permutation(rng, amount)
    heavy_load, ordinary = portions_of(amount, rows * top, reach, lean, True), portions_of(amount, rows * top, reach, lean, False)
    places = jnp.arange(amount)

    def named(tallies, turn):
        used = int((tallies > 0).sum())
        fixed = max(1, used // 4)
        moved = fixed + (places - fixed + turn * (used - fixed)) % max(1, amount - fixed)
        return jnp.zeros((amount,), jnp.int32).at[ranking[jnp.where(places < fixed, places, moved)]].set(jnp.asarray(tallies, jnp.int32))

    tallies = jnp.where(number % 4 == 0, named(heavy_load, number // 4), named(ordinary, number - number // 4 - 1))
    mixed = jax.random.permutation(jax.random.fold_in(own, 3), amount)
    donor, sink = mixed[0:amount // 2 * 2:2], mixed[1:amount // 2 * 2:2]
    slack = jnp.minimum(tallies[donor] - 1, reach - tallies[sink]) // 2
    slack = jnp.where((donor == ranking[0]) | (sink == ranking[0]) | (tallies[sink] == 0), 0, jnp.maximum(slack, 0))
    moved = jax.random.randint(jax.random.fold_in(own, 4), (amount // 2,), 0, 1 << 20) % (slack + 1)
    tallies = tallies.at[donor].add(-moved).at[sink].add(moved)
    items = jnp.searchsorted(jnp.cumsum(tallies), jnp.arange(rows * top), side="right").astype(jnp.int32)
    grid = items.reshape(top, rows).T
    grid = grid[jax.random.permutation(jax.random.fold_in(own, 1), rows)]
    turn = jax.random.randint(jax.random.fold_in(own, 2), (rows, 1), 0, top)
    return jnp.take_along_axis(grid, (jnp.arange(top)[None, :] + turn) % top, axis=1)


def portions_of(amount, total, limit, skew, full):
    loads = [(1 << 20) // math.isqrt(grade ** skew) + 1 for grade in range(1, amount + 1)]
    largest = limit if full else min(limit, max(-(-total // amount), total * loads[0] // sum(loads)))
    least = 1 if total - largest >= amount - 1 else 0
    given, rest = [largest] + [least] * (amount - 1), total - largest - least * (amount - 1)
    while rest > 0:
        candidates = [i for i in range(1, amount) if given[i] < largest] or [i for i in range(1, amount) if given[i] < limit]
        whole, budget = sum([loads[i] for i in candidates]), rest
        for i in candidates:
            more = min(limit - given[i], max(1, budget * loads[i] // whole), rest)
            given[i] = given[i] + more
            rest = rest - more
    return np.array(given)


def gaussian(own_key, dims, width, limit, pieces=(), held_as=jnp.bfloat16):
    gain = levels(own_key, dims, pieces, -0.22, 0.18) if pieces else 1.0
    entries = jax.random.normal(own_key, dims, jnp.float32) * width * gain
    return jnp.minimum(jnp.maximum(entries, -limit), limit).astype(held_as)


def setup_inputs(seed: int = 0) -> dict:
    splits = jax.random.split(jax.random.key(seed), 11)
    raw_blocks = gaussian(splits[0], (P_SIZE, BLOCKS * P_SIZE), 1.0, 6.0, ((1, 32),))
    patch_of_block_keys = jax.random.split(jax.random.fold_in(splits[1], 1), BLOCKS // BLK_DEV)
    patch_of_block_turns = jax.random.permutation(jax.random.fold_in(splits[1], 3), BLOCKS // BLK_DEV)
    patch_of_block = jax.vmap(lambda own, number: shared_out(jax.random.fold_in(splits[1], 2), own, number, BLK_DEV, NPATCH, 1, CAP, 2))(patch_of_block_keys, patch_of_block_turns).reshape((BLOCKS, 1))
    cell_of_block = plant(jax.random.randint(splits[2], (BLOCKS,), 0, CELLS), jax.random.fold_in(splits[2], 1), 0, CELLS - 1).astype(jnp.int32)
    band_of_block = plant(jax.random.randint(splits[3], (BLOCKS,), 0, BANDS), jax.random.fold_in(splits[3], 1), 0, BANDS - 1).astype(jnp.int32)
    block_weight = jnp.clip(jnp.exp(math.log(4.0) - 2.7725887 * jax.random.uniform(splits[4], (BLOCKS,), jnp.float32) ** levels(splits[4], (BLOCKS,), ((0, 32),), -0.2, 0.2)), 0.25, 4.0).astype(jnp.bfloat16)
    basis_coef = jnp.clip(0.25 + 0.75 * jax.random.uniform(splits[5], (BLOCKS, NBASIS), jnp.float32) ** levels(splits[5], (BLOCKS, NBASIS), ((0, 32),), -0.2, 0.2), 0.25, 1.0).astype(jnp.bfloat16)
    row_basis = gaussian(splits[6], (NBASIS, KT), KT ** -0.5, 1.0, (), jnp.float32)
    col_basis = gaussian(splits[7], (NBASIS, KT), KT ** -0.5, 1.0, (), jnp.float32)
    band_gain = jnp.clip(jnp.exp(jax.random.uniform(splits[8], (BANDS,), jnp.float32, math.log(0.5), math.log(2.0))), 0.5, 2.0)
    filter_taps = gaussian(splits[9], (KT,), KT ** -0.5, 1.0, (), jnp.float32)
    return {"raw_blocks": raw_blocks, "patch_of_block": patch_of_block, "cell_of_block": cell_of_block, "band_of_block": band_of_block, "block_weight": block_weight, "basis_coef": basis_coef, "row_basis": row_basis, "col_basis": col_basis, "band_gain": band_gain, "filter_taps": filter_taps}


highest = lax.Precision.HIGHEST


def toeplitz(tap_values, rows_out):
    tap_count = tap_values.shape[0]
    period = jnp.concatenate([tap_values, jnp.zeros((rows_out,), tap_values.dtype)])
    flat_row = jnp.tile(period, rows_out)[: rows_out * (rows_out + tap_count - 1)]
    return flat_row.reshape(rows_out, rows_out + tap_count - 1)


def kernel_stack(basis_taps):
    stacked = jnp.stack([toeplitz(basis_taps[k], B) for k in range(NBASIS)])
    return lax.optimization_barrier(stacked.astype(jnp.bfloat16)).astype(jnp.float32)


def match_group(row_kernels, col_kernels, raw_group, coef_group):
    sectioned = jnp.einsum("kip,npq->nkiq", row_kernels, raw_group.astype(jnp.float32), precision=highest)
    sectioned = lax.optimization_barrier(sectioned.astype(jnp.bfloat16)).astype(jnp.float32)
    basis_terms = jnp.einsum("nkiq,kjq->nkij", sectioned, col_kernels, precision=highest)
    return jnp.sum(coef_group.astype(jnp.float32)[:, :, None, None] * basis_terms, axis=1).astype(jnp.bfloat16)


def reference(raw_blocks, patch_of_block, cell_of_block, band_of_block, block_weight, basis_coef, row_basis, col_basis, band_gain, filter_taps):
    row_kernels = kernel_stack(row_basis)
    col_kernels = kernel_stack(col_basis)
    groups = BLOCKS // BLK_DEV
    bin_total = NPATCH * BANDS * CELLS
    target_bin = (patch_of_block[:, 0] * (BANDS * CELLS) + band_of_block * CELLS + cell_of_block).astype(jnp.int32)
    block_major = raw_blocks.reshape(P_SIZE, BLOCKS, P_SIZE).transpose(1, 0, 2)

    def accumulate(totals, inputs):
        raw_group, coef_group, weight_group, bin_group = inputs
        matched = match_group(row_kernels, col_kernels, raw_group, coef_group)
        contrib = matched.astype(jnp.float32) * weight_group.astype(jnp.float32)[:, None, None]
        return totals.at[bin_group].add(contrib), None

    totals, unused = lax.scan(
        accumulate,
        jnp.zeros((bin_total, B, B), jnp.float32),
        (block_major.reshape(groups, BLK_DEV, P_SIZE, P_SIZE), basis_coef.reshape(groups, BLK_DEV, NBASIS),
         block_weight.reshape(groups, BLK_DEV), target_bin.reshape(groups, BLK_DEV)))
    weight_sum = jax.ops.segment_sum(block_weight.astype(jnp.float32), target_bin, num_segments=bin_total)
    grid_shape = (NPATCH, BANDS, CR, CC)
    coadd_image = totals.reshape(grid_shape + (B, B)) / jnp.maximum(weight_sum.reshape(grid_shape), 1.0)[..., None, None]
    combined = jnp.sum(band_gain[None, :, None, None, None, None] * coadd_image, axis=1)
    patch_image = combined.transpose(0, 1, 3, 2, 4).reshape(NPATCH, CR * B, CC * B)
    patch_image = lax.optimization_barrier(patch_image.astype(jnp.bfloat16)).astype(jnp.float32)
    padded = jnp.pad(patch_image, ((0, 0), (R, R), (0, 0)))
    filter_round = lax.optimization_barrier(filter_taps.astype(jnp.bfloat16)).astype(jnp.float32)
    row_filter = toeplitz(filter_round, CR * B)
    col_filter = toeplitz(filter_round, CC * B)[:, R:R + CC * B].T
    smoothed = jnp.einsum("ij,pjx->pix", row_filter, padded, precision=highest)
    smoothed = lax.optimization_barrier(smoothed.astype(jnp.bfloat16)).astype(jnp.float32)
    return jnp.einsum("pix,xl->pil", smoothed, col_filter, precision=highest)
```

```python
import functools

import jax
import jax.numpy as jnp
from jax import lax
from jax.experimental import pallas as pl
from jax.experimental.pallas import tpu as pltpu
from jax.sharding import PartitionSpec as P

BANDS = 6
CR = 4
CC = 4
CELLS = 16
VMEM = pltpu.VMEM
SMEM = pltpu.SMEM


def up(value, unit):
    return -(-value // unit) * unit


def banded(row, rows, width):
    tile = pltpu.roll(jnp.broadcast_to(row, (8, width)), 0, 1, stride=1, stride_axis=0)
    return jnp.concatenate([tile if i == 0 else pltpu.roll(tile, 8 * i, 1) for i in range(rows // 8)], axis=0)


def lanes_at(row, start, width):
    parts = [row, jnp.zeros((1, width - start - row.shape[1]), row.dtype)]
    if start:
        parts.insert(0, jnp.zeros((1, start), row.dtype))
    return jnp.concatenate(parts, axis=1)


def match_kernel(coef_ref, raw_ref, row_ref, col_ref, out_ref, rowk_ref, colk_ref):
    margin_side = raw_ref.shape[0]
    basis_count = row_ref.shape[0]
    block_count, block_side, unused = out_ref.shape
    width = colk_ref.shape[0] // basis_count
    for k in range(basis_count):
        rows = banded(lanes_at(row_ref[k : k + 1, :], 0, width), block_side, width)
        rowk_ref[k * block_side : (k + 1) * block_side, :] = rows[:, :margin_side].astype(jnp.bfloat16)
        cols = banded(lanes_at(col_ref[k : k + 1, :], 0, width), block_side, width)
        colk_ref[k * width : (k + 1) * width, :] = cols.T.astype(jnp.bfloat16)
    for n in range(block_count):
        block = raw_ref[:, n * margin_side : (n + 1) * margin_side]
        sectioned = jnp.dot(rowk_ref[...], block, preferred_element_type=jnp.float32)
        total = None
        for k in range(basis_count):
            part = (sectioned[k * block_side : (k + 1) * block_side] * coef_ref[n, k]).astype(jnp.bfloat16)
            term = jnp.dot(
                part,
                colk_ref[k * width : k * width + margin_side, :],
                preferred_element_type=jnp.float32,
            )
            total = term if total is None else total + term
        out_ref[n] = total.astype(jnp.bfloat16)


def match_blocks(raw_blocks, coef, row_basis, col_basis, block_side):
    margin_side = raw_blocks.shape[0]
    block_count = raw_blocks.shape[1] // margin_side
    basis_count = row_basis.shape[0]
    width = up(margin_side, 128)
    flops = 2 * block_count * basis_count * block_side * margin_side * (margin_side + block_side)
    return pl.pallas_call(
        match_kernel,
        out_shape=jax.ShapeDtypeStruct((block_count, block_side, block_side), jnp.bfloat16),
        in_specs=[
            pl.BlockSpec(memory_space=SMEM),
            pl.BlockSpec(memory_space=VMEM),
            pl.BlockSpec(memory_space=VMEM),
            pl.BlockSpec(memory_space=VMEM),
        ],
        out_specs=pl.BlockSpec(memory_space=VMEM),
        scratch_shapes=[
            VMEM((basis_count * block_side, margin_side), jnp.bfloat16),
            VMEM((basis_count * width, block_side), jnp.bfloat16),
        ],
        compiler_params=pltpu.CompilerParams(vmem_limit_bytes=32 << 20),
        cost_estimate=pl.CostEstimate(flops=2 * flops, bytes_accessed=4 << 20, transcendentals=0),
        name="match_blocks",
    )(coef, raw_blocks, row_basis, col_basis)


def bin_kernel(bins_ref, scale_ref, own_ref, other_ref, *rest):
    outs, acc_ref = rest[:-1], rest[-1]
    step = outs[0].shape[0]
    chunk = pl.program_id(0)
    acc_ref[...] = jnp.zeros_like(acc_ref)
    for source, blocks_ref in enumerate((own_ref, other_ref)):

        def add(n, carry, source=source, blocks_ref=blocks_ref):
            place = bins_ref[source, n] - chunk * step
            group = bins_ref[source + 2, n]

            @pl.when((place >= 0) & (place < step) & (group >= 0))
            def _():
                slot = group * step + place
                acc_ref[slot] += scale_ref[source, n] * blocks_ref[n].astype(jnp.float32)

            return carry

        lax.fori_loop(0, blocks_ref.shape[0], add, 0)
    for index, out_ref in enumerate(outs):
        out_ref[...] = acc_ref[index * step : (index + 1) * step].astype(out_ref.dtype)


def bin_blocks(bins, scale, own, other, groups, size, name):
    block_side = own.shape[1]
    step = min(size, 16)
    whole = pl.BlockSpec(own.shape, lambda g: (0, 0, 0))
    part = pl.BlockSpec((step, block_side, block_side), lambda g: (g, 0, 0))
    shape = jax.ShapeDtypeStruct((size, block_side, block_side), jnp.bfloat16)
    return pl.pallas_call(
        bin_kernel,
        grid=(size // step,),
        out_shape=[shape] * groups,
        in_specs=[pl.BlockSpec(memory_space=SMEM), pl.BlockSpec(memory_space=SMEM), whole, whole],
        out_specs=[part] * groups,
        scratch_shapes=[VMEM((groups * step, block_side, block_side), jnp.float32)],
        compiler_params=pltpu.CompilerParams(vmem_limit_bytes=40 << 20),
        cost_estimate=pl.CostEstimate(
            flops=4 * own.size, bytes_accessed=4 * own.size + 2 * groups * size * block_side**2, transcendentals=0
        ),
        name=name,
    )(bins, scale, own, other)


def filter_kernel(taps_ref, mid_ref, low_ref, high_ref, out_ref):
    cells, side, unused = mid_ref.shape
    edge = low_ref.shape[1]
    tap_count = taps_ref.shape[1]
    radius = (tap_count - 1) // 2
    taps = taps_ref[...]
    rows_in = side + 2 * edge
    row_filter = banded(lanes_at(taps, edge - radius, up(rows_in + 1, 128)), side, up(rows_in + 1, 128))
    row_filter = row_filter[:, :rows_in].astype(jnp.bfloat16)
    col_filter = banded(lanes_at(taps, side - radius, 3 * side), side, 3 * side).astype(jnp.bfloat16).T
    zero = jnp.zeros((side, side), jnp.bfloat16)
    smoothed = [zero]
    for c in range(cells):
        column = jnp.concatenate([low_ref[c], mid_ref[c], high_ref[c]], axis=0)
        smoothed.append(jnp.dot(row_filter, column, preferred_element_type=jnp.float32).astype(jnp.bfloat16))
    smoothed.append(zero)
    for c in range(cells):
        window = jnp.concatenate(smoothed[c : c + 3], axis=1)
        out_ref[:, c * side : (c + 1) * side] = jnp.dot(window, col_filter, preferred_element_type=jnp.float32)


def detect(taps, mid, low, high):
    cells, side, unused = mid.shape
    return pl.pallas_call(
        filter_kernel,
        out_shape=jax.ShapeDtypeStruct((side, cells * side), jnp.float32),
        in_specs=[pl.BlockSpec(memory_space=VMEM)] * 4,
        out_specs=pl.BlockSpec(memory_space=VMEM),
        compiler_params=pltpu.CompilerParams(vmem_limit_bytes=32 << 20),
        name="detect",
    )(taps, mid, low, high)


def swap(array, axis, bit):
    count = lax.axis_size(axis)
    return lax.ppermute(array, axis, [(i, i ^ (1 << bit)) for i in range(count)])


def halves(parts, send):
    total = None
    for part in parts:
        half = part.shape[0] // 2
        piece = part[half:] if send else part[:half]
        piece = piece.astype(jnp.float32)
        total = piece if total is None else total + piece
    return total


def local(
    raw_blocks,
    patch_of_block,
    cell_of_block,
    band_of_block,
    block_weight,
    basis_coef,
    row_basis,
    col_basis,
    band_gain,
    filter_taps,
):
    sky_count = lax.axis_size("sky")
    band_count = lax.axis_size("band")
    sky_bits = sky_count.bit_length() - 1
    band_bits = band_count.bit_length() - 1
    margin_side = raw_blocks.shape[0]
    block_count = raw_blocks.shape[1] // margin_side
    radius = (filter_taps.shape[0] - 1) // 2
    block_side = margin_side - 2 * radius
    sky_here = lax.axis_index("sky")
    band_here = lax.axis_index("band")

    key = (patch_of_block[:, 0] * BANDS + band_of_block) * CELLS + cell_of_block
    facts = jnp.stack([key.astype(jnp.float32), block_weight.astype(jnp.float32)])
    all_facts = lax.all_gather(facts, ("sky", "band"), axis=0)

    matched = match_blocks(raw_blocks, basis_coef.astype(jnp.float32), row_basis, col_basis, block_side)
    from_pair = swap(matched, "band", 0)

    here = sky_here * band_count + band_here
    pair = jnp.stack([here, here ^ 1])
    near = jnp.concatenate(
        [lax.dynamic_slice_in_dim(all_facts, here, 1, 0), lax.dynamic_slice_in_dim(all_facts, here ^ 1, 1, 0)]
    )
    near_key, near_weight = near[:, 0], near[:, 1]
    same = near_key[:, :, None, None] == all_facts[None, None, :, 0]
    weight_sum = jnp.sum(jnp.where(same, all_facts[None, None, :, 1], 0.0), axis=(2, 3))
    near_key = near_key.astype(jnp.int32)
    cell = near_key % CELLS
    band = near_key // CELLS % BANDS
    gain = jnp.sum(jnp.where(band[..., None] == jnp.arange(BANDS), band_gain, 0.0), axis=2)
    scale = gain * near_weight / jnp.maximum(weight_sum, 1.0)

    sky_off = near_key // (CELLS * BANDS) ^ sky_here
    band_off = cell // CC ^ band_here
    column = cell % CC
    half_columns = CC // 2
    sky_low = sky_off & 1
    sky_rest = jnp.zeros_like(sky_off)
    for bit in range(1, sky_bits):
        sky_rest = sky_rest * 2 + (sky_off >> bit & 1)
    band_rest = jnp.zeros_like(band_off)
    for bit in range(1, band_bits):
        band_rest = band_rest * 2 + (band_off >> bit & 1)
    rest_count = sky_count // 2
    row_count = band_count // 2
    side_a = (band_rest * 2 + sky_low) * rest_count + sky_rest
    side_b = (sky_low * row_count + band_rest) * rest_count + sky_rest
    second = column >= half_columns
    place = jnp.where(second, side_b, side_a) * half_columns + column % half_columns
    size = sky_count * row_count * half_columns // 2
    mine = band_off & 1 == 0
    sent = place >= size
    place = place % size
    group = second.astype(jnp.int32)
    sent_bins = jnp.concatenate([place, jnp.where(mine & sent, group, -1)])
    kept_bins = jnp.concatenate([place, jnp.where(mine & ~sent, group, -1)])

    send_a, send_b = bin_blocks(sent_bins, scale, matched, from_pair, 2, size, "bins_sent")
    steps_a = [("band", bit) for bit in range(1, band_bits)] + [("sky", 0)]
    steps_b = [("sky", 0)] + [("band", bit) for bit in range(1, band_bits)]
    got_a, got_b = swap(send_a, *steps_a[0]), swap(send_b, *steps_b[0])
    keep_a, keep_b = bin_blocks(kept_bins, scale, matched, from_pair, 2, size, "bins_kept")
    parts_a, parts_b = [keep_a, got_a], [keep_b, got_b]
    for step_a, step_b in zip(steps_a[1:], steps_b[1:]):
        got_a = swap(halves(parts_a, True).astype(jnp.bfloat16), *step_a)
        got_b = swap(halves(parts_b, True).astype(jnp.bfloat16), *step_b)
        parts_a = [part[: part.shape[0] // 2] for part in parts_a] + [got_a]
        parts_b = [part[: part.shape[0] // 2] for part in parts_b] + [got_b]

    def by_sky(part):
        return part.reshape((rest_count, half_columns) + part.shape[1:])

    parts_a, parts_b = [by_sky(part) for part in parts_a], [by_sky(part) for part in parts_b]
    later = []
    for bit in range(1, sky_bits):
        outgoing = jnp.concatenate([halves(parts_a, True), halves(parts_b, True)], axis=1)
        for part in later:
            outgoing = outgoing + part[part.shape[0] // 2 :].astype(jnp.float32)
        got = swap(outgoing.astype(jnp.bfloat16), "sky", bit)
        parts_a = [part[: part.shape[0] // 2] for part in parts_a]
        parts_b = [part[: part.shape[0] // 2] for part in parts_b]
        later = [part[: part.shape[0] // 2] for part in later] + [got]

    def full(parts):
        return functools.reduce(jnp.add, [part.astype(jnp.float32) for part in parts])

    combined = jnp.concatenate([full(parts_a), full(parts_b)], axis=1) + full(later)
    combined = combined[0].astype(jnp.bfloat16)

    edge = up(radius, 16)
    forward = [(i, i + 1) for i in range(band_count - 1)]
    backward = [(i + 1, i) for i in range(band_count - 1)]
    low = lax.ppermute(combined[:, block_side - edge :], "band", forward)
    high = lax.ppermute(combined[:, :edge], "band", backward)
    taps = filter_taps.astype(jnp.bfloat16).astype(jnp.float32)[None]
    return detect(taps, combined, low, high)[None]


def solution(mesh):
    return jax.shard_map(
        local,
        mesh=mesh,
        in_specs=(
            P(None, ("sky", "band")),
            P(("sky", "band"), None),
            P(("sky", "band")),
            P(("sky", "band")),
            P(("sky", "band")),
            P(("sky", "band"), None),
            P(),
            P(),
            P(),
            P(),
        ),
        out_specs=P("sky", "band", None),
        check_vma=False,
    )
```

```python
import functools

import jax
import jax.numpy as jnp
from jax import lax
from jax.experimental import pallas as pl
from jax.experimental.pallas import tpu as pltpu
from jax.sharding import PartitionSpec as P

BANDS = 6
CR = 4
CC = 4
CELLS = 16
VMEM = pltpu.VMEM
SMEM = pltpu.SMEM


def up(value, unit):
    return -(-value // unit) * unit


def banded(row, rows, width):
    tile = pltpu.roll(jnp.broadcast_to(row, (8, width)), 0, 1, stride=1, stride_axis=0)
    return jnp.concatenate([tile if i == 0 else pltpu.roll(tile, 8 * i, 1) for i in range(rows // 8)], axis=0)


def lanes_at(row, start, width):
    parts = [row, jnp.zeros((1, width - start - row.shape[1]), row.dtype)]
    if start:
        parts.insert(0, jnp.zeros((1, start), row.dtype))
    return jnp.concatenate(parts, axis=1)


def match_part(raw_ref, coef_ref, rowk_ref, colk_ref, out_ref):
    margin_side = raw_ref.shape[0]
    basis_count = coef_ref.shape[1]
    block_count, block_side, unused = out_ref.shape
    width = colk_ref.shape[0] // basis_count
    coef = coef_ref[...].astype(jnp.float32)
    for n in range(block_count):
        block = raw_ref[:, n * margin_side : (n + 1) * margin_side]
        sectioned = jnp.dot(rowk_ref[...], block, preferred_element_type=jnp.float32)
        total = None
        for k in range(basis_count):
            part = sectioned[k * block_side : (k + 1) * block_side] * coef[n : n + 1, k : k + 1]
            term = jnp.dot(
                part.astype(jnp.bfloat16),
                colk_ref[k * width : k * width + margin_side, :],
                preferred_element_type=jnp.float32,
            )
            total = term if total is None else total + term
        out_ref[n] = total.astype(jnp.bfloat16)


def match_first(coef_ref, raw_ref, row_ref, col_ref, out_ref, rowk_ref, colk_ref):
    basis_count = row_ref.shape[0]
    margin_side = raw_ref.shape[0]
    block_side = out_ref.shape[1]
    width = colk_ref.shape[0] // basis_count
    for k in range(basis_count):
        rows = banded(lanes_at(row_ref[k : k + 1, :], 0, width), block_side, width)
        rowk_ref[k * block_side : (k + 1) * block_side, :] = rows[:, :margin_side].astype(jnp.bfloat16)
        cols = banded(lanes_at(col_ref[k : k + 1, :], 0, width), block_side, width)
        colk_ref[k * width : (k + 1) * width, :] = cols.T.astype(jnp.bfloat16)
    match_part(raw_ref, coef_ref, rowk_ref, colk_ref, out_ref)


def match_next(coef_ref, raw_ref, rowk_ref, colk_ref, out_ref):
    match_part(raw_ref, coef_ref, rowk_ref, colk_ref, out_ref)


def match_blocks(raw_blocks, coef, row_basis, col_basis, block_side):
    margin_side = raw_blocks.shape[0]
    block_count = raw_blocks.shape[1] // margin_side
    basis_count = row_basis.shape[0]
    width = up(margin_side, 128)
    count = 16 if block_count % 16 == 0 else block_count
    flops = 2 * count * basis_count * block_side * margin_side * (margin_side + block_side)

    def fixed(*place):
        return lambda g: place

    whole = [
        pl.BlockSpec((basis_count * block_side, margin_side), fixed(0, 0)),
        pl.BlockSpec((basis_count * width, block_side), fixed(0, 0)),
    ]
    out_spec = pl.BlockSpec((count, block_side, block_side), fixed(0, 0, 0))
    out_shape = jax.ShapeDtypeStruct((count, block_side, block_side), jnp.bfloat16)
    results, kernels = [], ()
    for part in range(block_count // count):
        first = part == 0
        basis = pl.BlockSpec(row_basis.shape, fixed(0, 0))
        found = pl.pallas_call(
            match_first if first else match_next,
            grid=(1,),
            out_shape=[
                out_shape,
                jax.ShapeDtypeStruct((basis_count * block_side, margin_side), jnp.bfloat16),
                jax.ShapeDtypeStruct((basis_count * width, block_side), jnp.bfloat16),
            ] if first else [out_shape],
            in_specs=[
                pl.BlockSpec((count, basis_count), fixed(part, 0)),
                pl.BlockSpec((margin_side, count * margin_side), fixed(0, part)),
            ] + ([basis, basis] if first else whole),
            out_specs=[out_spec] + (whole if first else []),
            compiler_params=pltpu.CompilerParams(vmem_limit_bytes=40 << 20),
            cost_estimate=pl.CostEstimate(flops=2 * flops, bytes_accessed=2 << 20, transcendentals=0),
            name="match_blocks",
        )(coef, raw_blocks, *((row_basis, col_basis) if first else kernels))
        results.append(found[0])
        kernels = kernels or tuple(found[1:])
    return results


def bin_kernel(sources, bins_ref, scale_ref, *rest):
    blocks_refs, outs, acc_ref = rest[:sources], rest[sources:-1], rest[-1]
    step = outs[0].shape[0]
    chunk = pl.program_id(0)
    acc_ref[...] = jnp.zeros_like(acc_ref)
    for source, blocks_ref in enumerate(blocks_refs):

        def add(n, carry, source=source, blocks_ref=blocks_ref):
            place = bins_ref[source, n] - chunk * step
            group = bins_ref[source + sources, n]

            @pl.when((place >= 0) & (place < step) & (group >= 0))
            def _():
                slot = group * step + place
                acc_ref[slot] += scale_ref[source, n] * blocks_ref[n].astype(jnp.float32)

            return carry

        lax.fori_loop(0, blocks_ref.shape[0], add, 0)
    for index, out_ref in enumerate(outs):
        out_ref[...] = acc_ref[index * step : (index + 1) * step].astype(out_ref.dtype)


def bin_blocks(bins, scale, blocks, groups, size, name):
    count, block_side, unused = blocks[0].shape
    step = min(size, 16)
    whole = pl.BlockSpec(blocks[0].shape, lambda g: (0, 0, 0))
    part = pl.BlockSpec((step, block_side, block_side), lambda g: (g, 0, 0))
    shape = jax.ShapeDtypeStruct((size, block_side, block_side), jnp.bfloat16)
    moved = 2 * len(blocks) * blocks[0].size + 2 * groups * size * block_side**2
    return pl.pallas_call(
        functools.partial(bin_kernel, len(blocks)),
        grid=(size // step,),
        out_shape=[shape] * groups,
        in_specs=[pl.BlockSpec(memory_space=SMEM), pl.BlockSpec(memory_space=SMEM)] + [whole] * len(blocks),
        out_specs=[part] * groups,
        scratch_shapes=[VMEM((groups * step, block_side, block_side), jnp.float32)],
        compiler_params=pltpu.CompilerParams(vmem_limit_bytes=40 << 20),
        cost_estimate=pl.CostEstimate(flops=2 * moved, bytes_accessed=moved, transcendentals=0),
        name=name,
    )(bins, scale, *blocks)


def filter_kernel(taps_ref, mid_ref, low_ref, high_ref, out_ref):
    cells, side, unused = mid_ref.shape
    edge = low_ref.shape[1]
    tap_count = taps_ref.shape[1]
    radius = (tap_count - 1) // 2
    taps = taps_ref[...]
    rows_in = side + 2 * edge
    row_filter = banded(lanes_at(taps, edge - radius, up(rows_in + 1, 128)), side, up(rows_in + 1, 128))
    row_filter = row_filter[:, :rows_in].astype(jnp.bfloat16)
    col_filter = banded(lanes_at(taps, side - radius, 3 * side), side, 3 * side).astype(jnp.bfloat16).T
    zero = jnp.zeros((side, side), jnp.bfloat16)
    smoothed = [zero]
    for c in range(cells):
        column = jnp.concatenate([low_ref[c], mid_ref[c], high_ref[c]], axis=0)
        smoothed.append(jnp.dot(row_filter, column, preferred_element_type=jnp.float32).astype(jnp.bfloat16))
    smoothed.append(zero)
    for c in range(cells):
        window = jnp.concatenate(smoothed[c : c + 3], axis=1)
        out_ref[:, c * side : (c + 1) * side] = jnp.dot(window, col_filter, preferred_element_type=jnp.float32)


def detect(taps, mid, low, high):
    cells, side, unused = mid.shape
    return pl.pallas_call(
        filter_kernel,
        out_shape=jax.ShapeDtypeStruct((side, cells * side), jnp.float32),
        in_specs=[pl.BlockSpec(memory_space=VMEM)] * 4,
        out_specs=pl.BlockSpec(memory_space=VMEM),
        compiler_params=pltpu.CompilerParams(vmem_limit_bytes=32 << 20),
        name="detect",
    )(taps, mid, low, high)


def swap(array, axis, bit):
    count = lax.axis_size(axis)
    return lax.ppermute(array, axis, [(i, i ^ (1 << bit)) for i in range(count)])


def halves(parts, send):
    total = None
    for part in parts:
        half = part.shape[0] // 2
        piece = part[half:] if send else part[:half]
        piece = piece.astype(jnp.float32)
        total = piece if total is None else total + piece
    return total


def local(
    raw_blocks,
    patch_of_block,
    cell_of_block,
    band_of_block,
    block_weight,
    basis_coef,
    row_basis,
    col_basis,
    band_gain,
    filter_taps,
):
    sky_count = lax.axis_size("sky")
    band_count = lax.axis_size("band")
    sky_bits = sky_count.bit_length() - 1
    band_bits = band_count.bit_length() - 1
    margin_side = raw_blocks.shape[0]
    block_count = raw_blocks.shape[1] // margin_side
    radius = (filter_taps.shape[0] - 1) // 2
    block_side = margin_side - 2 * radius
    sky_here = lax.axis_index("sky")
    band_here = lax.axis_index("band")

    key = (patch_of_block[:, 0] * BANDS + band_of_block) * CELLS + cell_of_block
    facts = jnp.stack([key.astype(jnp.float32), block_weight.astype(jnp.float32)])[None]
    for axis, bits in (("band", band_bits), ("sky", sky_bits)):
        for bit in range(bits):
            facts = jnp.concatenate([facts, swap(facts, axis, bit)])

    matched = match_blocks(raw_blocks, basis_coef, row_basis, col_basis, block_side)
    from_pair = [swap(part, "band", 0) for part in matched]

    near_key, near_weight = facts[:2, 0], facts[:2, 1]
    same = near_key[:, :, None, None] == facts[None, None, :, 0]
    weight_sum = jnp.sum(jnp.where(same, facts[None, None, :, 1], 0.0), axis=(2, 3))
    near_key = near_key.astype(jnp.int32)
    cell = near_key % CELLS
    band = near_key // CELLS % BANDS
    gain = jnp.sum(jnp.where(band[..., None] == jnp.arange(BANDS), band_gain, 0.0), axis=2)
    scale = gain * near_weight / jnp.maximum(weight_sum, 1.0)

    sky_off = near_key // (CELLS * BANDS) ^ sky_here
    band_off = cell // CC ^ band_here
    column = cell % CC
    half_columns = CC // 2
    sky_low = sky_off & 1
    sky_rest = jnp.zeros_like(sky_off)
    for bit in range(1, sky_bits):
        sky_rest = sky_rest * 2 + (sky_off >> bit & 1)
    band_rest = jnp.zeros_like(band_off)
    for bit in range(1, band_bits):
        band_rest = band_rest * 2 + (band_off >> bit & 1)
    rest_count = sky_count // 2
    row_count = band_count // 2
    side_a = (band_rest * 2 + sky_low) * rest_count + sky_rest
    side_b = (sky_low * row_count + band_rest) * rest_count + sky_rest
    second = column >= half_columns
    place = jnp.where(second, side_b, side_a) * half_columns + column % half_columns
    size = sky_count * row_count * half_columns // 2
    mine = band_off & 1 == 0
    sent = place >= size
    place = place % size
    group = second.astype(jnp.int32)
    near_blocks = matched + from_pair
    scale, place, sent_group, kept_group = (
        value.reshape(len(near_blocks), -1)
        for value in (scale, place, jnp.where(mine & sent, group, -1), jnp.where(mine & ~sent, group, -1))
    )
    sent_bins = jnp.concatenate([place, sent_group])
    kept_bins = jnp.concatenate([place, kept_group])

    send_a, send_b = bin_blocks(sent_bins, scale, near_blocks, 2, size, "bins_sent")
    steps_a = [("band", bit) for bit in range(1, band_bits)] + [("sky", 0)]
    steps_b = [("sky", 0)] + [("band", bit) for bit in range(1, band_bits)]
    got_a, got_b = swap(send_a, *steps_a[0]), swap(send_b, *steps_b[0])
    keep_a, keep_b = bin_blocks(kept_bins, scale, near_blocks, 2, size, "bins_kept")
    parts_a, parts_b = [keep_a, got_a], [keep_b, got_b]
    for step_a, step_b in zip(steps_a[1:], steps_b[1:]):
        got_a = swap(halves(parts_a, True).astype(jnp.bfloat16), *step_a)
        got_b = swap(halves(parts_b, True).astype(jnp.bfloat16), *step_b)
        parts_a = [part[: part.shape[0] // 2] for part in parts_a] + [got_a]
        parts_b = [part[: part.shape[0] // 2] for part in parts_b] + [got_b]

    def by_sky(part):
        return part.reshape((rest_count, half_columns) + part.shape[1:])

    parts_a, parts_b = [by_sky(part) for part in parts_a], [by_sky(part) for part in parts_b]
    later = []
    for bit in range(1, sky_bits):
        outgoing = jnp.concatenate([halves(parts_a, True), halves(parts_b, True)], axis=1)
        for part in later:
            outgoing = outgoing + part[part.shape[0] // 2 :].astype(jnp.float32)
        got = swap(outgoing.astype(jnp.bfloat16), "sky", bit)
        parts_a = [part[: part.shape[0] // 2] for part in parts_a]
        parts_b = [part[: part.shape[0] // 2] for part in parts_b]
        later = [part[: part.shape[0] // 2] for part in later] + [got]

    def full(parts):
        return functools.reduce(jnp.add, [part.astype(jnp.float32) for part in parts])

    combined = jnp.concatenate([full(parts_a), full(parts_b)], axis=1) + full(later)
    combined = combined[0].astype(jnp.bfloat16)

    edge = up(radius, 16)
    forward = [(i, i + 1) for i in range(band_count - 1)]
    backward = [(i + 1, i) for i in range(band_count - 1)]
    low = lax.ppermute(combined[:, block_side - edge :], "band", forward)
    high = lax.ppermute(combined[:, :edge], "band", backward)
    taps = filter_taps.astype(jnp.bfloat16).astype(jnp.float32)[None]
    return detect(taps, combined, low, high)[None]


def solution(mesh):
    return jax.shard_map(
        local,
        mesh=mesh,
        in_specs=(
            P(None, ("sky", "band")),
            P(("sky", "band"), None),
            P(("sky", "band")),
            P(("sky", "band")),
            P(("sky", "band")),
            P(("sky", "band"), None),
            P(),
            P(),
            P(),
            P(),
        ),
        out_specs=P("sky", "band", None),
        check_vma=False,
    )
```

```python
import functools

import jax
import jax.numpy as jnp
from jax import lax
from jax.experimental import pallas as pl
from jax.experimental.pallas import tpu as pltpu
from jax.sharding import PartitionSpec as P

BANDS = 6
CR = 4
CC = 4
CELLS = 16
VMEM = pltpu.VMEM
SMEM = pltpu.SMEM


def up(value, unit):
    return -(-value // unit) * unit


def banded(row, rows, width):
    tile = pltpu.roll(jnp.broadcast_to(row, (8, width)), 0, 1, stride=1, stride_axis=0)
    return jnp.concatenate([tile if i == 0 else pltpu.roll(tile, 8 * i, 1) for i in range(rows // 8)], axis=0)


def lanes_at(row, start, width):
    parts = [row, jnp.zeros((1, width - start - row.shape[1]), row.dtype)]
    if start:
        parts.insert(0, jnp.zeros((1, start), row.dtype))
    return jnp.concatenate(parts, axis=1)


def match_part(first, raw_ref, coef_ref, rowk_ref, colk_ref, out_ref):
    margin_side = raw_ref.shape[0]
    basis_count = coef_ref.shape[0]
    count, block_side, unused = out_ref.shape
    width = colk_ref.shape[0] // basis_count
    for n in range(count):
        here = first + n
        block = raw_ref[:, here * margin_side : (here + 1) * margin_side]
        sectioned = jnp.dot(rowk_ref[...], block, preferred_element_type=jnp.float32)
        total = None
        for k in range(basis_count):
            part = sectioned[k * block_side : (k + 1) * block_side] * coef_ref[k : k + 1, here : here + 1]
            term = jnp.dot(
                part.astype(jnp.bfloat16),
                colk_ref[k * width : k * width + margin_side, :],
                preferred_element_type=jnp.float32,
            )
            total = term if total is None else total + term
        out_ref[n] = total.astype(jnp.bfloat16)


def match_first(
    coef_hbm, raw_hbm, row_hbm, col_hbm, out_ref, raw_ref, coef_ref, rowk_ref, colk_ref, coef_in, row_ref, col_ref, sems
):
    basis_count = row_ref.shape[0]
    margin_side = raw_ref.shape[0]
    count, block_side, unused = out_ref.shape
    width = colk_ref.shape[0] // basis_count
    cut = min(up(count * margin_side, 128), raw_ref.shape[1])
    small = [
        pltpu.make_async_copy(source, target, sems.at[i])
        for i, (source, target) in enumerate(((row_hbm, row_ref), (col_hbm, col_ref), (coef_hbm, coef_in)))
    ]
    large = [
        pltpu.make_async_copy(raw_hbm.at[:, low:high], raw_ref.at[:, low:high], sems.at[3 + i])
        for i, (low, high) in enumerate(((0, cut), (cut, raw_ref.shape[1])))
        if high > low
    ]
    for copy in small + large:
        copy.start()
    for copy in small:
        copy.wait()
    coef_ref[...] = coef_in[...].astype(jnp.float32)
    for k in range(basis_count):
        rows = banded(lanes_at(row_ref[k : k + 1, :], 0, width), block_side, width)
        rowk_ref[k * block_side : (k + 1) * block_side, :] = rows[:, :margin_side].astype(jnp.bfloat16)
        cols = banded(lanes_at(col_ref[k : k + 1, :], 0, width), block_side, width)
        colk_ref[k * width : (k + 1) * width, :] = cols.T.astype(jnp.bfloat16)
    large[0].wait()
    match_part(0, raw_ref, coef_ref, rowk_ref, colk_ref, out_ref)
    for copy in large[1:]:
        copy.wait()


def match_next(first, after_ref, raw_ref, coef_ref, rowk_ref, colk_ref, out_ref):
    match_part(first, raw_ref, coef_ref, rowk_ref, colk_ref, out_ref)


def match_blocks(first, count, operands, block_side, after):
    raw = operands[1] if first == 0 else operands[0]
    margin_side = raw.shape[0]
    basis_count = operands[0].shape[0] if first == 0 else operands[1].shape[0]
    width = up(margin_side, 128)
    flops = 2 * count * basis_count * block_side * margin_side * (margin_side + block_side)
    out_shape = [jax.ShapeDtypeStruct((count, block_side, block_side), jnp.bfloat16)]
    scratch = []
    if first == 0:
        coef, raw, row_basis, col_basis = operands
        out_shape += [
            jax.ShapeDtypeStruct(raw.shape, raw.dtype),
            jax.ShapeDtypeStruct(coef.shape, jnp.float32),
            jax.ShapeDtypeStruct((basis_count * block_side, margin_side), jnp.bfloat16),
            jax.ShapeDtypeStruct((basis_count * width, block_side), jnp.bfloat16),
        ]
        scratch = [
            VMEM(coef.shape, coef.dtype),
            VMEM(row_basis.shape, row_basis.dtype),
            VMEM(col_basis.shape, col_basis.dtype),
            pltpu.SemaphoreType.DMA((5,)),
        ]
        in_specs = [pl.BlockSpec(memory_space=pltpu.HBM)] * 4
    else:
        in_specs = [pl.BlockSpec(memory_space=pl.ANY)] + [pl.BlockSpec(memory_space=VMEM)] * 4
        operands = (after,) + tuple(operands)
    return pl.pallas_call(
        match_first if first == 0 else functools.partial(match_next, first),
        out_shape=out_shape,
        in_specs=in_specs,
        out_specs=[pl.BlockSpec(memory_space=VMEM)] * len(out_shape),
        scratch_shapes=scratch,
        compiler_params=pltpu.CompilerParams(vmem_limit_bytes=40 << 20),
        cost_estimate=pl.CostEstimate(flops=4 * flops, bytes_accessed=2 << 20, transcendentals=0),
        name="match_first" if first == 0 else "match_next",
    )(*operands)


def bin_kernel(sources, bins_ref, scale_ref, *rest):
    blocks_refs, outs, acc_ref = rest[:sources], rest[sources:-1], rest[-1]
    step = outs[0].shape[0]
    chunk = pl.program_id(0)
    acc_ref[...] = jnp.zeros_like(acc_ref)
    for source, blocks_ref in enumerate(blocks_refs):

        def add(n, carry, source=source, blocks_ref=blocks_ref):
            place = bins_ref[source, n] - chunk * step
            group = bins_ref[source + sources, n]

            @pl.when((place >= 0) & (place < step) & (group >= 0))
            def _():
                slot = group * step + place
                acc_ref[slot] += scale_ref[source, n] * blocks_ref[n].astype(jnp.float32)

            return carry

        lax.fori_loop(0, blocks_ref.shape[0], add, 0)
    for index, out_ref in enumerate(outs):
        out_ref[...] = acc_ref[index * step : (index + 1) * step].astype(out_ref.dtype)


def bin_blocks(bins, scale, blocks, groups, size, name):
    count, block_side, unused = blocks[0].shape
    step = min(size, 16)
    whole = pl.BlockSpec(blocks[0].shape, lambda g: (0, 0, 0))
    part = pl.BlockSpec((step, block_side, block_side), lambda g: (g, 0, 0))
    shape = jax.ShapeDtypeStruct((size, block_side, block_side), jnp.bfloat16)
    moved = 2 * len(blocks) * blocks[0].size + 2 * groups * size * block_side**2
    return pl.pallas_call(
        functools.partial(bin_kernel, len(blocks)),
        grid=(size // step,),
        out_shape=[shape] * groups,
        in_specs=[pl.BlockSpec(memory_space=SMEM), pl.BlockSpec(memory_space=SMEM)] + [whole] * len(blocks),
        out_specs=[part] * groups,
        scratch_shapes=[VMEM((groups * step, block_side, block_side), jnp.float32)],
        compiler_params=pltpu.CompilerParams(vmem_limit_bytes=40 << 20),
        cost_estimate=pl.CostEstimate(flops=2 * moved, bytes_accessed=moved, transcendentals=0),
        name=name,
    )(bins, scale, *blocks)


def filter_kernel(taps_ref, even_ref, odd_ref, out_ref):
    half, rows_in, side = even_ref.shape
    edge = (rows_in - side) // 2
    radius = (taps_ref.shape[1] - 1) // 2
    taps = taps_ref[...]
    width = up(rows_in + 1, 128)
    row_filter = banded(lanes_at(taps, edge - radius, width), side, width)[:, :rows_in].astype(jnp.bfloat16)
    col_filter = banded(lanes_at(taps, side - radius, 3 * side), side, 3 * side).T.astype(jnp.bfloat16)
    zero = jnp.zeros((side, side), jnp.bfloat16)
    smoothed = [zero]
    for half_ref in (even_ref, odd_ref):
        for c in range(half):
            rows = jnp.dot(row_filter, half_ref[c], preferred_element_type=jnp.float32)
            smoothed.append(rows.astype(jnp.bfloat16))
    smoothed.append(zero)
    for c in range(2 * half):
        window = jnp.concatenate(smoothed[c : c + 3], axis=1)
        out_ref[:, c * side : (c + 1) * side] = jnp.dot(window, col_filter, preferred_element_type=jnp.float32)


def detect(taps, left, right):
    half, unused, side = left.shape
    return pl.pallas_call(
        filter_kernel,
        out_shape=jax.ShapeDtypeStruct((side, 2 * half * side), jnp.float32),
        in_specs=[pl.BlockSpec(memory_space=VMEM)] * 3,
        out_specs=pl.BlockSpec(memory_space=VMEM),
        compiler_params=pltpu.CompilerParams(vmem_limit_bytes=32 << 20),
        name="detect",
    )(taps, left, right)


def halves(parts, send):
    total = None
    for part in parts:
        half = part.shape[0] // 2
        piece = (part[half:] if send else part[:half]).astype(jnp.float32)
        total = piece if total is None else total + piece
    return total


def local(
    raw_blocks,
    patch_of_block,
    cell_of_block,
    band_of_block,
    block_weight,
    basis_coef,
    row_basis,
    col_basis,
    band_gain,
    filter_taps,
):
    sky_count = lax.axis_size("sky")
    band_count = lax.axis_size("band")
    sky_bits = sky_count.bit_length() - 1
    band_bits = band_count.bit_length() - 1
    device_count = sky_count * band_count
    margin_side = raw_blocks.shape[0]
    block_count = raw_blocks.shape[1] // margin_side
    radius = (filter_taps.shape[0] - 1) // 2
    block_side = margin_side - 2 * radius
    half_columns = CC // 2
    sky_here = lax.axis_index("sky")
    band_here = lax.axis_index("band")
    side_here = band_here & 1

    def swap(array, even_bit, odd_bit=None):
        bits = (even_bit, even_bit if odd_bit is None else odd_bit)
        return lax.ppermute(array, ("sky", "band"), [(i, i ^ (1 << bits[i & 1])) for i in range(device_count)])

    key = (patch_of_block[:, 0] * BANDS + band_of_block) * CELLS + cell_of_block
    facts = jnp.stack([key.astype(jnp.float32), block_weight.astype(jnp.float32)])[None]
    part_count = 4 if block_count % 4 == 0 else 1
    part_blocks = block_count // part_count
    operands = (basis_coef.T, raw_blocks, row_basis, col_basis)
    matched, from_pair = [], []
    for bit in range(max(band_bits + sky_bits, part_count)):
        got = swap(facts, bit) if bit < band_bits + sky_bits else None
        if bit < part_count:
            found = match_blocks(bit * part_blocks, part_blocks, operands, block_side, facts)
            if bit == 0:
                operands = tuple(found[1:])
            matched.append(found[0])
            from_pair.append(swap(found[0], 0))
        if got is not None:
            facts = jnp.concatenate([facts, got])

    near_key, near_weight = facts[:2, 0], facts[:2, 1]
    same = near_key[:, :, None, None] == facts[None, None, :, 0]
    weight_sum = jnp.sum(jnp.where(same, facts[None, None, :, 1], 0.0), axis=(2, 3))
    near_key = near_key.astype(jnp.int32)
    cell = near_key % CELLS
    band = near_key // CELLS % BANDS
    gain = jnp.sum(jnp.where(band[..., None] == jnp.arange(BANDS), band_gain, 0.0), axis=2)
    scale = gain * near_weight / jnp.maximum(weight_sum, 1.0)

    turn = [1, band_bits, band_bits + 1]
    later = list(range(2, band_bits)) + list(range(band_bits + 2, band_bits + sky_bits))
    steps = list(zip(turn + later, turn[2:] + turn[:2] + later))
    row = cell // CC
    column = cell % CC
    owner_off = (near_key // (CELLS * BANDS) ^ sky_here) << band_bits | (row ^ band_here)
    places = []
    for side in range(2):
        place = jnp.zeros_like(owner_off)
        for step in steps:
            place = place * 2 + (owner_off >> step[side] & 1)
        places.append(place)
    place = jnp.where(side_here == 0, places[0], places[1])
    place = (place * 2 + (row & 1)) * half_columns + column % half_columns
    mine = column // half_columns == side_here
    size = (1 << len(steps)) * half_columns
    sent = place >= size
    place = place % size
    near_blocks = matched + from_pair
    scale, place, sent_group, kept_group = (
        value.reshape(len(near_blocks), -1)
        for value in (scale, place, jnp.where(mine & sent, 0, -1), jnp.where(mine & ~sent, 0, -1))
    )
    (outgoing,) = bin_blocks(jnp.concatenate([place, sent_group]), scale, near_blocks, 1, size, "bins_sent")
    got = swap(outgoing, *steps[0])
    (kept,) = bin_blocks(jnp.concatenate([place, kept_group]), scale, near_blocks, 1, size, "bins_kept")
    parts = [kept, got]
    for step in steps[1:]:
        got = swap(halves(parts, True).astype(jnp.bfloat16), *step)
        parts = [part[: part.shape[0] // 2] for part in parts] + [got]
    total = functools.reduce(jnp.add, [part.astype(jnp.float32) for part in parts])
    rows = total.astype(jnp.bfloat16).reshape(2, half_columns, block_side, block_side)

    edge = up(radius, 16)
    upper = band_here < 2
    outer = jnp.where(upper, rows[1, :, block_side - edge :], rows[0, :, :edge])
    outer = swap(outer, 1)
    first_rows = jnp.concatenate([jnp.where(upper, 0, outer), rows[0], rows[1, :, :edge]], axis=1)
    second_rows = jnp.concatenate([rows[0, :, block_side - edge :], rows[1], jnp.where(upper, outer, 0)], axis=1)
    even = side_here == 0
    own = jnp.where(even, first_rows, second_rows)
    other = swap(jnp.where(even, second_rows, first_rows), 0)
    taps = filter_taps.astype(jnp.bfloat16).astype(jnp.float32)[None]
    return detect(taps, jnp.where(even, own, other), jnp.where(even, other, own))[None]


def solution(mesh):
    return jax.shard_map(
        local,
        mesh=mesh,
        in_specs=(
            P(None, ("sky", "band")),
            P(("sky", "band"), None),
            P(("sky", "band")),
            P(("sky", "band")),
            P(("sky", "band")),
            P(("sky", "band"), None),
            P(),
            P(),
            P(),
            P(),
        ),
        out_specs=P("sky", "band", None),
        check_vma=False,
    )
```

```python
import functools

import jax
import jax.numpy as jnp
from jax import lax
from jax.experimental import pallas as pl
from jax.experimental.pallas import tpu as pltpu
from jax.sharding import PartitionSpec as P

BANDS = 6
CR = 4
CC = 4
CELLS = 16
VMEM = pltpu.VMEM
SMEM = pltpu.SMEM


def up(value, unit):
    return -(-value // unit) * unit


def banded(row, rows, width):
    tile = pltpu.roll(jnp.broadcast_to(row, (8, width)), 0, 1, stride=1, stride_axis=0)
    return jnp.concatenate([tile if i == 0 else pltpu.roll(tile, 8 * i, 1) for i in range(rows // 8)], axis=0)


def lanes_at(row, start, width):
    parts = [row, jnp.zeros((1, width - start - row.shape[1]), row.dtype)]
    if start:
        parts.insert(0, jnp.zeros((1, start), row.dtype))
    return jnp.concatenate(parts, axis=1)


def match_kernel(small_ref, raw_ref, out_ref, rowk_ref, colk_ref):
    margin_side = raw_ref.shape[0]
    basis_count = small_ref.shape[0] // 3
    count, block_side, unused = out_ref.shape
    tap_count = margin_side - block_side + 1
    width = colk_ref.shape[0] // basis_count
    for k in range(basis_count):
        rows = banded(lanes_at(small_ref[k : k + 1, :tap_count], 0, width), block_side, width)
        rowk_ref[k * block_side : (k + 1) * block_side, :] = rows[:, :margin_side].astype(jnp.bfloat16)
        place = basis_count + k
        cols = banded(lanes_at(small_ref[place : place + 1, :tap_count], 0, width), block_side, width)
        colk_ref[k * width : (k + 1) * width, :] = cols.T.astype(jnp.bfloat16)
    for n in range(count):
        block = raw_ref[:, n * margin_side : (n + 1) * margin_side]
        sectioned = jnp.dot(rowk_ref[...], block, preferred_element_type=jnp.float32)
        total = None
        for k in range(basis_count):
            place = 2 * basis_count + k
            part = sectioned[k * block_side : (k + 1) * block_side] * small_ref[place : place + 1, n : n + 1]
            term = jnp.dot(
                part.astype(jnp.bfloat16),
                colk_ref[k * width : k * width + margin_side, :],
                preferred_element_type=jnp.float32,
            )
            total = term if total is None else total + term
        out_ref[n] = total.astype(jnp.bfloat16)


def match_blocks(raw, coef, row_basis, col_basis, block_side):
    margin_side = raw.shape[0]
    count = raw.shape[1] // margin_side
    basis_count, tap_count = row_basis.shape
    width = up(margin_side, 128)
    lanes = max(count, tap_count)
    small = [row_basis, col_basis, coef.T.astype(jnp.float32)]
    small = jnp.concatenate([jnp.pad(part, ((0, 0), (0, lanes - part.shape[1]))) for part in small])
    flops = 2 * count * basis_count * block_side * margin_side * (margin_side + block_side)
    return pl.pallas_call(
        match_kernel,
        out_shape=jax.ShapeDtypeStruct((count, block_side, block_side), jnp.bfloat16),
        in_specs=[pl.BlockSpec(memory_space=VMEM)] * 2,
        out_specs=pl.BlockSpec(memory_space=VMEM),
        scratch_shapes=[
            VMEM((basis_count * block_side, margin_side), jnp.bfloat16),
            VMEM((basis_count * width, block_side), jnp.bfloat16),
        ],
        compiler_params=pltpu.CompilerParams(vmem_limit_bytes=16 << 20),
        cost_estimate=pl.CostEstimate(flops=4 * flops, bytes_accessed=4 << 20, transcendentals=0),
        name="match_blocks",
    )(small, raw)


def bin_kernel(sources, bins_ref, scale_ref, *rest):
    blocks_refs, outs, acc_ref = rest[:sources], rest[sources:-1], rest[-1]
    step = outs[0].shape[0]
    chunk = pl.program_id(0)
    acc_ref[...] = jnp.zeros_like(acc_ref)
    for source, blocks_ref in enumerate(blocks_refs):

        def add(n, carry, source=source, blocks_ref=blocks_ref):
            place = bins_ref[source, n] - chunk * step
            group = bins_ref[source + sources, n]

            @pl.when((place >= 0) & (place < step) & (group >= 0))
            def _():
                slot = group * step + place
                acc_ref[slot] += scale_ref[source, n] * blocks_ref[n].astype(jnp.float32)

            return carry

        lax.fori_loop(0, blocks_ref.shape[0], add, 0)
    for index, out_ref in enumerate(outs):
        out_ref[...] = acc_ref[index * step : (index + 1) * step].astype(out_ref.dtype)


def bin_blocks(bins, scale, blocks, groups, size, name):
    count, block_side, unused = blocks[0].shape
    step = min(size, 32)
    whole = pl.BlockSpec(blocks[0].shape, lambda g: (0, 0, 0))
    part = pl.BlockSpec((step, block_side, block_side), lambda g: (g, 0, 0))
    shape = jax.ShapeDtypeStruct((size, block_side, block_side), jnp.bfloat16)
    moved = 2 * len(blocks) * blocks[0].size + 2 * groups * size * block_side**2
    return pl.pallas_call(
        functools.partial(bin_kernel, len(blocks)),
        grid=(size // step,),
        out_shape=[shape] * groups,
        in_specs=[pl.BlockSpec(memory_space=SMEM), pl.BlockSpec(memory_space=SMEM)] + [whole] * len(blocks),
        out_specs=[part] * groups,
        scratch_shapes=[VMEM((groups * step, block_side, block_side), jnp.float32)],
        compiler_params=pltpu.CompilerParams(vmem_limit_bytes=40 << 20),
        cost_estimate=pl.CostEstimate(flops=2 * moved, bytes_accessed=moved, transcendentals=0),
        name=name,
    )(bins, scale, *blocks)


def filter_kernel(taps_ref, mid_ref, low_ref, high_ref, out_ref):
    cells, side, unused = mid_ref.shape
    edge = low_ref.shape[1]
    tap_count = taps_ref.shape[1]
    radius = (tap_count - 1) // 2
    taps = taps_ref[...]
    rows_in = side + 2 * edge
    row_filter = banded(lanes_at(taps, edge - radius, up(rows_in + 1, 128)), side, up(rows_in + 1, 128))
    row_filter = row_filter[:, :rows_in].astype(jnp.bfloat16)
    col_filter = banded(lanes_at(taps, side - radius, 3 * side), side, 3 * side).astype(jnp.bfloat16).T
    zero = jnp.zeros((side, side), jnp.bfloat16)
    smoothed = [zero]
    for c in range(cells):
        column = jnp.concatenate([low_ref[c], mid_ref[c], high_ref[c]], axis=0)
        smoothed.append(jnp.dot(row_filter, column, preferred_element_type=jnp.float32).astype(jnp.bfloat16))
    smoothed.append(zero)
    for c in range(cells):
        window = jnp.concatenate(smoothed[c : c + 3], axis=1)
        out_ref[:, c * side : (c + 1) * side] = jnp.dot(window, col_filter, preferred_element_type=jnp.float32)


def detect(taps, mid, low, high):
    cells, side, unused = mid.shape
    return pl.pallas_call(
        filter_kernel,
        out_shape=jax.ShapeDtypeStruct((side, cells * side), jnp.float32),
        in_specs=[pl.BlockSpec(memory_space=VMEM)] * 4,
        out_specs=pl.BlockSpec(memory_space=VMEM),
        compiler_params=pltpu.CompilerParams(vmem_limit_bytes=32 << 20),
        name="detect",
    )(taps, mid, low, high)


def local(
    raw_blocks,
    patch_of_block,
    cell_of_block,
    band_of_block,
    block_weight,
    basis_coef,
    row_basis,
    col_basis,
    band_gain,
    filter_taps,
):
    sky_count = lax.axis_size("sky")
    band_count = lax.axis_size("band")
    margin_side = raw_blocks.shape[0]
    block_count = raw_blocks.shape[1] // margin_side
    radius = (filter_taps.shape[0] - 1) // 2
    block_side = margin_side - 2 * radius
    here = lax.axis_index("sky") * band_count + lax.axis_index("band")

    key = (patch_of_block[:, 0] * BANDS + band_of_block) * CELLS + cell_of_block
    facts = jnp.stack([key.astype(jnp.float32), block_weight.astype(jnp.float32)])
    facts = jnp.pad(facts, ((0, 6), (0, up(block_count, 128) - block_count)))
    facts = lax.all_gather(facts, ("sky", "band"), axis=0, tiled=True)
    facts = facts.reshape(sky_count * band_count, 8, -1)[:, :2, :block_count]

    matched = match_blocks(raw_blocks, basis_coef, row_basis, col_basis, block_side)

    own_key = key.astype(jnp.float32)
    same = own_key[:, None, None] == facts[None, :, 0]
    weight_sum = jnp.sum(jnp.where(same, facts[None, :, 1], 0.0), axis=(1, 2))
    gain = jnp.sum(jnp.where(band_of_block[:, None] == jnp.arange(BANDS), band_gain, 0.0), axis=1)
    scale = gain * block_weight.astype(jnp.float32) / jnp.maximum(weight_sum, 1.0)
    place = patch_of_block[:, 0] * CELLS + cell_of_block
    bins = jnp.stack([place, jnp.zeros_like(place)])
    (outgoing,) = bin_blocks(bins, scale[None], [matched], 1, sky_count * CELLS, "bins")
    combined = lax.psum_scatter(outgoing, ("sky", "band"), scatter_dimension=0, tiled=True)

    edge = up(radius, 16)
    forward = [(i, i + 1) for i in range(band_count - 1)]
    backward = [(i + 1, i) for i in range(band_count - 1)]
    low = lax.ppermute(combined[:, block_side - edge :], "band", forward)
    high = lax.ppermute(combined[:, :edge], "band", backward)
    taps = filter_taps.astype(jnp.bfloat16).astype(jnp.float32)[None]
    return detect(taps, combined, low, high)[None]


def solution(mesh):
    return jax.shard_map(
        local,
        mesh=mesh,
        in_specs=(
            P(None, ("sky", "band")),
            P(("sky", "band"), None),
            P(("sky", "band")),
            P(("sky", "band")),
            P(("sky", "band")),
            P(("sky", "band"), None),
            P(),
            P(),
            P(),
            P(),
        ),
        out_specs=P("sky", "band", None),
        check_vma=False,
    )
```

```python
import functools

import jax
import jax.numpy as jnp
from jax import lax
from jax.experimental import pallas as pl
from jax.experimental.pallas import tpu as pltpu
from jax.sharding import PartitionSpec as P

BANDS = 6
CR = 4
CC = 4
CELLS = 16
VMEM = pltpu.VMEM
SMEM = pltpu.SMEM


def up(value, unit):
    return -(-value // unit) * unit


def banded(row, rows, width):
    tile = pltpu.roll(jnp.broadcast_to(row, (8, width)), 0, 1, stride=1, stride_axis=0)
    return jnp.concatenate([tile if i == 0 else pltpu.roll(tile, 8 * i, 1) for i in range(rows // 8)], axis=0)


def lanes_at(row, start, width):
    parts = [row, jnp.zeros((1, width - start - row.shape[1]), row.dtype)]
    if start:
        parts.insert(0, jnp.zeros((1, start), row.dtype))
    return jnp.concatenate(parts, axis=1)


def match_part(first, small_ref, raw_ref, rowk_ref, colk_ref, out_ref):
    margin_side = raw_ref.shape[0]
    basis_count = small_ref.shape[0] // 3
    count, block_side, unused = out_ref.shape
    width = colk_ref.shape[0] // basis_count
    for n in range(count):
        here = first + n
        block = raw_ref[:, here * margin_side : (here + 1) * margin_side]
        sectioned = jnp.dot(rowk_ref[...], block, preferred_element_type=jnp.float32)
        total = None
        for k in range(basis_count):
            place = 2 * basis_count + k
            part = sectioned[k * block_side : (k + 1) * block_side] * small_ref[place : place + 1, here : here + 1]
            term = jnp.dot(
                part.astype(jnp.bfloat16),
                colk_ref[k * width : k * width + margin_side, :],
                preferred_element_type=jnp.float32,
            )
            total = term if total is None else total + term
        out_ref[n] = total.astype(jnp.bfloat16)


def match_first(small_ref, raw_ref, out_ref, rowk_ref, colk_ref):
    margin_side = raw_ref.shape[0]
    basis_count = small_ref.shape[0] // 3
    block_side = out_ref.shape[1]
    tap_count = margin_side - block_side + 1
    width = colk_ref.shape[0] // basis_count
    for k in range(basis_count):
        rows = banded(lanes_at(small_ref[k : k + 1, :tap_count], 0, width), block_side, width)
        rowk_ref[k * block_side : (k + 1) * block_side, :] = rows[:, :margin_side].astype(jnp.bfloat16)
        place = basis_count + k
        cols = banded(lanes_at(small_ref[place : place + 1, :tap_count], 0, width), block_side, width)
        colk_ref[k * width : (k + 1) * width, :] = cols.T.astype(jnp.bfloat16)
    match_part(0, small_ref, raw_ref, rowk_ref, colk_ref, out_ref)


def match_next(first, after_ref, small_ref, raw_ref, rowk_ref, colk_ref, out_ref):
    match_part(first, small_ref, raw_ref, rowk_ref, colk_ref, out_ref)


def match_blocks(first, count, small, raw, kernels, block_side, after):
    margin_side = raw.shape[0]
    basis_count = small.shape[0] // 3
    width = up(margin_side, 128)
    flops = 2 * count * basis_count * block_side * margin_side * (margin_side + block_side)
    out_shape = [jax.ShapeDtypeStruct((count, block_side, block_side), jnp.bfloat16)]
    if first == 0:
        out_shape += [
            jax.ShapeDtypeStruct((basis_count * block_side, margin_side), jnp.bfloat16),
            jax.ShapeDtypeStruct((basis_count * width, block_side), jnp.bfloat16),
        ]
        operands = (small, raw)
    else:
        operands = (after, small, raw) + kernels
    spaces = [VMEM] * len(operands) if first == 0 else [pl.ANY] + [VMEM] * (len(operands) - 1)
    found = pl.pallas_call(
        match_first if first == 0 else functools.partial(match_next, first),
        out_shape=out_shape,
        in_specs=[pl.BlockSpec(memory_space=space) for space in spaces],
        out_specs=[pl.BlockSpec(memory_space=VMEM)] * len(out_shape),
        compiler_params=pltpu.CompilerParams(vmem_limit_bytes=12 << 20),
        cost_estimate=pl.CostEstimate(flops=4 * flops, bytes_accessed=2 << 20, transcendentals=0),
        name="match_first" if first == 0 else "match_next",
    )(*operands)
    return found[0], kernels or tuple(found[1:])


def bin_kernel(sources, bins_ref, scale_ref, *rest):
    blocks_refs, rest = rest[:sources], rest[sources:]
    groups = len(rest) // 2
    outs, accs = rest[:groups], rest[groups:]
    step = outs[0].shape[0]
    low = pl.program_id(0) * step
    count = blocks_refs[0].shape[0]
    starts = [sum(out.shape[1] for out in outs[:group]) for group in range(groups + 1)]
    for acc_ref in accs:
        acc_ref[...] = jnp.zeros_like(acc_ref)
    for source, blocks_ref in enumerate(blocks_refs):
        for n in range(count):

            @pl.when(bins_ref[groups * sources + source, n] > 0)
            def _(source=source, blocks_ref=blocks_ref, n=n):
                scale = scale_ref[source, n]
                for group, acc_ref in enumerate(accs):
                    place = bins_ref[group * sources + source, n] - low
                    slot = jnp.where((place >= 0) & (place < step), place, step)
                    acc_ref[slot] += scale * blocks_ref[n, starts[group] : starts[group + 1]].astype(jnp.float32)

    for out_ref, acc_ref in zip(outs, accs):
        out_ref[...] = acc_ref[:step].astype(out_ref.dtype)


def bin_blocks(bins, scale, blocks, rows, size, name):
    count, block_side, unused = blocks[0].shape
    step = min(size, 32)
    whole = pl.BlockSpec(blocks[0].shape, lambda g: (0, 0, 0))
    moved = 2 * len(blocks) * blocks[0].size + 2 * size * block_side**2
    return pl.pallas_call(
        functools.partial(bin_kernel, len(blocks)),
        grid=(size // step,),
        out_shape=[jax.ShapeDtypeStruct((size, height, block_side), jnp.bfloat16) for height in rows],
        in_specs=[pl.BlockSpec(memory_space=SMEM), pl.BlockSpec(memory_space=SMEM)] + [whole] * len(blocks),
        out_specs=[pl.BlockSpec((step, height, block_side), lambda g: (g, 0, 0)) for height in rows],
        scratch_shapes=[VMEM((step + 1, height, block_side), jnp.float32) for height in rows],
        compiler_params=pltpu.CompilerParams(vmem_limit_bytes=20 << 20),
        cost_estimate=pl.CostEstimate(flops=2 * moved, bytes_accessed=moved, transcendentals=0),
        name=name,
    )(bins, scale, *blocks)


def filter_kernel(taps_ref, mid_ref, low_ref, high_ref, out_ref):
    cells, side, unused = mid_ref.shape
    edge = low_ref.shape[1]
    tap_count = taps_ref.shape[1]
    radius = (tap_count - 1) // 2
    taps = taps_ref[...]
    rows_in = side + 2 * edge
    row_filter = banded(lanes_at(taps, edge - radius, up(rows_in + 1, 128)), side, up(rows_in + 1, 128))
    row_filter = row_filter[:, :rows_in].astype(jnp.bfloat16)
    col_filter = banded(lanes_at(taps, side - radius, 3 * side), side, 3 * side).astype(jnp.bfloat16).T
    zero = jnp.zeros((side, side), jnp.bfloat16)
    smoothed = [zero]
    for c in range(cells):
        column = jnp.concatenate([low_ref[c], mid_ref[c], high_ref[c]], axis=0)
        smoothed.append(jnp.dot(row_filter, column, preferred_element_type=jnp.float32).astype(jnp.bfloat16))
    smoothed.append(zero)
    for c in range(cells):
        window = jnp.concatenate(smoothed[c : c + 3], axis=1)
        out_ref[:, c * side : (c + 1) * side] = jnp.dot(window, col_filter, preferred_element_type=jnp.float32)


def detect(taps, mid, low, high):
    cells, side, unused = mid.shape
    return pl.pallas_call(
        filter_kernel,
        out_shape=jax.ShapeDtypeStruct((side, cells * side), jnp.float32),
        in_specs=[pl.BlockSpec(memory_space=VMEM)] * 4,
        out_specs=pl.BlockSpec(memory_space=VMEM),
        compiler_params=pltpu.CompilerParams(vmem_limit_bytes=12 << 20),
        name="detect",
    )(taps, mid, low, high)


def halves(parts, send):
    total = None
    for part in parts:
        half = part.shape[0] // 2
        piece = (part[half:] if send else part[:half]).astype(jnp.float32)
        total = piece if total is None else total + piece
    return total


def first_halves(parts):
    return [part[: part.shape[0] // 2] for part in parts]


def local(
    raw_blocks,
    patch_of_block,
    cell_of_block,
    band_of_block,
    block_weight,
    basis_coef,
    row_basis,
    col_basis,
    band_gain,
    filter_taps,
):
    sky_count = lax.axis_size("sky")
    band_count = lax.axis_size("band")
    sky_bits = sky_count.bit_length() - 1
    band_bits = band_count.bit_length() - 1
    margin_side = raw_blocks.shape[0]
    block_count = raw_blocks.shape[1] // margin_side
    radius = (filter_taps.shape[0] - 1) // 2
    block_side = margin_side - 2 * radius
    sky_here = lax.axis_index("sky")
    band_here = lax.axis_index("band")

    def swap(array, bit):
        axis, count, bit = ("band", band_count, bit) if bit < band_bits else ("sky", sky_count, bit - band_bits)
        return lax.ppermute(array, axis, [(i, i ^ (1 << bit)) for i in range(count)])

    key = (patch_of_block[:, 0] * BANDS + band_of_block) * CELLS + cell_of_block
    facts = jnp.stack([key.astype(jnp.float32), block_weight.astype(jnp.float32)])[None]
    small = [row_basis, col_basis, basis_coef.T.astype(jnp.float32)]
    lanes = max(part.shape[1] for part in small)
    small = jnp.concatenate([jnp.pad(part, ((0, 0), (0, lanes - part.shape[1]))) for part in small])
    part_count = 4 if block_count % 4 == 0 else 1
    part_blocks = block_count // part_count
    kernels, matched, from_pair = (), [], []
    for bit in range(max(band_bits + sky_bits, part_count)):
        got = swap(facts, bit) if bit < band_bits + sky_bits else None
        if bit < part_count:
            found, kernels = match_blocks(
                bit * part_blocks, part_blocks, small, raw_blocks, kernels, block_side, facts
            )
            matched.append(found)
            from_pair.append(swap(found, 0))
        if got is not None:
            facts = jnp.concatenate([facts, got])

    near_key, near_weight = facts[:2, 0], facts[:2, 1]
    same = near_key[:, :, None, None] == facts[None, None, :, 0]
    weight_sum = jnp.sum(jnp.where(same, facts[None, None, :, 1], 0.0), axis=(2, 3))
    near_key = near_key.astype(jnp.int32)
    cell = near_key % CELLS
    band = near_key // CELLS % BANDS
    gain = jnp.sum(jnp.where(band[..., None] == jnp.arange(BANDS), band_gain, 0.0), axis=2)
    scale = gain * near_weight / jnp.maximum(weight_sum, 1.0)

    turn = [1, band_bits, band_bits + 1]
    later = list(range(2, band_bits)) + list(range(band_bits + 2, band_bits + sky_bits))
    orders = [turn[group:] + turn[:group] for group in range(3)]
    heights = [up(block_side // 3, 16)] * 2
    heights.append(block_side - sum(heights))
    owner_off = (near_key // (CELLS * BANDS) ^ sky_here) << band_bits | (cell // CC ^ band_here)
    near_blocks = matched + from_pair

    def rows_of(value):
        return value.astype(jnp.int32).reshape(len(near_blocks), -1)

    size = (1 << (len(turn) + len(later) - 1)) * CC
    sent_bins, kept_bins = [], []
    for order in orders:
        place = jnp.zeros_like(owner_off)
        for bit in order + later:
            place = place * 2 + (owner_off >> bit & 1)
        place = place * CC + cell % CC
        sent_bins.append(rows_of(jnp.where(place >= size, place - size, size)))
        kept_bins.append(rows_of(jnp.minimum(place, size)))
    mine = rows_of(owner_off & 1 == 0)
    scale = scale.reshape(len(near_blocks), -1)
    outgoing = bin_blocks(jnp.concatenate(sent_bins + [mine]), scale, near_blocks, heights, size, "bins_sent")
    got = [swap(part, order[0]) for part, order in zip(outgoing, orders)]
    kept = bin_blocks(jnp.concatenate(kept_bins + [mine]), scale, near_blocks, heights, size, "bins_kept")
    groups = [list(pair) for pair in zip(kept, got)]
    for phase in range(1, len(turn)):
        got = [swap(halves(parts, True).astype(jnp.bfloat16), order[phase]) for parts, order in zip(groups, orders)]
        groups = [first_halves(parts) + [part] for parts, part in zip(groups, got)]
    joined = []
    for bit in later:
        outgoing = jnp.concatenate([halves(parts, True) for parts in groups], axis=1)
        for part in joined:
            outgoing = outgoing + part[part.shape[0] // 2 :].astype(jnp.float32)
        got = swap(outgoing.astype(jnp.bfloat16), bit)
        groups = [first_halves(parts) for parts in groups]
        joined = first_halves(joined) + [got]

    def full(parts):
        return functools.reduce(jnp.add, [part.astype(jnp.float32) for part in parts])

    combined = jnp.concatenate([full(parts) for parts in groups], axis=1)
    if joined:
        combined = combined + full(joined)
    combined = combined.astype(jnp.bfloat16)

    edge = up(radius, 16)
    forward = [(i, i + 1) for i in range(band_count - 1)]
    backward = [(i + 1, i) for i in range(band_count - 1)]
    low = lax.ppermute(combined[:, block_side - edge :], "band", forward)
    high = lax.ppermute(combined[:, :edge], "band", backward)
    taps = filter_taps.astype(jnp.bfloat16).astype(jnp.float32)[None]
    return detect(taps, combined, low, high)[None]


def solution(mesh):
    return jax.shard_map(
        local,
        mesh=mesh,
        in_specs=(
            P(None, ("sky", "band")),
            P(("sky", "band"), None),
            P(("sky", "band")),
            P(("sky", "band")),
            P(("sky", "band")),
            P(("sky", "band"), None),
            P(),
            P(),
            P(),
            P(),
        ),
        out_specs=P("sky", "band", None),
        check_vma=False,
    )
```

```python
import functools

import jax
import jax.numpy as jnp
from jax import lax
from jax.experimental import pallas as pl
from jax.experimental.pallas import tpu as pltpu
from jax.sharding import PartitionSpec as P

BANDS = 6
CR = 4
CC = 4
CELLS = 16
VMEM = pltpu.VMEM
SMEM = pltpu.SMEM


def up(value, unit):
    return -(-value // unit) * unit


def banded(row, rows, width):
    tile = pltpu.roll(jnp.broadcast_to(row, (8, width)), 0, 1, stride=1, stride_axis=0)
    return jnp.concatenate([tile if i == 0 else pltpu.roll(tile, 8 * i, 1) for i in range(rows // 8)], axis=0)


def lanes_at(row, start, width):
    parts = [row, jnp.zeros((1, width - start - row.shape[1]), row.dtype)]
    if start:
        parts.insert(0, jnp.zeros((1, start), row.dtype))
    return jnp.concatenate(parts, axis=1)


def match_kernel(small_ref, raw_ref, *rest):
    outs, (rowk_ref, colk_ref) = rest[:-2], rest[-2:]
    margin_side = raw_ref.shape[0]
    basis_count = small_ref.shape[0] // 3
    count, unused, block_side = outs[0].shape
    tap_count = margin_side - block_side + 1
    width = colk_ref.shape[0] // basis_count
    for k in range(basis_count):
        rows = banded(lanes_at(small_ref[k : k + 1, :tap_count], 0, width), block_side, width)
        rowk_ref[k * block_side : (k + 1) * block_side, :] = rows[:, :margin_side].astype(jnp.bfloat16)
        place = basis_count + k
        cols = banded(lanes_at(small_ref[place : place + 1, :tap_count], 0, width), block_side, width)
        colk_ref[k * width : (k + 1) * width, :] = cols.T.astype(jnp.bfloat16)
    for n in range(count):
        block = raw_ref[:, n * margin_side : (n + 1) * margin_side]
        sectioned = jnp.dot(rowk_ref[...], block, preferred_element_type=jnp.float32)
        total = None
        for k in range(basis_count):
            place = 2 * basis_count + k
            part = sectioned[k * block_side : (k + 1) * block_side] * small_ref[place : place + 1, n : n + 1]
            term = jnp.dot(
                part.astype(jnp.bfloat16),
                colk_ref[k * width : k * width + margin_side, :],
                preferred_element_type=jnp.float32,
            )
            total = term if total is None else total + term
        total = total.astype(jnp.bfloat16)
        start = 0
        for out_ref in outs:
            out_ref[n] = total[start : start + out_ref.shape[1]]
            start += out_ref.shape[1]


def match_blocks(small, raw, rows, block_side):
    margin_side = raw.shape[0]
    count = raw.shape[1] // margin_side
    basis_count = small.shape[0] // 3
    width = up(margin_side, 128)
    flops = 2 * count * basis_count * block_side * margin_side * (margin_side + block_side)
    return pl.pallas_call(
        match_kernel,
        out_shape=[jax.ShapeDtypeStruct((count, height, block_side), jnp.bfloat16) for height in rows],
        in_specs=[pl.BlockSpec(memory_space=VMEM)] * 2,
        out_specs=[pl.BlockSpec(memory_space=VMEM)] * len(rows),
        scratch_shapes=[
            VMEM((basis_count * block_side, margin_side), jnp.bfloat16),
            VMEM((basis_count * width, block_side), jnp.bfloat16),
        ],
        compiler_params=pltpu.CompilerParams(vmem_limit_bytes=12 << 20),
        cost_estimate=pl.CostEstimate(flops=4 * flops, bytes_accessed=4 << 20, transcendentals=0),
        name="match_blocks",
    )(small, raw)


def bin_kernel(bins_ref, scale_ref, *rest):
    groups = len(rest) // 4
    owns, others, outs, accs = (rest[i * groups : (i + 1) * groups] for i in range(4))
    step = outs[0].shape[0]
    low = pl.program_id(0) * step
    for group in range(groups):
        acc_ref = accs[group]
        acc_ref[...] = jnp.zeros_like(acc_ref)
        for source, blocks_ref in enumerate((owns[group], others[group])):
            for n in range(blocks_ref.shape[0]):
                slot = bins_ref[2 * group + source, n] - low

                @pl.when((slot >= 0) & (slot < step))
                def _(acc_ref=acc_ref, blocks_ref=blocks_ref, n=n, slot=slot, row=source * (group + 1)):
                    acc_ref[slot] += scale_ref[row, n] * blocks_ref[n].astype(jnp.float32)

        outs[group][...] = acc_ref[...].astype(outs[group].dtype)


def bin_blocks(bins, scale, own, other, size, name):
    step = min(size, 32)
    blocks = list(own) + list(other)
    rows = [part.shape[1:] for part in own]
    moved = 2 * sum(part.size for part in blocks) + 2 * size * sum(height * width for height, width in rows)
    return pl.pallas_call(
        bin_kernel,
        grid=(size // step,),
        out_shape=[jax.ShapeDtypeStruct((size,) + shape, jnp.bfloat16) for shape in rows],
        in_specs=[pl.BlockSpec(memory_space=SMEM), pl.BlockSpec(memory_space=SMEM)]
        + [pl.BlockSpec(part.shape, lambda g: (0, 0, 0)) for part in blocks],
        out_specs=[pl.BlockSpec((step,) + shape, lambda g: (g, 0, 0)) for shape in rows],
        scratch_shapes=[VMEM((step,) + shape, jnp.float32) for shape in rows],
        compiler_params=pltpu.CompilerParams(vmem_limit_bytes=20 << 20),
        cost_estimate=pl.CostEstimate(flops=2 * moved, bytes_accessed=moved, transcendentals=0),
        name=name,
    )(bins, scale, *blocks)


def filter_kernel(taps_ref, mid_ref, low_ref, high_ref, out_ref):
    cells, side, unused = mid_ref.shape
    edge = low_ref.shape[1]
    tap_count = taps_ref.shape[1]
    radius = (tap_count - 1) // 2
    taps = taps_ref[...]
    rows_in = side + 2 * edge
    row_filter = banded(lanes_at(taps, edge - radius, up(rows_in + 1, 128)), side, up(rows_in + 1, 128))
    row_filter = row_filter[:, :rows_in].astype(jnp.bfloat16)
    col_filter = banded(lanes_at(taps, side - radius, 3 * side), side, 3 * side).astype(jnp.bfloat16).T
    zero = jnp.zeros((side, side), jnp.bfloat16)
    smoothed = [zero]
    for c in range(cells):
        column = jnp.concatenate([low_ref[c], mid_ref[c], high_ref[c]], axis=0)
        smoothed.append(jnp.dot(row_filter, column, preferred_element_type=jnp.float32).astype(jnp.bfloat16))
    smoothed.append(zero)
    for c in range(cells):
        window = jnp.concatenate(smoothed[c : c + 3], axis=1)
        out_ref[:, c * side : (c + 1) * side] = jnp.dot(window, col_filter, preferred_element_type=jnp.float32)


def detect(taps, mid, low, high):
    cells, side, unused = mid.shape
    return pl.pallas_call(
        filter_kernel,
        out_shape=jax.ShapeDtypeStruct((side, cells * side), jnp.float32),
        in_specs=[pl.BlockSpec(memory_space=VMEM)] * 4,
        out_specs=pl.BlockSpec(memory_space=VMEM),
        compiler_params=pltpu.CompilerParams(vmem_limit_bytes=12 << 20),
        name="detect",
    )(taps, mid, low, high)


def halves(parts, send):
    total = None
    for part in parts:
        half = part.shape[0] // 2
        piece = (part[half:] if send else part[:half]).astype(jnp.float32)
        total = piece if total is None else total + piece
    return total


def first_halves(parts):
    return [part[: part.shape[0] // 2] for part in parts]


def local(
    raw_blocks,
    patch_of_block,
    cell_of_block,
    band_of_block,
    block_weight,
    basis_coef,
    row_basis,
    col_basis,
    band_gain,
    filter_taps,
):
    sky_count = lax.axis_size("sky")
    band_count = lax.axis_size("band")
    sky_bits = sky_count.bit_length() - 1
    band_bits = band_count.bit_length() - 1
    margin_side = raw_blocks.shape[0]
    block_count = raw_blocks.shape[1] // margin_side
    radius = (filter_taps.shape[0] - 1) // 2
    block_side = margin_side - 2 * radius
    sky_here = lax.axis_index("sky")
    band_here = lax.axis_index("band")

    def swap(array, bit):
        axis, count, bit = ("band", band_count, bit) if bit < band_bits else ("sky", sky_count, bit - band_bits)
        return lax.ppermute(array, axis, [(i, i ^ (1 << bit)) for i in range(count)])

    turn = [1, band_bits, band_bits + 1]
    later = list(range(2, band_bits)) + list(range(band_bits + 2, band_bits + sky_bits))
    orders = [turn[group:] + turn[:group] for group in range(len(turn))]
    heights = [up(block_side // 3, 16)] * 2
    heights.append(block_side - sum(heights))

    key = (patch_of_block[:, 0] * BANDS + band_of_block) * CELLS + cell_of_block
    facts = jnp.stack([key.astype(jnp.float32), block_weight.astype(jnp.float32)])[None]
    small = [row_basis, col_basis, basis_coef.T.astype(jnp.float32)]
    lanes = max(part.shape[1] for part in small)
    small = jnp.concatenate([jnp.pad(part, ((0, 0), (0, lanes - part.shape[1]))) for part in small])
    matched = match_blocks(small, raw_blocks, heights, block_side)
    others = [swap(part, order[0]) for part, order in zip(matched, orders)]
    for bit in range(band_bits + sky_bits):
        facts = jnp.concatenate([facts, swap(facts, bit)])

    near = jnp.stack([facts[0]] + [facts[1 << order[0]] for order in orders])
    near_key, near_weight = near[:, 0], near[:, 1]
    same = near_key[:, :, None, None] == facts[None, None, :, 0]
    weight_sum = jnp.sum(jnp.where(same, facts[None, None, :, 1], 0.0), axis=(2, 3))
    near_key = near_key.astype(jnp.int32)
    cell = near_key % CELLS
    band = near_key // CELLS % BANDS
    gain = jnp.sum(jnp.where(band[..., None] == jnp.arange(BANDS), band_gain, 0.0), axis=2)
    scale = gain * near_weight / jnp.maximum(weight_sum, 1.0)

    owner_off = (near_key // (CELLS * BANDS) ^ sky_here) << band_bits | (cell // CC ^ band_here)
    size = (1 << (len(turn) + len(later) - 1)) * CC
    sent_bins, kept_bins = [], []
    for group, order in enumerate(orders):
        for row in (0, group + 1):
            off = owner_off[row]
            place = jnp.zeros_like(off)
            for bit in [0] + order[1:] + later:
                place = place * 2 + (off >> bit & 1)
            place = place * CC + cell[row] % CC
            mine = off >> order[0] & 1 == 0
            sent_bins.append(jnp.where(mine, place - size, -1))
            kept_bins.append(jnp.where(mine & (place < size), place, -1))
    outgoing = bin_blocks(jnp.stack(sent_bins), scale, matched, others, size, "bins_sent")
    got = [swap(part, 0) for part in outgoing]
    kept = bin_blocks(jnp.stack(kept_bins), scale, matched, others, size, "bins_kept")
    groups = [list(pair) for pair in zip(kept, got)]
    for phase in range(1, len(turn)):
        got = [swap(halves(parts, True).astype(jnp.bfloat16), order[phase]) for parts, order in zip(groups, orders)]
        groups = [first_halves(parts) + [part] for parts, part in zip(groups, got)]
    joined = []
    for bit in later:
        outgoing = jnp.concatenate([halves(parts, True) for parts in groups], axis=1)
        for part in joined:
            outgoing = outgoing + part[part.shape[0] // 2 :].astype(jnp.float32)
        got = swap(outgoing.astype(jnp.bfloat16), bit)
        groups = [first_halves(parts) for parts in groups]
        joined = first_halves(joined) + [got]

    def full(parts):
        return functools.reduce(jnp.add, [part.astype(jnp.float32) for part in parts])

    combined = jnp.concatenate([full(parts) for parts in groups], axis=1)
    if joined:
        combined = combined + full(joined)
    combined = combined.astype(jnp.bfloat16)

    edge = up(radius, 16)
    forward = [(i, i + 1) for i in range(band_count - 1)]
    backward = [(i + 1, i) for i in range(band_count - 1)]
    low = lax.ppermute(combined[:, block_side - edge :], "band", forward)
    high = lax.ppermute(combined[:, :edge], "band", backward)
    taps = filter_taps.astype(jnp.bfloat16).astype(jnp.float32)[None]
    return detect(taps, combined, low, high)[None]


def solution(mesh):
    return jax.shard_map(
        local,
        mesh=mesh,
        in_specs=(
            P(None, ("sky", "band")),
            P(("sky", "band"), None),
            P(("sky", "band")),
            P(("sky", "band")),
            P(("sky", "band")),
            P(("sky", "band"), None),
            P(),
            P(),
            P(),
            P(),
        ),
        out_specs=P("sky", "band", None),
        check_vma=False,
    )
```

```python
import functools

import jax
import jax.numpy as jnp
from jax import lax
from jax.experimental import pallas as pl
from jax.experimental.pallas import tpu as pltpu
from jax.sharding import PartitionSpec as P

BANDS = 6
CR = 4
CC = 4
CELLS = 16
VMEM = pltpu.VMEM
SMEM = pltpu.SMEM


def up(value, unit):
    return -(-value // unit) * unit


def banded(row, rows, width):
    tile = pltpu.roll(jnp.broadcast_to(row, (8, width)), 0, 1, stride=1, stride_axis=0)
    return jnp.concatenate([tile if i == 0 else pltpu.roll(tile, 8 * i, 1) for i in range(rows // 8)], axis=0)


def lanes_at(row, start, width):
    parts = [row, jnp.zeros((1, width - start - row.shape[1]), row.dtype)]
    if start:
        parts.insert(0, jnp.zeros((1, start), row.dtype))
    return jnp.concatenate(parts, axis=1)


def match_kernel(small_ref, raw_ref, out_ref, rowk_ref, colk_ref):
    margin_side = raw_ref.shape[0]
    basis_count = small_ref.shape[0] // 3
    count, block_side, unused = out_ref.shape
    tap_count = margin_side - block_side + 1
    width = colk_ref.shape[0] // basis_count
    for k in range(basis_count):
        rows = banded(lanes_at(small_ref[k : k + 1, :tap_count], 0, width), block_side, width)
        rowk_ref[k * block_side : (k + 1) * block_side, :] = rows[:, :margin_side].astype(jnp.bfloat16)
        place = basis_count + k
        cols = banded(lanes_at(small_ref[place : place + 1, :tap_count], 0, width), block_side, width)
        colk_ref[k * width : (k + 1) * width, :] = cols.T.astype(jnp.bfloat16)
    for n in range(count):
        block = raw_ref[:, n * margin_side : (n + 1) * margin_side]
        sectioned = jnp.dot(rowk_ref[...], block, preferred_element_type=jnp.float32)
        total = None
        for k in range(basis_count):
            place = 2 * basis_count + k
            part = sectioned[k * block_side : (k + 1) * block_side] * small_ref[place : place + 1, n : n + 1]
            term = jnp.dot(
                part.astype(jnp.bfloat16),
                colk_ref[k * width : k * width + margin_side, :],
                preferred_element_type=jnp.float32,
            )
            total = term if total is None else total + term
        out_ref[n] = total.astype(jnp.bfloat16)


def match_blocks(small, raw, block_side):
    margin_side = raw.shape[0]
    count = raw.shape[1] // margin_side
    basis_count = small.shape[0] // 3
    width = up(margin_side, 128)
    flops = 2 * count * basis_count * block_side * margin_side * (margin_side + block_side)
    return pl.pallas_call(
        match_kernel,
        out_shape=jax.ShapeDtypeStruct((count, block_side, block_side), jnp.bfloat16),
        in_specs=[pl.BlockSpec(memory_space=VMEM)] * 2,
        out_specs=pl.BlockSpec(memory_space=VMEM),
        scratch_shapes=[
            VMEM((basis_count * block_side, margin_side), jnp.bfloat16),
            VMEM((basis_count * width, block_side), jnp.bfloat16),
        ],
        compiler_params=pltpu.CompilerParams(vmem_limit_bytes=12 << 20),
        cost_estimate=pl.CostEstimate(flops=4 * flops, bytes_accessed=4 << 20, transcendentals=0),
        name="match_blocks",
    )(small, raw)


def bin_kernel(bins_ref, scale_ref, *rest):
    (own_ref, other_ref), outs, acc_ref = rest[:2], rest[2:-1], rest[-1]
    size = outs[0].shape[0]
    step = acc_ref.shape[0]
    low = pl.program_id(0) * step
    acc_ref[...] = jnp.zeros_like(acc_ref)
    for source, blocks_ref in enumerate((own_ref, other_ref)):
        for n in range(blocks_ref.shape[0]):
            slot = bins_ref[source, n] - low

            @pl.when((slot >= 0) & (slot < step))
            def _(source=source, blocks_ref=blocks_ref, n=n, slot=slot):
                acc_ref[slot] += scale_ref[source, n] * blocks_ref[n].astype(jnp.float32)

    for index, out_ref in enumerate(outs):
        out_ref[...] = acc_ref[index * size : (index + 1) * size].astype(out_ref.dtype)


def bin_blocks(bins, scale, own, other, groups, size, name):
    block_side = own.shape[1]
    if groups * size > 64:
        groups, size, split = 1, groups * size, groups
    else:
        split = 1
    step = min(groups * size, 64)
    whole = pl.BlockSpec(own.shape, lambda g: (0, 0, 0))
    part = pl.BlockSpec((step // groups, block_side, block_side), lambda g: (g, 0, 0))
    moved = 4 * own.size + 2 * groups * size * block_side**2
    found = pl.pallas_call(
        bin_kernel,
        grid=(groups * size // step,),
        out_shape=[jax.ShapeDtypeStruct((size, block_side, block_side), jnp.bfloat16)] * groups,
        in_specs=[pl.BlockSpec(memory_space=SMEM), pl.BlockSpec(memory_space=SMEM), whole, whole],
        out_specs=[part] * groups,
        scratch_shapes=[VMEM((step, block_side, block_side), jnp.float32)],
        compiler_params=pltpu.CompilerParams(vmem_limit_bytes=20 << 20),
        cost_estimate=pl.CostEstimate(flops=2 * moved, bytes_accessed=moved, transcendentals=0),
        name=name,
    )(bins, scale, own, other)
    if split > 1:
        found = jnp.split(found[0], split)
    return found


def filter_kernel(taps_ref, mid_ref, low_ref, high_ref, out_ref):
    cells, side, unused = mid_ref.shape
    edge = low_ref.shape[1]
    tap_count = taps_ref.shape[1]
    radius = (tap_count - 1) // 2
    taps = taps_ref[...]
    rows_in = side + 2 * edge
    row_filter = banded(lanes_at(taps, edge - radius, up(rows_in + 1, 128)), side, up(rows_in + 1, 128))
    row_filter = row_filter[:, :rows_in].astype(jnp.bfloat16)
    col_filter = banded(lanes_at(taps, side - radius, 3 * side), side, 3 * side).astype(jnp.bfloat16).T
    zero = jnp.zeros((side, side), jnp.bfloat16)
    smoothed = [zero]
    for c in range(cells):
        column = jnp.concatenate([low_ref[c], mid_ref[c], high_ref[c]], axis=0)
        smoothed.append(jnp.dot(row_filter, column, preferred_element_type=jnp.float32).astype(jnp.bfloat16))
    smoothed.append(zero)
    for c in range(cells):
        window = jnp.concatenate(smoothed[c : c + 3], axis=1)
        out_ref[:, c * side : (c + 1) * side] = jnp.dot(window, col_filter, preferred_element_type=jnp.float32)


def detect(taps, mid, low, high):
    cells, side, unused = mid.shape
    return pl.pallas_call(
        filter_kernel,
        out_shape=jax.ShapeDtypeStruct((side, cells * side), jnp.float32),
        in_specs=[pl.BlockSpec(memory_space=VMEM)] * 4,
        out_specs=pl.BlockSpec(memory_space=VMEM),
        compiler_params=pltpu.CompilerParams(vmem_limit_bytes=12 << 20),
        name="detect",
    )(taps, mid, low, high)


def swap(array, axis, bit):
    count = lax.axis_size(axis)
    return lax.ppermute(array, axis, [(i, i ^ (1 << bit)) for i in range(count)])


def halves(parts, send):
    total = None
    for part in parts:
        half = part.shape[0] // 2
        piece = (part[half:] if send else part[:half]).astype(jnp.float32)
        total = piece if total is None else total + piece
    return total


def local(
    raw_blocks,
    patch_of_block,
    cell_of_block,
    band_of_block,
    block_weight,
    basis_coef,
    row_basis,
    col_basis,
    band_gain,
    filter_taps,
):
    sky_count = lax.axis_size("sky")
    band_count = lax.axis_size("band")
    sky_bits = sky_count.bit_length() - 1
    band_bits = band_count.bit_length() - 1
    margin_side = raw_blocks.shape[0]
    block_count = raw_blocks.shape[1] // margin_side
    radius = (filter_taps.shape[0] - 1) // 2
    block_side = margin_side - 2 * radius
    sky_here = lax.axis_index("sky")
    band_here = lax.axis_index("band")

    key = (patch_of_block[:, 0] * BANDS + band_of_block) * CELLS + cell_of_block
    facts = jnp.stack([key.astype(jnp.float32), block_weight.astype(jnp.float32)])
    chip_facts = jnp.concatenate(
        [facts]
        + [lax.ppermute(facts, "band", [(i, i ^ off) for i in range(band_count)]) for off in range(1, band_count)]
    )
    small = [row_basis, col_basis, basis_coef.T.astype(jnp.float32)]
    lanes = max(part.shape[1] for part in small)
    small = jnp.concatenate([jnp.pad(part, ((0, 0), (0, lanes - part.shape[1]))) for part in small])
    matched = match_blocks(small, raw_blocks, block_side)
    from_pair = swap(matched, "band", 0)
    all_facts = lax.all_gather(chip_facts, "sky", axis=0, tiled=True).reshape(-1, 2, block_count)

    near_key, near_weight = (chip_facts[:4].reshape(2, 2, block_count)[:, i] for i in range(2))
    same = near_key[:, :, None, None] == all_facts[None, None, :, 0]
    weight_sum = jnp.sum(jnp.where(same, all_facts[None, None, :, 1], 0.0), axis=(2, 3))
    near_key = near_key.astype(jnp.int32)
    cell = near_key % CELLS
    band = near_key // CELLS % BANDS
    gain = jnp.sum(jnp.where(band[..., None] == jnp.arange(BANDS), band_gain, 0.0), axis=2)
    scale = gain * near_weight / jnp.maximum(weight_sum, 1.0)

    sky_off = near_key // (CELLS * BANDS) ^ sky_here
    band_off = cell // CC ^ band_here
    column = cell % CC
    half_columns = CC // 2
    sky_low = sky_off & 1
    sky_rest = jnp.zeros_like(sky_off)
    for bit in range(1, sky_bits):
        sky_rest = sky_rest * 2 + (sky_off >> bit & 1)
    band_rest = jnp.zeros_like(band_off)
    for bit in range(1, band_bits):
        band_rest = band_rest * 2 + (band_off >> bit & 1)
    rest_count = sky_count // 2
    row_count = band_count // 2
    side_a = (band_rest * 2 + sky_low) * rest_count + sky_rest
    side_b = (sky_low * row_count + band_rest) * rest_count + sky_rest
    second = column >= half_columns
    place = jnp.where(second, side_b, side_a) * half_columns + column % half_columns
    size = sky_count * row_count * half_columns // 2
    mine = band_off & 1 == 0
    sent = place >= size
    place = place % size
    group = second.astype(jnp.int32)
    place = group * size + place
    sent_bins = jnp.where(mine & sent, place, -1)
    kept_bins = jnp.where(mine & ~sent, place, -1)
    send_a, send_b = bin_blocks(sent_bins, scale, matched, from_pair, 2, size, "bins_sent")
    steps_a = [("band", bit) for bit in range(1, band_bits)] + [("sky", 0)]
    steps_b = [("sky", 0)] + [("band", bit) for bit in range(1, band_bits)]
    got_a, got_b = swap(send_a, *steps_a[0]), swap(send_b, *steps_b[0])
    keep_a, keep_b = bin_blocks(kept_bins, scale, matched, from_pair, 2, size, "bins_kept")
    parts_a, parts_b = [keep_a, got_a], [keep_b, got_b]
    for step_a, step_b in zip(steps_a[1:], steps_b[1:]):
        got_a = swap(halves(parts_a, True).astype(jnp.bfloat16), *step_a)
        got_b = swap(halves(parts_b, True).astype(jnp.bfloat16), *step_b)
        parts_a = [part[: part.shape[0] // 2] for part in parts_a] + [got_a]
        parts_b = [part[: part.shape[0] // 2] for part in parts_b] + [got_b]

    def by_sky(part):
        return part.reshape((rest_count, half_columns) + part.shape[1:])

    parts_a, parts_b = [by_sky(part) for part in parts_a], [by_sky(part) for part in parts_b]
    later = []
    for bit in range(1, sky_bits):
        outgoing = jnp.concatenate([halves(parts_a, True), halves(parts_b, True)], axis=1)
        for part in later:
            outgoing = outgoing + part[part.shape[0] // 2 :].astype(jnp.float32)
        got = swap(outgoing.astype(jnp.bfloat16), "sky", bit)
        parts_a = [part[: part.shape[0] // 2] for part in parts_a]
        parts_b = [part[: part.shape[0] // 2] for part in parts_b]
        later = [part[: part.shape[0] // 2] for part in later] + [got]

    def full(parts):
        return functools.reduce(jnp.add, [part.astype(jnp.float32) for part in parts])

    combined = jnp.concatenate([full(parts_a), full(parts_b)], axis=1) + full(later)
    combined = combined[0].astype(jnp.bfloat16)

    edge = up(radius, 16)
    forward = [(i, i + 1) for i in range(band_count - 1)]
    backward = [(i + 1, i) for i in range(band_count - 1)]
    low = lax.ppermute(combined[:, block_side - edge :], "band", forward)
    high = lax.ppermute(combined[:, :edge], "band", backward)
    taps = filter_taps.astype(jnp.bfloat16).astype(jnp.float32)[None]
    return detect(taps, combined, low, high)[None]


def solution(mesh):
    return jax.shard_map(
        local,
        mesh=mesh,
        in_specs=(
            P(None, ("sky", "band")),
            P(("sky", "band"), None),
            P(("sky", "band")),
            P(("sky", "band")),
            P(("sky", "band")),
            P(("sky", "band"), None),
            P(),
            P(),
            P(),
            P(),
        ),
        out_specs=P("sky", "band", None),
        check_vma=False,
    )
```

```python
import functools

import jax
import jax.numpy as jnp
from jax import lax
from jax.experimental import pallas as pl
from jax.experimental.pallas import tpu as pltpu
from jax.sharding import PartitionSpec as P

BANDS = 6
CR = 4
CC = 4
CELLS = 16
VMEM = pltpu.VMEM
SMEM = pltpu.SMEM


def up(value, unit):
    return -(-value // unit) * unit


def banded(row, rows, width):
    tile = pltpu.roll(jnp.broadcast_to(row, (8, width)), 0, 1, stride=1, stride_axis=0)
    return jnp.concatenate([tile if i == 0 else pltpu.roll(tile, 8 * i, 1) for i in range(rows // 8)], axis=0)


def lanes_at(row, start, width):
    parts = [row, jnp.zeros((1, width - start - row.shape[1]), row.dtype)]
    if start:
        parts.insert(0, jnp.zeros((1, start), row.dtype))
    return jnp.concatenate(parts, axis=1)


def match_part(first, small_ref, raw_ref, rowk_ref, colk_ref, outs):
    margin_side = raw_ref.shape[0]
    basis_count = small_ref.shape[0] // 3
    count, unused, block_side = outs[0].shape
    width = colk_ref.shape[0] // basis_count
    for n in range(count):
        here = first + n
        block = raw_ref[:, here * margin_side : (here + 1) * margin_side]
        sectioned = jnp.dot(rowk_ref[...], block, preferred_element_type=jnp.float32)
        total = None
        for k in range(basis_count):
            place = 2 * basis_count + k
            part = sectioned[k * block_side : (k + 1) * block_side] * small_ref[place : place + 1, here : here + 1]
            term = jnp.dot(
                part.astype(jnp.bfloat16),
                colk_ref[k * width : k * width + margin_side, :],
                preferred_element_type=jnp.float32,
            )
            total = term if total is None else total + term
        total = total.astype(jnp.bfloat16)
        start = 0
        for out_ref in outs:
            out_ref[n] = total[start : start + out_ref.shape[1]]
            start += out_ref.shape[1]


def match_first(after_ref, small_ref, raw_ref, *rest):
    outs, (rowk_ref, colk_ref) = rest[:-2], rest[-2:]
    margin_side = raw_ref.shape[0]
    basis_count = small_ref.shape[0] // 3
    block_side = outs[0].shape[2]
    tap_count = margin_side - block_side + 1
    width = colk_ref.shape[0] // basis_count
    for k in range(basis_count):
        rows = banded(lanes_at(small_ref[k : k + 1, :tap_count], 0, width), block_side, width)
        rowk_ref[k * block_side : (k + 1) * block_side, :] = rows[:, :margin_side].astype(jnp.bfloat16)
        place = basis_count + k
        cols = banded(lanes_at(small_ref[place : place + 1, :tap_count], 0, width), block_side, width)
        colk_ref[k * width : (k + 1) * width, :] = cols.T.astype(jnp.bfloat16)
    match_part(0, small_ref, raw_ref, rowk_ref, colk_ref, outs)


def match_next(first, after_ref, small_ref, raw_ref, rowk_ref, colk_ref, *outs):
    match_part(first, small_ref, raw_ref, rowk_ref, colk_ref, outs)


def match_blocks(first, count, small, raw, kernels, rows, block_side, after):
    margin_side = raw.shape[0]
    basis_count = small.shape[0] // 3
    width = up(margin_side, 128)
    flops = 2 * count * basis_count * block_side * margin_side * (margin_side + block_side)
    out_shape = [jax.ShapeDtypeStruct((count, height, block_side), jnp.bfloat16) for height in rows]
    if first == 0:
        out_shape += [
            jax.ShapeDtypeStruct((basis_count * block_side, margin_side), jnp.bfloat16),
            jax.ShapeDtypeStruct((basis_count * width, block_side), jnp.bfloat16),
        ]
    found = pl.pallas_call(
        match_first if first == 0 else functools.partial(match_next, first),
        out_shape=out_shape,
        in_specs=[pl.BlockSpec(memory_space=pl.ANY)] + [pl.BlockSpec(memory_space=VMEM)] * (2 + len(kernels)),
        out_specs=[pl.BlockSpec(memory_space=VMEM)] * len(out_shape),
        compiler_params=pltpu.CompilerParams(vmem_limit_bytes=12 << 20),
        cost_estimate=pl.CostEstimate(flops=4 * flops, bytes_accessed=2 << 20, transcendentals=0),
        name="match_first" if first == 0 else "match_next",
    )(after, small, raw, *kernels)
    return found[: len(rows)], kernels or tuple(found[len(rows) :])


def bin_kernel(groups, bins_ref, scale_ref, *rest):
    blocks_refs, (out_ref, acc_ref) = rest[:-2], rest[-2:]
    parts = len(blocks_refs) // (2 * groups)
    step = acc_ref.shape[0]
    low = pl.program_id(0) * step
    acc_ref[...] = jnp.zeros_like(acc_ref)
    for index, blocks_ref in enumerate(blocks_refs):
        line, part = index // parts, index % parts
        group, source = line // 2, line % 2
        count = blocks_ref.shape[0]
        for n in range(count):
            slot = bins_ref[line, part * count + n] - low

            @pl.when((slot >= 0) & (slot < step))
            def _(blocks_ref=blocks_ref, n=n, slot=slot, row=source * (group + 1), place=part * count + n):
                acc_ref[slot] += scale_ref[row, place] * blocks_ref[n].astype(jnp.float32)

    out_ref[...] = acc_ref[...].astype(out_ref.dtype)


def bin_blocks(bins, scale, blocks, groups, size, name):
    shape = blocks[0].shape[1:]
    step = min(groups * size, 64)
    moved = 2 * sum(part.size for part in blocks) + 2 * groups * size * shape[0] * shape[1]
    return pl.pallas_call(
        functools.partial(bin_kernel, groups),
        grid=(groups * size // step,),
        out_shape=jax.ShapeDtypeStruct((groups * size,) + shape, jnp.bfloat16),
        in_specs=[pl.BlockSpec(memory_space=SMEM), pl.BlockSpec(memory_space=SMEM)]
        + [pl.BlockSpec(part.shape, lambda g: (0, 0, 0)) for part in blocks],
        out_specs=pl.BlockSpec((step,) + shape, lambda g: (g, 0, 0)),
        scratch_shapes=[VMEM((step,) + shape, jnp.float32)],
        compiler_params=pltpu.CompilerParams(vmem_limit_bytes=20 << 20),
        cost_estimate=pl.CostEstimate(flops=2 * moved, bytes_accessed=moved, transcendentals=0),
        name=name,
    )(bins, scale, *blocks)


def filter_kernel(taps_ref, mid_ref, low_ref, high_ref, out_ref):
    cells, side, unused = mid_ref.shape
    edge = low_ref.shape[1]
    tap_count = taps_ref.shape[1]
    radius = (tap_count - 1) // 2
    taps = taps_ref[...]
    rows_in = side + 2 * edge
    row_filter = banded(lanes_at(taps, edge - radius, up(rows_in + 1, 128)), side, up(rows_in + 1, 128))
    row_filter = row_filter[:, :rows_in].astype(jnp.bfloat16)
    col_filter = banded(lanes_at(taps, side - radius, 3 * side), side, 3 * side).astype(jnp.bfloat16).T
    zero = jnp.zeros((side, side), jnp.bfloat16)
    smoothed = [zero]
    for c in range(cells):
        column = jnp.concatenate([low_ref[c], mid_ref[c], high_ref[c]], axis=0)
        smoothed.append(jnp.dot(row_filter, column, preferred_element_type=jnp.float32).astype(jnp.bfloat16))
    smoothed.append(zero)
    for c in range(cells):
        window = jnp.concatenate(smoothed[c : c + 3], axis=1)
        out_ref[:, c * side : (c + 1) * side] = jnp.dot(window, col_filter, preferred_element_type=jnp.float32)


def detect(taps, mid, low, high):
    cells, side, unused = mid.shape
    return pl.pallas_call(
        filter_kernel,
        out_shape=jax.ShapeDtypeStruct((side, cells * side), jnp.float32),
        in_specs=[pl.BlockSpec(memory_space=VMEM)] * 4,
        out_specs=pl.BlockSpec(memory_space=VMEM),
        compiler_params=pltpu.CompilerParams(vmem_limit_bytes=12 << 20),
        name="detect",
    )(taps, mid, low, high)


def halves(parts, send):
    total = None
    for part in parts:
        half = part.shape[0] // 2
        piece = (part[half:] if send else part[:half]).astype(jnp.float32)
        total = piece if total is None else total + piece
    return total


def first_halves(parts):
    return [part[: part.shape[0] // 2] for part in parts]


def local(
    raw_blocks,
    patch_of_block,
    cell_of_block,
    band_of_block,
    block_weight,
    basis_coef,
    row_basis,
    col_basis,
    band_gain,
    filter_taps,
):
    sky_count = lax.axis_size("sky")
    band_count = lax.axis_size("band")
    sky_bits = sky_count.bit_length() - 1
    band_bits = band_count.bit_length() - 1
    margin_side = raw_blocks.shape[0]
    block_count = raw_blocks.shape[1] // margin_side
    radius = (filter_taps.shape[0] - 1) // 2
    block_side = margin_side - 2 * radius
    sky_here = lax.axis_index("sky")
    band_here = lax.axis_index("band")

    def swap(array, bit):
        axis, count, bit = ("band", band_count, bit) if bit < band_bits else ("sky", sky_count, bit - band_bits)
        return lax.ppermute(array, axis, [(i, i ^ (1 << bit)) for i in range(count)])

    turn = [1, band_bits]
    later = list(range(2, band_bits)) + list(range(band_bits + 1, band_bits + sky_bits))
    orders = [turn[group:] + turn[:group] for group in range(len(turn))]
    heights = [block_side // len(orders)] * len(orders)

    key = (patch_of_block[:, 0] * BANDS + band_of_block) * CELLS + cell_of_block
    facts = jnp.stack([key.astype(jnp.float32), block_weight.astype(jnp.float32)])[None]
    facts = jnp.concatenate(
        [facts]
        + [lax.ppermute(facts, "band", [(i, i ^ off) for i in range(band_count)]) for off in range(1, band_count)]
    )
    small = [row_basis, col_basis, basis_coef.T.astype(jnp.float32)]
    lanes = max(part.shape[1] for part in small)
    small = jnp.concatenate([jnp.pad(part, ((0, 0), (0, lanes - part.shape[1]))) for part in small])
    part_count = 2 if block_count % 2 == 0 else 1
    part_blocks = block_count // part_count
    kernels, own, others = (), [[], []], [[], []]
    for part in range(max(part_count, sky_bits)):
        got = swap(facts, band_bits + part) if part < sky_bits else None
        if part < part_count:
            found, kernels = match_blocks(
                part * part_blocks, part_blocks, small, raw_blocks, kernels, heights, block_side, facts
            )
            for group, order in enumerate(orders):
                own[group].append(found[group])
                others[group].append(swap(found[group], order[0]))
        if got is not None:
            facts = jnp.concatenate([facts, got])

    near = jnp.stack([facts[0]] + [facts[1 << order[0]] for order in orders])
    near_key, near_weight = near[:, 0], near[:, 1]
    same = near_key[:, :, None, None] == facts[None, None, :, 0]
    weight_sum = jnp.sum(jnp.where(same, facts[None, None, :, 1], 0.0), axis=(2, 3))
    near_key = near_key.astype(jnp.int32)
    cell = near_key % CELLS
    band = near_key // CELLS % BANDS
    gain = jnp.sum(jnp.where(band[..., None] == jnp.arange(BANDS), band_gain, 0.0), axis=2)
    scale = gain * near_weight / jnp.maximum(weight_sum, 1.0)

    owner_off = (near_key // (CELLS * BANDS) ^ sky_here) << band_bits | (cell // CC ^ band_here)
    size = (1 << (len(turn) + len(later) - 1)) * CC
    sent_bins, kept_bins, blocks = [], [], []
    for group, order in enumerate(orders):
        blocks += own[group] + others[group]
        for row in (0, group + 1):
            off = owner_off[row]
            place = jnp.zeros_like(off)
            for bit in [0] + order[1:] + later:
                place = place * 2 + (off >> bit & 1)
            place = place * CC + cell[row] % CC
            mine = off >> order[0] & 1 == 0
            sent_bins.append(jnp.where(mine & (place >= size), place - size + group * size, -1))
            kept_bins.append(jnp.where(mine & (place < size), place + group * size, -1))
    outgoing = bin_blocks(jnp.stack(sent_bins), scale, blocks, len(orders), size, "bins_sent")
    got = swap(outgoing, 0)
    kept = bin_blocks(jnp.stack(kept_bins), scale, blocks, len(orders), size, "bins_kept")
    groups = [[part[group * size : (group + 1) * size] for part in (kept, got)] for group in range(len(orders))]
    for phase in range(1, len(turn)):
        got = [swap(halves(parts, True).astype(jnp.bfloat16), order[phase]) for parts, order in zip(groups, orders)]
        groups = [first_halves(parts) + [part] for parts, part in zip(groups, got)]
    joined = []
    for bit in later:
        outgoing = jnp.concatenate([halves(parts, True) for parts in groups], axis=1)
        for part in joined:
            outgoing = outgoing + part[part.shape[0] // 2 :].astype(jnp.float32)
        got = swap(outgoing.astype(jnp.bfloat16), bit)
        groups = [first_halves(parts) for parts in groups]
        joined = first_halves(joined) + [got]

    def full(parts):
        return functools.reduce(jnp.add, [part.astype(jnp.float32) for part in parts])

    combined = jnp.concatenate([full(parts) for parts in groups], axis=1)
    if joined:
        combined = combined + full(joined)
    combined = combined.astype(jnp.bfloat16)

    edge = up(radius, 16)
    forward = [(i, i + 1) for i in range(band_count - 1)]
    backward = [(i + 1, i) for i in range(band_count - 1)]
    low = lax.ppermute(combined[:, block_side - edge :], "band", forward)
    high = lax.ppermute(combined[:, :edge], "band", backward)
    taps = filter_taps.astype(jnp.bfloat16).astype(jnp.float32)[None]
    return detect(taps, combined, low, high)[None]


def solution(mesh):
    return jax.shard_map(
        local,
        mesh=mesh,
        in_specs=(
            P(None, ("sky", "band")),
            P(("sky", "band"), None),
            P(("sky", "band")),
            P(("sky", "band")),
            P(("sky", "band")),
            P(("sky", "band"), None),
            P(),
            P(),
            P(),
            P(),
        ),
        out_specs=P("sky", "band", None),
        check_vma=False,
    )
```

```python
import functools

import jax
import jax.numpy as jnp
from jax import lax
from jax.experimental import pallas as pl
from jax.experimental.pallas import tpu as pltpu
from jax.sharding import PartitionSpec as P

BANDS = 6
CR = 4
CC = 4
CELLS = 16
VMEM = pltpu.VMEM
SMEM = pltpu.SMEM


def up(value, unit):
    return -(-value // unit) * unit


def banded(row, rows, width):
    tile = pltpu.roll(jnp.broadcast_to(row, (8, width)), 0, 1, stride=1, stride_axis=0)
    return jnp.concatenate([tile if i == 0 else pltpu.roll(tile, 8 * i, 1) for i in range(rows // 8)], axis=0)


def lanes_at(row, start, width):
    parts = [row, jnp.zeros((1, width - start - row.shape[1]), row.dtype)]
    if start:
        parts.insert(0, jnp.zeros((1, start), row.dtype))
    return jnp.concatenate(parts, axis=1)


def match_part(first, small_ref, raw_ref, rowk_ref, colk_ref, outs):
    margin_side = raw_ref.shape[0]
    basis_count = small_ref.shape[0] // 3
    count, unused, block_side = outs[0].shape
    width = colk_ref.shape[0] // basis_count
    for n in range(count):
        here = first + n
        block = raw_ref[:, here * margin_side : (here + 1) * margin_side]
        sectioned = jnp.dot(rowk_ref[...], block, preferred_element_type=jnp.float32)
        total = None
        for k in range(basis_count):
            place = 2 * basis_count + k
            part = sectioned[k * block_side : (k + 1) * block_side] * small_ref[place : place + 1, here : here + 1]
            term = jnp.dot(
                part.astype(jnp.bfloat16),
                colk_ref[k * width : k * width + margin_side, :],
                preferred_element_type=jnp.float32,
            )
            total = term if total is None else total + term
        total = total.astype(jnp.bfloat16)
        start = 0
        for out_ref in outs:
            out_ref[n] = total[start : start + out_ref.shape[1]]
            start += out_ref.shape[1]


def match_first(after_ref, small_ref, raw_ref, *rest):
    outs, (rowk_ref, colk_ref) = rest[:-2], rest[-2:]
    margin_side = raw_ref.shape[0]
    basis_count = small_ref.shape[0] // 3
    block_side = outs[0].shape[2]
    tap_count = margin_side - block_side + 1
    width = colk_ref.shape[0] // basis_count
    for k in range(basis_count):
        rows = banded(lanes_at(small_ref[k : k + 1, :tap_count], 0, width), block_side, width)
        rowk_ref[k * block_side : (k + 1) * block_side, :] = rows[:, :margin_side].astype(jnp.bfloat16)
        place = basis_count + k
        cols = banded(lanes_at(small_ref[place : place + 1, :tap_count], 0, width), block_side, width)
        colk_ref[k * width : (k + 1) * width, :] = cols.T.astype(jnp.bfloat16)
    match_part(0, small_ref, raw_ref, rowk_ref, colk_ref, outs)


def match_next(first, after_ref, small_ref, raw_ref, rowk_ref, colk_ref, *outs):
    match_part(first, small_ref, raw_ref, rowk_ref, colk_ref, outs)


def match_blocks(first, count, small, raw, kernels, rows, block_side, after):
    margin_side = raw.shape[0]
    basis_count = small.shape[0] // 3
    width = up(margin_side, 128)
    flops = 2 * count * basis_count * block_side * margin_side * (margin_side + block_side)
    out_shape = [jax.ShapeDtypeStruct((count, height, block_side), jnp.bfloat16) for height in rows]
    if first == 0:
        out_shape += [
            jax.ShapeDtypeStruct((basis_count * block_side, margin_side), jnp.bfloat16),
            jax.ShapeDtypeStruct((basis_count * width, block_side), jnp.bfloat16),
        ]
    found = pl.pallas_call(
        match_first if first == 0 else functools.partial(match_next, first),
        out_shape=out_shape,
        in_specs=[pl.BlockSpec(memory_space=pl.ANY)] + [pl.BlockSpec(memory_space=VMEM)] * (2 + len(kernels)),
        out_specs=[pl.BlockSpec(memory_space=VMEM)] * len(out_shape),
        compiler_params=pltpu.CompilerParams(vmem_limit_bytes=12 << 20),
        cost_estimate=pl.CostEstimate(flops=4 * flops, bytes_accessed=2 << 20, transcendentals=0),
        name="match_first" if first == 0 else "match_next",
    )(after, small, raw, *kernels)
    return found[: len(rows)], kernels or tuple(found[len(rows) :])


def bin_kernel(groups, bins_ref, scale_ref, *rest):
    blocks_refs, (out_ref, acc_ref) = rest[:-2], rest[-2:]
    parts = len(blocks_refs) // (2 * groups)
    step = acc_ref.shape[0]
    low = pl.program_id(0) * step
    acc_ref[...] = jnp.zeros_like(acc_ref)
    for index, blocks_ref in enumerate(blocks_refs):
        line, part = index // parts, index % parts
        group, source = line // 2, line % 2
        count = blocks_ref.shape[0]
        for n in range(count):
            slot = bins_ref[line, part * count + n] - low

            @pl.when((slot >= 0) & (slot < step))
            def _(blocks_ref=blocks_ref, n=n, slot=slot, row=source * (group + 1), place=part * count + n):
                acc_ref[slot] += scale_ref[row, place] * blocks_ref[n].astype(jnp.float32)

    out_ref[...] = acc_ref[...].astype(out_ref.dtype)


def bin_blocks(bins, scale, blocks, groups, size, name):
    shape = blocks[0].shape[1:]
    step = min(groups * size, 64)
    moved = 2 * sum(part.size for part in blocks) + 2 * groups * size * shape[0] * shape[1]
    return pl.pallas_call(
        functools.partial(bin_kernel, groups),
        grid=(groups * size // step,),
        out_shape=jax.ShapeDtypeStruct((groups * size,) + shape, jnp.bfloat16),
        in_specs=[pl.BlockSpec(memory_space=SMEM), pl.BlockSpec(memory_space=SMEM)]
        + [pl.BlockSpec(part.shape, lambda g: (0, 0, 0)) for part in blocks],
        out_specs=pl.BlockSpec((step,) + shape, lambda g: (g, 0, 0)),
        scratch_shapes=[VMEM((step,) + shape, jnp.float32)],
        compiler_params=pltpu.CompilerParams(vmem_limit_bytes=20 << 20),
        cost_estimate=pl.CostEstimate(flops=2 * moved, bytes_accessed=moved, transcendentals=0),
        name=name,
    )(bins, scale, *blocks)


def filters_kernel(edge, taps_ref, rows_ref, cols_ref):
    side, rows_in = rows_ref.shape
    radius = (taps_ref.shape[1] - 1) // 2
    taps = taps_ref[...]
    width = up(rows_in + 1, 128)
    rows_ref[...] = banded(lanes_at(taps, edge - radius, width), side, width)[:, :rows_in].astype(jnp.bfloat16)
    cols_ref[...] = banded(lanes_at(taps, side - radius, 3 * side), side, 3 * side).T.astype(jnp.bfloat16)


def filters(taps, side, edge):
    return pl.pallas_call(
        functools.partial(filters_kernel, edge),
        out_shape=[
            jax.ShapeDtypeStruct((side, side + 2 * edge), jnp.bfloat16),
            jax.ShapeDtypeStruct((3 * side, side), jnp.bfloat16),
        ],
        in_specs=[pl.BlockSpec(memory_space=VMEM)],
        out_specs=[pl.BlockSpec(memory_space=VMEM)] * 2,
        compiler_params=pltpu.CompilerParams(vmem_limit_bytes=12 << 20),
        cost_estimate=pl.CostEstimate(flops=1 << 20, bytes_accessed=1 << 20, transcendentals=0),
        name="filters",
    )(taps)


def filter_kernel(row_filter_ref, col_filter_ref, mid_ref, low_ref, high_ref, out_ref):
    cells, side, unused = mid_ref.shape
    zero = jnp.zeros((side, side), jnp.bfloat16)
    smoothed = [zero]
    for c in range(cells):
        column = jnp.concatenate([low_ref[c], mid_ref[c], high_ref[c]], axis=0)
        rows = jnp.dot(row_filter_ref[...], column, preferred_element_type=jnp.float32)
        smoothed.append(rows.astype(jnp.bfloat16))
    smoothed.append(zero)
    for c in range(cells):
        window = jnp.concatenate(smoothed[c : c + 3], axis=1)
        out_ref[:, c * side : (c + 1) * side] = jnp.dot(
            window, col_filter_ref[...], preferred_element_type=jnp.float32
        )


def detect(row_filter, col_filter, mid, low, high):
    cells, side, unused = mid.shape
    return pl.pallas_call(
        filter_kernel,
        out_shape=jax.ShapeDtypeStruct((side, cells * side), jnp.float32),
        in_specs=[pl.BlockSpec(memory_space=VMEM)] * 5,
        out_specs=pl.BlockSpec(memory_space=VMEM),
        compiler_params=pltpu.CompilerParams(vmem_limit_bytes=12 << 20),
        name="detect",
    )(row_filter, col_filter, mid, low, high)


def halves(parts, send):
    total = None
    for part in parts:
        half = part.shape[0] // 2
        piece = (part[half:] if send else part[:half]).astype(jnp.float32)
        total = piece if total is None else total + piece
    return total


def first_halves(parts):
    return [part[: part.shape[0] // 2] for part in parts]


def local(
    raw_blocks,
    patch_of_block,
    cell_of_block,
    band_of_block,
    block_weight,
    basis_coef,
    row_basis,
    col_basis,
    band_gain,
    filter_taps,
):
    sky_count = lax.axis_size("sky")
    band_count = lax.axis_size("band")
    sky_bits = sky_count.bit_length() - 1
    band_bits = band_count.bit_length() - 1
    margin_side = raw_blocks.shape[0]
    block_count = raw_blocks.shape[1] // margin_side
    radius = (filter_taps.shape[0] - 1) // 2
    block_side = margin_side - 2 * radius
    sky_here = lax.axis_index("sky")
    band_here = lax.axis_index("band")

    def swap(array, bit):
        axis, count, bit = ("band", band_count, bit) if bit < band_bits else ("sky", sky_count, bit - band_bits)
        return lax.ppermute(array, axis, [(i, i ^ (1 << bit)) for i in range(count)])

    band_bit, sky_bit, next_bit = 1, band_bits, band_bits + 1
    orders = [[band_bit, next_bit, sky_bit], [sky_bit, band_bit, next_bit]]
    later = list(range(2, band_bits)) + list(range(band_bits + 2, band_bits + sky_bits))
    heights = [block_side // len(orders)] * len(orders)

    key = (patch_of_block[:, 0] * BANDS + band_of_block) * CELLS + cell_of_block
    facts = jnp.stack([key.astype(jnp.float32), block_weight.astype(jnp.float32)])[None]
    facts = jnp.concatenate(
        [facts]
        + [lax.ppermute(facts, "band", [(i, i ^ off) for i in range(band_count)]) for off in range(1, band_count)]
    )
    small = [row_basis, col_basis, basis_coef.T.astype(jnp.float32)]
    lanes = max(part.shape[1] for part in small)
    small = jnp.concatenate([jnp.pad(part, ((0, 0), (0, lanes - part.shape[1]))) for part in small])
    part_count = 2 if block_count % 2 == 0 else 1
    part_blocks = block_count // part_count
    kernels, own, others = (), [[], []], [[], []]
    for part in range(max(part_count, sky_bits)):
        got = swap(facts, band_bits + part) if part < sky_bits else None
        if part < part_count:
            found, kernels = match_blocks(
                part * part_blocks, part_blocks, small, raw_blocks, kernels, heights, block_side, facts
            )
            for group, order in enumerate(orders):
                own[group].append(found[group])
                others[group].append(swap(found[group], order[0]))
        if got is not None:
            facts = jnp.concatenate([facts, got])

    near = jnp.stack([facts[0]] + [facts[1 << order[0]] for order in orders])
    near_key, near_weight = near[:, 0], near[:, 1]
    same = near_key[:, :, None, None] == facts[None, None, :, 0]
    weight_sum = jnp.sum(jnp.where(same, facts[None, None, :, 1], 0.0), axis=(2, 3))
    near_key = near_key.astype(jnp.int32)
    cell = near_key % CELLS
    band = near_key // CELLS % BANDS
    gain = jnp.sum(jnp.where(band[..., None] == jnp.arange(BANDS), band_gain, 0.0), axis=2)
    scale = gain * near_weight / jnp.maximum(weight_sum, 1.0)

    owner_off = (near_key // (CELLS * BANDS) ^ sky_here) << band_bits | (cell // CC ^ band_here)
    size = (1 << (len(orders[0]) + len(later) - 1)) * CC
    sent_bins, kept_bins, blocks = [], [], []
    for group, order in enumerate(orders):
        blocks += own[group] + others[group]
        for row in (0, group + 1):
            off = owner_off[row]
            place = jnp.zeros_like(off)
            for bit in [0] + order[1:] + later:
                place = place * 2 + (off >> bit & 1)
            place = place * CC + cell[row] % CC
            mine = off >> order[0] & 1 == 0
            sent_bins.append(jnp.where(mine & (place >= size), place - size + group * size, -1))
            kept_bins.append(jnp.where(mine & (place < size), place + group * size, -1))
    outgoing = bin_blocks(jnp.stack(sent_bins), scale, blocks, len(orders), size, "bins_sent")
    got = swap(outgoing, 0)
    kept = bin_blocks(jnp.stack(kept_bins), scale, blocks, len(orders), size, "bins_kept")
    groups = [[part[group * size : (group + 1) * size] for part in (kept, got)] for group in range(len(orders))]
    for phase in range(1, len(orders[0])):
        got = [swap(halves(parts, True).astype(jnp.bfloat16), order[phase]) for parts, order in zip(groups, orders)]
        groups = [first_halves(parts) + [part] for parts, part in zip(groups, got)]
    joined = []
    for bit in later:
        outgoing = jnp.concatenate([halves(parts, True) for parts in groups], axis=1)
        for part in joined:
            outgoing = outgoing + part[part.shape[0] // 2 :].astype(jnp.float32)
        got = swap(outgoing.astype(jnp.bfloat16), bit)
        groups = [first_halves(parts) for parts in groups]
        joined = first_halves(joined) + [got]

    def full(parts):
        return functools.reduce(jnp.add, [part.astype(jnp.float32) for part in parts])

    combined = jnp.concatenate([full(parts) for parts in groups], axis=1)
    if joined:
        combined = combined + full(joined)
    combined = combined.astype(jnp.bfloat16)

    edge = up(radius, 16)
    top, bottom = combined[:, :edge], combined[:, block_side - edge :]
    even = band_here & 1 == 0
    inner = [(i, i + 1) for i in range(1, band_count - 1, 2)]
    beyond = lax.ppermute(jnp.where(even, top, bottom), "band", inner + [(i, j) for j, i in inner])
    paired = swap(jnp.where(even, bottom, top), 0)
    taps = filter_taps.astype(jnp.bfloat16).astype(jnp.float32)[None]
    row_filter, col_filter = filters(taps, block_side, edge)
    return detect(
        row_filter, col_filter, combined, jnp.where(even, beyond, paired), jnp.where(even, paired, beyond)
    )[None]


def solution(mesh):
    return jax.shard_map(
        local,
        mesh=mesh,
        in_specs=(
            P(None, ("sky", "band")),
            P(("sky", "band"), None),
            P(("sky", "band")),
            P(("sky", "band")),
            P(("sky", "band")),
            P(("sky", "band"), None),
            P(),
            P(),
            P(),
            P(),
        ),
        out_specs=P("sky", "band", None),
        check_vma=False,
    )
```

```python
import functools

import jax
import jax.numpy as jnp
from jax import lax
from jax.experimental import pallas as pl
from jax.experimental.pallas import tpu as pltpu
from jax.sharding import PartitionSpec as P

BANDS = 6
CR = 4
CC = 4
CELLS = 16
VMEM = pltpu.VMEM
SMEM = pltpu.SMEM


def up(value, unit):
    return -(-value // unit) * unit


def banded(row, rows, width):
    tile = pltpu.roll(jnp.broadcast_to(row, (8, width)), 0, 1, stride=1, stride_axis=0)
    return jnp.concatenate([tile if i == 0 else pltpu.roll(tile, 8 * i, 1) for i in range(rows // 8)], axis=0)


def lanes_at(row, start, width):
    parts = [row, jnp.zeros((1, width - start - row.shape[1]), row.dtype)]
    if start:
        parts.insert(0, jnp.zeros((1, start), row.dtype))
    return jnp.concatenate(parts, axis=1)


def load_kernel(*refs):
    sources, (facts_ref, coef_ref, rowk_ref, colk_ref, raw_ref) = refs[:8], refs[8:13]
    patch_ref, cell_ref, band_ref, weight_ref, row_ref, col_ref, coef_in = targets = refs[13:20]
    sems = refs[20]
    copies = [
        pltpu.make_async_copy(source, target, sems.at[i])
        for i, (source, target) in enumerate(zip(sources, targets + (raw_ref,)))
    ]
    for copy in copies:
        copy.start()
    for copy in copies[:-1]:
        copy.wait()
    key = (patch_ref[...] * BANDS + band_ref[...]) * CELLS + cell_ref[...]
    facts_ref[0, 0:1, :] = key.astype(jnp.float32)
    facts_ref[0, 1:2, :] = weight_ref[...].astype(jnp.float32).reshape(1, -1)
    coef_ref[...] = coef_in[...].astype(jnp.float32)
    basis_count, margin_side = row_ref.shape[0], raw_ref.shape[0]
    block_side = rowk_ref.shape[0] // basis_count
    width = colk_ref.shape[0] // basis_count
    for k in range(basis_count):
        rows = banded(lanes_at(row_ref[k : k + 1, :], 0, width), block_side, width)
        rowk_ref[k * block_side : (k + 1) * block_side, :] = rows[:, :margin_side].astype(jnp.bfloat16)
        cols = banded(lanes_at(col_ref[k : k + 1, :], 0, width), block_side, width)
        colk_ref[k * width : (k + 1) * width, :] = cols.T.astype(jnp.bfloat16)
    copies[-1].wait()


def load(patch, cell, band, weight, row_basis, col_basis, coef, raw, block_side):
    basis_count = row_basis.shape[0]
    margin_side = raw.shape[0]
    width = up(margin_side, 128)
    operands = (patch, cell, band, weight, row_basis, col_basis, coef, raw)
    out_shape = [
        jax.ShapeDtypeStruct((1, 2, patch.shape[1]), jnp.float32),
        jax.ShapeDtypeStruct(coef.shape, jnp.float32),
        jax.ShapeDtypeStruct((basis_count * block_side, margin_side), jnp.bfloat16),
        jax.ShapeDtypeStruct((basis_count * width, block_side), jnp.bfloat16),
        jax.ShapeDtypeStruct(raw.shape, raw.dtype),
    ]
    return pl.pallas_call(
        load_kernel,
        out_shape=out_shape,
        in_specs=[pl.BlockSpec(memory_space=pltpu.HBM)] * len(operands),
        out_specs=[pl.BlockSpec(memory_space=VMEM)] * len(out_shape),
        scratch_shapes=[VMEM(value.shape, value.dtype) for value in operands[:-1]]
        + [pltpu.SemaphoreType.DMA((len(operands),))],
        compiler_params=pltpu.CompilerParams(vmem_limit_bytes=12 << 20),
        cost_estimate=pl.CostEstimate(flops=1 << 20, bytes_accessed=4 << 20, transcendentals=0),
        name="load",
    )(*(pltpu.with_memory_space_constraint(value, pltpu.HBM) for value in operands))


def match_kernel(first, count, skip, fresh, after_ref, coef_ref, rowk_ref, colk_ref, raw_ref, *outs):
    margin_side = raw_ref.shape[0]
    basis_count = coef_ref.shape[0]
    outs = outs if fresh else outs[len(outs) // 2 :]
    block_side = outs[0].shape[2]
    width = colk_ref.shape[0] // basis_count
    for n in range(count):
        here = first + n
        block = raw_ref[:, here * margin_side : (here + 1) * margin_side]
        sectioned = jnp.dot(rowk_ref[...], block, preferred_element_type=jnp.float32)
        total = None
        for k in range(basis_count):
            part = sectioned[k * block_side : (k + 1) * block_side] * coef_ref[k : k + 1, here : here + 1]
            term = jnp.dot(
                part.astype(jnp.bfloat16),
                colk_ref[k * width : k * width + margin_side, :],
                preferred_element_type=jnp.float32,
            )
            total = term if total is None else total + term
        total = total.astype(jnp.bfloat16)
        start = 0
        for out_ref in outs:
            out_ref[skip + n] = total[start : start + out_ref.shape[1]]
            start += out_ref.shape[1]


def match_blocks(first, count, size, loaded, rows, block_side, after, into=()):
    raw = loaded[-1]
    basis_count = loaded[0].shape[0]
    skip = size - count if into else 0
    flops = 2 * count * basis_count * block_side * raw.shape[0] * (raw.shape[0] + block_side)
    return pl.pallas_call(
        functools.partial(match_kernel, first, count, skip, not into),
        out_shape=[jax.ShapeDtypeStruct((size, height, block_side), jnp.bfloat16) for height in rows],
        in_specs=[pl.BlockSpec(memory_space=pl.ANY)] + [pl.BlockSpec(memory_space=VMEM)] * (len(loaded) + len(into)),
        out_specs=[pl.BlockSpec(memory_space=VMEM)] * len(rows),
        input_output_aliases={1 + len(loaded) + i: i for i in range(len(into))},
        compiler_params=pltpu.CompilerParams(vmem_limit_bytes=8 << 20),
        cost_estimate=pl.CostEstimate(flops=4 * flops, bytes_accessed=2 << 20, transcendentals=0),
        name="match_blocks",
    )(after, *loaded, *into)


def bin_kernel(groups, bins_ref, scale_ref, after_ref, *rest):
    blocks_refs, (out_ref, acc_ref) = rest[:-2], rest[-2:]
    parts = len(blocks_refs) // (2 * groups)
    step = acc_ref.shape[0]
    low = pl.program_id(0) * step
    acc_ref[...] = jnp.zeros_like(acc_ref)
    for index, blocks_ref in enumerate(blocks_refs):
        line, part = index // parts, index % parts
        group, source = line // 2, line % 2
        start = sum(ref.shape[0] for ref in blocks_refs[:part])
        for n in range(blocks_ref.shape[0]):
            slot = bins_ref[line, start + n] - low

            @pl.when((slot >= 0) & (slot < step))
            def _(blocks_ref=blocks_ref, n=n, slot=slot, row=source * (group + 1), place=start + n):
                acc_ref[slot] += scale_ref[row, place] * blocks_ref[n].astype(jnp.float32)

    out_ref[...] = acc_ref[...].astype(out_ref.dtype)


def bin_blocks(bins, scale, blocks, groups, size, name, after):
    shape = blocks[0].shape[1:]
    step = min(groups * size, 64)
    moved = 2 * sum(part.size for part in blocks) + 2 * groups * size * shape[0] * shape[1]
    return pl.pallas_call(
        functools.partial(bin_kernel, groups),
        grid=(groups * size // step,),
        out_shape=jax.ShapeDtypeStruct((groups * size,) + shape, jnp.bfloat16),
        in_specs=[pl.BlockSpec(memory_space=SMEM), pl.BlockSpec(memory_space=SMEM), pl.BlockSpec(memory_space=pl.ANY)]
        + [pl.BlockSpec(part.shape, lambda g: (0, 0, 0)) for part in blocks],
        out_specs=pl.BlockSpec((step,) + shape, lambda g: (g, 0, 0)),
        scratch_shapes=[VMEM((step,) + shape, jnp.float32)],
        compiler_params=pltpu.CompilerParams(vmem_limit_bytes=20 << 20),
        cost_estimate=pl.CostEstimate(flops=2 * moved, bytes_accessed=moved, transcendentals=0),
        name=name,
    )(bins, scale, after, *blocks)


def filters_kernel(edge, taps_ref, rows_ref, cols_ref):
    side, rows_in = rows_ref.shape
    radius = (taps_ref.shape[1] - 1) // 2
    taps = taps_ref[...]
    width = up(rows_in + 1, 128)
    rows_ref[...] = banded(lanes_at(taps, edge - radius, width), side, width)[:, :rows_in].astype(jnp.bfloat16)
    cols_ref[...] = banded(lanes_at(taps, side - radius, 3 * side), side, 3 * side).T.astype(jnp.bfloat16)


def filters(taps, side, edge):
    return pl.pallas_call(
        functools.partial(filters_kernel, edge),
        out_shape=[
            jax.ShapeDtypeStruct((side, side + 2 * edge), jnp.bfloat16),
            jax.ShapeDtypeStruct((3 * side, side), jnp.bfloat16),
        ],
        in_specs=[pl.BlockSpec(memory_space=VMEM)],
        out_specs=[pl.BlockSpec(memory_space=VMEM)] * 2,
        compiler_params=pltpu.CompilerParams(vmem_limit_bytes=12 << 20),
        cost_estimate=pl.CostEstimate(flops=1 << 20, bytes_accessed=1 << 20, transcendentals=0),
        name="filters",
    )(taps)


def filter_kernel(row_filter_ref, col_filter_ref, mid_ref, low_ref, high_ref, out_ref):
    cells, side, unused = mid_ref.shape
    zero = jnp.zeros((side, side), jnp.bfloat16)
    smoothed = [zero]
    for c in range(cells):
        column = jnp.concatenate([low_ref[c], mid_ref[c], high_ref[c]], axis=0)
        rows = jnp.dot(row_filter_ref[...], column, preferred_element_type=jnp.float32)
        smoothed.append(rows.astype(jnp.bfloat16))
    smoothed.append(zero)
    for c in range(cells):
        window = jnp.concatenate(smoothed[c : c + 3], axis=1)
        out_ref[:, c * side : (c + 1) * side] = jnp.dot(
            window, col_filter_ref[...], preferred_element_type=jnp.float32
        )


def detect(row_filter, col_filter, mid, low, high):
    cells, side, unused = mid.shape
    return pl.pallas_call(
        filter_kernel,
        out_shape=jax.ShapeDtypeStruct((side, cells * side), jnp.float32),
        in_specs=[pl.BlockSpec(memory_space=VMEM)] * 5,
        out_specs=pl.BlockSpec(memory_space=VMEM),
        compiler_params=pltpu.CompilerParams(vmem_limit_bytes=12 << 20),
        name="detect",
    )(row_filter, col_filter, mid, low, high)


def halves(parts, send):
    total = None
    for part in parts:
        half = part.shape[0] // 2
        piece = (part[half:] if send else part[:half]).astype(jnp.float32)
        total = piece if total is None else total + piece
    return total


def first_halves(parts):
    return [part[: part.shape[0] // 2] for part in parts]


def local(
    raw_blocks,
    patch_of_block,
    cell_of_block,
    band_of_block,
    block_weight,
    basis_coef,
    row_basis,
    col_basis,
    band_gain,
    filter_taps,
):
    sky_count = lax.axis_size("sky")
    band_count = lax.axis_size("band")
    sky_bits = sky_count.bit_length() - 1
    band_bits = band_count.bit_length() - 1
    margin_side = raw_blocks.shape[0]
    block_count = raw_blocks.shape[1] // margin_side
    radius = (filter_taps.shape[0] - 1) // 2
    block_side = margin_side - 2 * radius
    sky_here = lax.axis_index("sky")
    band_here = lax.axis_index("band")

    def swap(array, bit):
        axis, count, bit = ("band", band_count, bit) if bit < band_bits else ("sky", sky_count, bit - band_bits)
        return lax.ppermute(array, axis, [(i, i ^ (1 << bit)) for i in range(count)])

    band_bit, sky_bit, next_bit = 1, band_bits, band_bits + 1
    orders = [[band_bit, next_bit, sky_bit], [sky_bit, band_bit, next_bit]]
    later = list(range(2, band_bits)) + list(range(band_bits + 2, band_bits + sky_bits))
    heights = [block_side // len(orders)] * len(orders)

    own_facts, *loaded = load(
        patch_of_block.reshape(1, -1),
        cell_of_block.reshape(1, -1),
        band_of_block.reshape(1, -1),
        block_weight,
        row_basis,
        col_basis,
        basis_coef.T,
        raw_blocks,
        block_side,
    )
    facts = jnp.concatenate(
        [own_facts]
        + [lax.ppermute(own_facts, "band", [(i, i ^ off) for i in range(band_count)]) for off in range(1, band_count)]
    )
    cut, early = block_count * 5 // 8, block_count * 3 // 8
    own, others = [[], []], [[], []]
    begun = match_blocks(0, early, cut, loaded, heights, block_side, own_facts)
    for part in range(max(2, sky_bits)):
        got = swap(facts, band_bits + part) if part < sky_bits else None
        if part == 0:
            found = match_blocks(early, cut - early, cut, loaded, heights, block_side, facts, begun)
        elif part == 1:
            found = match_blocks(cut, block_count - cut, block_count - cut, loaded, heights, block_side, facts)
        if part < 2:
            for group, order in enumerate(orders):
                own[group].append(found[group])
                others[group].append(swap(found[group], order[0]))
        if got is not None:
            facts = jnp.concatenate([facts, got])

    near = jnp.stack([facts[0]] + [facts[1 << order[0]] for order in orders])
    near_key, near_weight = near[:, 0], near[:, 1]
    same = near_key[:, :, None, None] == facts[None, None, :, 0]
    weight_sum = jnp.sum(jnp.where(same, facts[None, None, :, 1], 0.0), axis=(2, 3))
    near_key = near_key.astype(jnp.int32)
    cell = near_key % CELLS
    band = near_key // CELLS % BANDS
    gain = jnp.sum(jnp.where(band[..., None] == jnp.arange(BANDS), band_gain, 0.0), axis=2)
    scale = gain * near_weight / jnp.maximum(weight_sum, 1.0)

    owner_off = (near_key // (CELLS * BANDS) ^ sky_here) << band_bits | (cell // CC ^ band_here)
    size = (1 << (len(orders[0]) + len(later) - 1)) * CC
    half = size // 2
    bins, blocks = ([], [], []), []
    for group, order in enumerate(orders):
        blocks += own[group] + others[group]
        for row in (0, group + 1):
            off = owner_off[row]
            place = jnp.zeros_like(off)
            for bit in [0] + order[1:] + later:
                place = place * 2 + (off >> bit & 1)
            place = place * CC + cell[row] % CC
            place = jnp.where(off >> order[0] & 1 == 0, place, -1)
            for lines, low, count in zip(bins, (size, half, 0), (size, half, half)):
                lines.append(jnp.where((place >= low) & (place < low + count), place - low + group * count, -1))
    for_pair, for_next, for_rest = (jnp.stack(lines) for lines in bins)
    got = swap(bin_blocks(for_pair, scale, blocks, len(orders), size, "bins_for_pair", scale), 0)
    sent = bin_blocks(for_next, scale, blocks, len(orders), half, "bins_for_next", scale)
    edge = up(radius, 16)
    taps = filter_taps.astype(jnp.bfloat16).astype(jnp.float32)[None]
    row_filter, col_filter = filters(taps, block_side, edge)
    kept = bin_blocks(for_rest, scale, blocks, len(orders), half, "bins_kept", row_filter)
    groups = []
    for group, order in enumerate(orders):
        mine = got[group * size : (group + 1) * size]
        outgoing = sent[group * half : (group + 1) * half].astype(jnp.float32) + mine[half:].astype(jnp.float32)
        back = swap(outgoing.astype(jnp.bfloat16), order[1])
        groups.append([kept[group * half : (group + 1) * half], mine[:half], back])
    got = [swap(halves(parts, True).astype(jnp.bfloat16), order[2]) for parts, order in zip(groups, orders)]
    groups = [first_halves(parts) + [part] for parts, part in zip(groups, got)]
    joined = []
    for bit in later:
        outgoing = jnp.concatenate([halves(parts, True) for parts in groups], axis=1)
        for part in joined:
            outgoing = outgoing + part[part.shape[0] // 2 :].astype(jnp.float32)
        got = swap(outgoing.astype(jnp.bfloat16), bit)
        groups = [first_halves(parts) for parts in groups]
        joined = first_halves(joined) + [got]

    def full(parts):
        return functools.reduce(jnp.add, [part.astype(jnp.float32) for part in parts])

    combined = jnp.concatenate([full(parts) for parts in groups], axis=1)
    if joined:
        combined = combined + full(joined)
    combined = combined.astype(jnp.bfloat16)

    top, bottom = combined[:, :edge], combined[:, block_side - edge :]
    even = band_here & 1 == 0
    inner = [(i, i + 1) for i in range(1, band_count - 1, 2)]
    beyond = lax.ppermute(jnp.where(even, top, bottom), "band", inner + [(i, j) for j, i in inner])
    paired = swap(jnp.where(even, bottom, top), 0)
    return detect(
        row_filter, col_filter, combined, jnp.where(even, beyond, paired), jnp.where(even, paired, beyond)
    )[None]


def solution(mesh):
    return jax.shard_map(
        local,
        mesh=mesh,
        in_specs=(
            P(None, ("sky", "band")),
            P(("sky", "band"), None),
            P(("sky", "band")),
            P(("sky", "band")),
            P(("sky", "band")),
            P(("sky", "band"), None),
            P(),
            P(),
            P(),
            P(),
        ),
        out_specs=P("sky", "band", None),
        check_vma=False,
    )
```

```python
import functools

import jax
import jax.numpy as jnp
from jax import lax
from jax.experimental import pallas as pl
from jax.experimental.pallas import tpu as pltpu
from jax.sharding import PartitionSpec as P

BANDS = 6
CR = 4
CC = 4
CELLS = 16
VMEM = pltpu.VMEM
SMEM = pltpu.SMEM


def up(value, unit):
    return -(-value // unit) * unit


def banded(row, rows, width):
    tile = pltpu.roll(jnp.broadcast_to(row, (8, width)), 0, 1, stride=1, stride_axis=0)
    return jnp.concatenate([tile if i == 0 else pltpu.roll(tile, 8 * i, 1) for i in range(rows // 8)], axis=0)


def lanes_at(row, start, width):
    parts = [row, jnp.zeros((1, width - start - row.shape[1]), row.dtype)]
    if start:
        parts.insert(0, jnp.zeros((1, start), row.dtype))
    return jnp.concatenate(parts, axis=1)


def load_kernel(*refs):
    sources, (facts_ref, coef_ref, rowk_ref, colk_ref, raw_ref) = refs[:8], refs[8:13]
    patch_ref, cell_ref, band_ref, weight_ref, row_ref, col_ref, coef_in = targets = refs[13:20]
    sems = refs[20]
    copies = [
        pltpu.make_async_copy(source, target, sems.at[i])
        for i, (source, target) in enumerate(zip(sources, targets + (raw_ref,)))
    ]
    for copy in copies:
        copy.start()
    for copy in copies[:-1]:
        copy.wait()
    key = (patch_ref[...] * BANDS + band_ref[...]) * CELLS + cell_ref[...]
    facts_ref[0, 0:1, :] = key.astype(jnp.float32)
    facts_ref[0, 1:2, :] = weight_ref[...].astype(jnp.float32).reshape(1, -1)
    coef_ref[...] = coef_in[...].astype(jnp.float32)
    basis_count, margin_side = row_ref.shape[0], raw_ref.shape[0]
    block_side = rowk_ref.shape[0] // basis_count
    width = colk_ref.shape[0] // basis_count
    for k in range(basis_count):
        rows = banded(lanes_at(row_ref[k : k + 1, :], 0, width), block_side, width)
        rowk_ref[k * block_side : (k + 1) * block_side, :] = rows[:, :margin_side].astype(jnp.bfloat16)
        cols = banded(lanes_at(col_ref[k : k + 1, :], 0, width), block_side, width)
        colk_ref[k * width : (k + 1) * width, :] = cols.T.astype(jnp.bfloat16)
    copies[-1].wait()


def load(patch, cell, band, weight, row_basis, col_basis, coef, raw, block_side):
    basis_count = row_basis.shape[0]
    margin_side = raw.shape[0]
    width = up(margin_side, 128)
    operands = (patch, cell, band, weight, row_basis, col_basis, coef, raw)
    out_shape = [
        jax.ShapeDtypeStruct((1, 2, patch.shape[1]), jnp.float32),
        jax.ShapeDtypeStruct(coef.shape, jnp.float32),
        jax.ShapeDtypeStruct((basis_count * block_side, margin_side), jnp.bfloat16),
        jax.ShapeDtypeStruct((basis_count * width, block_side), jnp.bfloat16),
        jax.ShapeDtypeStruct(raw.shape, raw.dtype),
    ]
    return pl.pallas_call(
        load_kernel,
        out_shape=out_shape,
        in_specs=[pl.BlockSpec(memory_space=pltpu.HBM)] * len(operands),
        out_specs=[pl.BlockSpec(memory_space=VMEM)] * len(out_shape),
        scratch_shapes=[VMEM(value.shape, value.dtype) for value in operands[:-1]]
        + [pltpu.SemaphoreType.DMA((len(operands),))],
        compiler_params=pltpu.CompilerParams(vmem_limit_bytes=12 << 20),
        cost_estimate=pl.CostEstimate(flops=1 << 20, bytes_accessed=4 << 20, transcendentals=0),
        name="load",
    )(*(pltpu.with_memory_space_constraint(value, pltpu.HBM) for value in operands))


def match_kernel(first, count, skip, fresh, after_ref, coef_ref, rowk_ref, colk_ref, raw_ref, *outs):
    margin_side = raw_ref.shape[0]
    basis_count = coef_ref.shape[0]
    outs = outs if fresh else outs[len(outs) // 2 :]
    block_side = outs[0].shape[2]
    width = colk_ref.shape[0] // basis_count
    for n in range(count):
        here = first + n
        block = raw_ref[:, here * margin_side : (here + 1) * margin_side]
        sectioned = jnp.dot(rowk_ref[...], block, preferred_element_type=jnp.float32)
        total = None
        for k in range(basis_count):
            part = sectioned[k * block_side : (k + 1) * block_side] * coef_ref[k : k + 1, here : here + 1]
            term = jnp.dot(
                part.astype(jnp.bfloat16),
                colk_ref[k * width : k * width + margin_side, :],
                preferred_element_type=jnp.float32,
            )
            total = term if total is None else total + term
        total = total.astype(jnp.bfloat16)
        start = 0
        for out_ref in outs:
            out_ref[skip + n] = total[start : start + out_ref.shape[1]]
            start += out_ref.shape[1]


def match_blocks(first, count, size, loaded, rows, block_side, after, into=()):
    raw = loaded[-1]
    basis_count = loaded[0].shape[0]
    skip = size - count if into else 0
    flops = 2 * count * basis_count * block_side * raw.shape[0] * (raw.shape[0] + block_side)
    return pl.pallas_call(
        functools.partial(match_kernel, first, count, skip, not into),
        out_shape=[jax.ShapeDtypeStruct((size, height, block_side), jnp.bfloat16) for height in rows],
        in_specs=[pl.BlockSpec(memory_space=pl.ANY)] + [pl.BlockSpec(memory_space=VMEM)] * (len(loaded) + len(into)),
        out_specs=[pl.BlockSpec(memory_space=VMEM)] * len(rows),
        input_output_aliases={1 + len(loaded) + i: i for i in range(len(into))},
        compiler_params=pltpu.CompilerParams(vmem_limit_bytes=8 << 20),
        cost_estimate=pl.CostEstimate(flops=4 * flops, bytes_accessed=2 << 20, transcendentals=0),
        name="match_blocks",
    )(after, *loaded, *into)


def bin_kernel(stepped, bins_ref, scale_ref, after_ref, *rest):
    blocks_refs, (out_ref, acc_ref) = rest[:-2], rest[-2:]
    parts = len(blocks_refs) // 2
    step = acc_ref.shape[0]
    acc_ref[...] = jnp.zeros_like(acc_ref)
    for index, blocks_ref in enumerate(blocks_refs):
        line, part = index // parts, index % parts
        start = sum(ref.shape[0] for ref in blocks_refs[:part])
        for n in range(blocks_ref.shape[0]):
            slot = bins_ref[line, start + n]
            if stepped:
                slot = slot - pl.program_id(0) * step

            @pl.when((slot >= 0) & (slot < step) if stepped else slot >= 0)
            def _(blocks_ref=blocks_ref, n=n, slot=slot, line=line, place=start + n):
                acc_ref[slot] += scale_ref[line, place] * blocks_ref[n].astype(jnp.float32)

    out_ref[...] = acc_ref[...].astype(out_ref.dtype)


def bin_blocks(bins, scale, blocks, size, name, after):
    shape = blocks[0].shape[1:]
    step = min(size, 64)
    stepped = step < size
    moved = 2 * sum(part.size for part in blocks) + 2 * size * shape[0] * shape[1]
    if stepped:
        grid = (size // step,)
        block_specs = [pl.BlockSpec(part.shape, lambda g: (0, 0, 0)) for part in blocks]
        out_spec = pl.BlockSpec((step,) + shape, lambda g: (g, 0, 0))
    else:
        grid = ()
        block_specs = [pl.BlockSpec(memory_space=VMEM)] * len(blocks)
        out_spec = pl.BlockSpec(memory_space=VMEM)
    return pl.pallas_call(
        functools.partial(bin_kernel, stepped),
        grid=grid,
        out_shape=jax.ShapeDtypeStruct((size,) + shape, jnp.bfloat16),
        in_specs=[pl.BlockSpec(memory_space=SMEM), pl.BlockSpec(memory_space=SMEM), pl.BlockSpec(memory_space=pl.ANY)]
        + block_specs,
        out_specs=out_spec,
        scratch_shapes=[VMEM((step,) + shape, jnp.float32)],
        compiler_params=pltpu.CompilerParams(vmem_limit_bytes=20 << 20),
        cost_estimate=pl.CostEstimate(flops=2 * moved, bytes_accessed=moved, transcendentals=0),
        name=name,
    )(bins, scale, after, *blocks)


def filters_kernel(edge, taps_ref, rows_ref, cols_ref):
    side, rows_in = rows_ref.shape
    radius = (taps_ref.shape[1] - 1) // 2
    taps = taps_ref[...]
    width = up(rows_in + 1, 128)
    rows_ref[...] = banded(lanes_at(taps, edge - radius, width), side, width)[:, :rows_in].astype(jnp.bfloat16)
    cols_ref[...] = banded(lanes_at(taps, side - radius, 3 * side), side, 3 * side).T.astype(jnp.bfloat16)


def filters(taps, side, edge):
    return pl.pallas_call(
        functools.partial(filters_kernel, edge),
        out_shape=[
            jax.ShapeDtypeStruct((side, side + 2 * edge), jnp.bfloat16),
            jax.ShapeDtypeStruct((3 * side, side), jnp.bfloat16),
        ],
        in_specs=[pl.BlockSpec(memory_space=VMEM)],
        out_specs=[pl.BlockSpec(memory_space=VMEM)] * 2,
        compiler_params=pltpu.CompilerParams(vmem_limit_bytes=12 << 20),
        cost_estimate=pl.CostEstimate(flops=1 << 20, bytes_accessed=1 << 20, transcendentals=0),
        name="filters",
    )(taps)


def filter_kernel(row_filter_ref, col_filter_ref, mid_ref, low_ref, high_ref, out_ref):
    cells, side, unused = mid_ref.shape
    zero = jnp.zeros((side, side), jnp.bfloat16)
    smoothed = [zero]
    for c in range(cells):
        column = jnp.concatenate([low_ref[c], mid_ref[c], high_ref[c]], axis=0)
        rows = jnp.dot(row_filter_ref[...], column, preferred_element_type=jnp.float32)
        smoothed.append(rows.astype(jnp.bfloat16))
    smoothed.append(zero)
    for c in range(cells):
        window = jnp.concatenate(smoothed[c : c + 3], axis=1)
        out_ref[:, c * side : (c + 1) * side] = jnp.dot(
            window, col_filter_ref[...], preferred_element_type=jnp.float32
        )


def detect(row_filter, col_filter, mid, low, high):
    cells, side, unused = mid.shape
    return pl.pallas_call(
        filter_kernel,
        out_shape=jax.ShapeDtypeStruct((side, cells * side), jnp.float32),
        in_specs=[pl.BlockSpec(memory_space=VMEM)] * 5,
        out_specs=pl.BlockSpec(memory_space=VMEM),
        compiler_params=pltpu.CompilerParams(vmem_limit_bytes=12 << 20),
        name="detect",
    )(row_filter, col_filter, mid, low, high)


def halves(parts, send):
    total = None
    for part in parts:
        half = part.shape[0] // 2
        piece = (part[half:] if send else part[:half]).astype(jnp.float32)
        total = piece if total is None else total + piece
    return total


def first_halves(parts):
    return [part[: part.shape[0] // 2] for part in parts]


def local(
    raw_blocks,
    patch_of_block,
    cell_of_block,
    band_of_block,
    block_weight,
    basis_coef,
    row_basis,
    col_basis,
    band_gain,
    filter_taps,
):
    sky_count = lax.axis_size("sky")
    band_count = lax.axis_size("band")
    sky_bits = sky_count.bit_length() - 1
    band_bits = band_count.bit_length() - 1
    margin_side = raw_blocks.shape[0]
    block_count = raw_blocks.shape[1] // margin_side
    radius = (filter_taps.shape[0] - 1) // 2
    block_side = margin_side - 2 * radius
    sky_here = lax.axis_index("sky")
    band_here = lax.axis_index("band")

    def swap(array, bit):
        axis, count, bit = ("band", band_count, bit) if bit < band_bits else ("sky", sky_count, bit - band_bits)
        return lax.ppermute(array, axis, [(i, i ^ (1 << bit)) for i in range(count)])

    band_bit, sky_bit, next_bit = 1, band_bits, band_bits + 1
    orders = [[band_bit, next_bit, sky_bit], [sky_bit, band_bit, next_bit]]
    later = list(range(2, band_bits)) + list(range(band_bits + 2, band_bits + sky_bits))
    heights = [block_side // len(orders)] * len(orders)

    own_facts, *loaded = load(
        patch_of_block.reshape(1, -1),
        cell_of_block.reshape(1, -1),
        band_of_block.reshape(1, -1),
        block_weight,
        row_basis,
        col_basis,
        basis_coef.T,
        raw_blocks,
        block_side,
    )
    facts = jnp.concatenate(
        [own_facts]
        + [lax.ppermute(own_facts, "band", [(i, i ^ off) for i in range(band_count)]) for off in range(1, band_count)]
    )
    cut, early = block_count * 5 // 8, block_count * 3 // 8
    own, others = [[], []], [[], []]
    begun = match_blocks(0, early, cut, loaded, heights, block_side, own_facts)
    for part in range(max(2, sky_bits)):
        got = swap(facts, band_bits + part) if part < sky_bits else None
        if part == 0:
            found = match_blocks(early, cut - early, cut, loaded, heights, block_side, facts, begun)
        elif part == 1:
            found = match_blocks(cut, block_count - cut, block_count - cut, loaded, heights, block_side, facts)
        if part < 2:
            for group, order in enumerate(orders):
                own[group].append(found[group])
                others[group].append(swap(found[group], order[0]))
        if got is not None:
            facts = jnp.concatenate([facts, got])

    near = jnp.stack([facts[0]] + [facts[1 << order[0]] for order in orders])
    near_key, near_weight = near[:, 0], near[:, 1]
    same = near_key[:, :, None, None] == facts[None, None, :, 0]
    weight_sum = jnp.sum(jnp.where(same, facts[None, None, :, 1], 0.0), axis=(2, 3))
    near_key = near_key.astype(jnp.int32)
    cell = near_key % CELLS
    band = near_key // CELLS % BANDS
    gain = jnp.sum(jnp.where(band[..., None] == jnp.arange(BANDS), band_gain, 0.0), axis=2)
    scale = gain * near_weight / jnp.maximum(weight_sum, 1.0)

    owner_off = (near_key // (CELLS * BANDS) ^ sky_here) << band_bits | (cell // CC ^ band_here)
    size = (1 << (len(orders[0]) + len(later) - 1)) * CC
    half = size // 2
    blocks, bins, scales = [], [], []
    for group, order in enumerate(orders):
        blocks.append(own[group] + others[group])
        scales.append(jnp.stack([scale[0], scale[group + 1]]))
        off = jnp.stack([owner_off[0], owner_off[group + 1]])
        place = jnp.zeros_like(off)
        for bit in [0] + order[1:] + later:
            place = place * 2 + (off >> bit & 1)
        place = place * CC + jnp.stack([cell[0], cell[group + 1]]) % CC
        place = jnp.where(off >> order[0] & 1 == 0, place, -1)
        bins.append(
            [
                jnp.where((place >= low) & (place < low + count), place - low, -1)
                for low, count in ((size, size), (half, half), (0, half))
            ]
        )
    from_pair = [
        swap(bin_blocks(lines[0], factor, parts, size, "bins_for_pair", others[1 - group][-1]), 0)
        for group, (lines, factor, parts) in enumerate(zip(bins, scales, blocks))
    ]
    edge = up(radius, 16)
    taps = filter_taps.astype(jnp.bfloat16).astype(jnp.float32)[None]
    row_filter, col_filter = filters(taps, block_side, edge)
    groups = []
    for lines, factor, parts, order, mine in zip(bins, scales, blocks, orders, from_pair):
        sent = bin_blocks(lines[1], factor, parts, half, "bins_for_next", factor)
        back = swap((sent.astype(jnp.float32) + mine[half:].astype(jnp.float32)).astype(jnp.bfloat16), order[1])
        kept = bin_blocks(lines[2], factor, parts, half, "bins_kept", row_filter)
        groups.append([kept, mine[:half], back])
    got = [swap(halves(parts, True).astype(jnp.bfloat16), order[2]) for parts, order in zip(groups, orders)]
    groups = [first_halves(parts) + [part] for parts, part in zip(groups, got)]
    joined = []
    for bit in later:
        outgoing = jnp.concatenate([halves(parts, True) for parts in groups], axis=1)
        for part in joined:
            outgoing = outgoing + part[part.shape[0] // 2 :].astype(jnp.float32)
        got = swap(outgoing.astype(jnp.bfloat16), bit)
        groups = [first_halves(parts) for parts in groups]
        joined = first_halves(joined) + [got]

    def full(parts):
        return functools.reduce(jnp.add, [part.astype(jnp.float32) for part in parts])

    combined = jnp.concatenate([full(parts) for parts in groups], axis=1)
    if joined:
        combined = combined + full(joined)
    combined = combined.astype(jnp.bfloat16)

    top, bottom = combined[:, :edge], combined[:, block_side - edge :]
    even = band_here & 1 == 0
    inner = [(i, i + 1) for i in range(1, band_count - 1, 2)]
    beyond = lax.ppermute(jnp.where(even, top, bottom), "band", inner + [(i, j) for j, i in inner])
    paired = swap(jnp.where(even, bottom, top), 0)
    return detect(
        row_filter, col_filter, combined, jnp.where(even, beyond, paired), jnp.where(even, paired, beyond)
    )[None]


def solution(mesh):
    return jax.shard_map(
        local,
        mesh=mesh,
        in_specs=(
            P(None, ("sky", "band")),
            P(("sky", "band"), None),
            P(("sky", "band")),
            P(("sky", "band")),
            P(("sky", "band")),
            P(("sky", "band"), None),
            P(),
            P(),
            P(),
            P(),
        ),
        out_specs=P("sky", "band", None),
        check_vma=False,
    )
```

```python
import functools

import jax
import jax.numpy as jnp
from jax import lax
from jax.experimental import pallas as pl
from jax.experimental.pallas import tpu as pltpu
from jax.sharding import PartitionSpec as P

BANDS = 6
CR = 4
CC = 4
CELLS = 16
VMEM = pltpu.VMEM
SMEM = pltpu.SMEM


def up(value, unit):
    return -(-value // unit) * unit


def banded(row, rows, width):
    tile = pltpu.roll(jnp.broadcast_to(row, (8, width)), 0, 1, stride=1, stride_axis=0)
    return jnp.concatenate([tile if i == 0 else pltpu.roll(tile, 8 * i, 1) for i in range(rows // 8)], axis=0)


def lanes_at(row, start, width):
    parts = [row, jnp.zeros((1, width - start - row.shape[1]), row.dtype)]
    if start:
        parts.insert(0, jnp.zeros((1, start), row.dtype))
    return jnp.concatenate(parts, axis=1)


def load_kernel(*refs):
    sources, (facts_ref, coef_ref, rowk_ref, colk_ref, raw_ref) = refs[:8], refs[8:13]
    patch_ref, cell_ref, band_ref, weight_ref, row_ref, col_ref, coef_in = targets = refs[13:20]
    sems = refs[20]
    copies = [
        pltpu.make_async_copy(source, target, sems.at[i])
        for i, (source, target) in enumerate(zip(sources, targets + (raw_ref,)))
    ]
    for copy in copies:
        copy.start()
    for copy in copies[:-1]:
        copy.wait()
    key = (patch_ref[...] * BANDS + band_ref[...]) * CELLS + cell_ref[...]
    facts_ref[0, 0:1, :] = key.astype(jnp.float32)
    facts_ref[0, 1:2, :] = weight_ref[...].astype(jnp.float32).reshape(1, -1)
    coef_ref[...] = coef_in[...].astype(jnp.float32)
    basis_count, margin_side = row_ref.shape[0], raw_ref.shape[0]
    block_side = rowk_ref.shape[0] // basis_count
    width = colk_ref.shape[0] // basis_count
    for k in range(basis_count):
        rows = banded(lanes_at(row_ref[k : k + 1, :], 0, width), block_side, width)
        rowk_ref[k * block_side : (k + 1) * block_side, :] = rows[:, :margin_side].astype(jnp.bfloat16)
        cols = banded(lanes_at(col_ref[k : k + 1, :], 0, width), block_side, width)
        colk_ref[k * width : (k + 1) * width, :] = cols.T.astype(jnp.bfloat16)
    copies[-1].wait()


def load(patch, cell, band, weight, row_basis, col_basis, coef, raw, block_side):
    basis_count = row_basis.shape[0]
    margin_side = raw.shape[0]
    width = up(margin_side, 128)
    operands = (patch, cell, band, weight, row_basis, col_basis, coef, raw)
    out_shape = [
        jax.ShapeDtypeStruct((1, 2, patch.shape[1]), jnp.float32),
        jax.ShapeDtypeStruct(coef.shape, jnp.float32),
        jax.ShapeDtypeStruct((basis_count * block_side, margin_side), jnp.bfloat16),
        jax.ShapeDtypeStruct((basis_count * width, block_side), jnp.bfloat16),
        jax.ShapeDtypeStruct(raw.shape, raw.dtype),
    ]
    return pl.pallas_call(
        load_kernel,
        out_shape=out_shape,
        in_specs=[pl.BlockSpec(memory_space=pltpu.HBM)] * len(operands),
        out_specs=[pl.BlockSpec(memory_space=VMEM)] * len(out_shape),
        scratch_shapes=[VMEM(value.shape, value.dtype) for value in operands[:-1]]
        + [pltpu.SemaphoreType.DMA((len(operands),))],
        compiler_params=pltpu.CompilerParams(vmem_limit_bytes=12 << 20),
        cost_estimate=pl.CostEstimate(flops=1 << 20, bytes_accessed=4 << 20, transcendentals=0),
        name="load",
    )(*(pltpu.with_memory_space_constraint(value, pltpu.HBM) for value in operands))


def match_kernel(first, count, skip, fresh, after_ref, coef_ref, rowk_ref, colk_ref, raw_ref, *outs):
    margin_side = raw_ref.shape[0]
    basis_count = coef_ref.shape[0]
    outs = outs if fresh else outs[len(outs) // 2 :]
    block_side = outs[0].shape[2]
    width = colk_ref.shape[0] // basis_count
    for n in range(count):
        here = first + n
        block = raw_ref[:, here * margin_side : (here + 1) * margin_side]
        sectioned = jnp.dot(rowk_ref[...], block, preferred_element_type=jnp.float32)
        total = None
        for k in range(basis_count):
            part = sectioned[k * block_side : (k + 1) * block_side] * coef_ref[k : k + 1, here : here + 1]
            term = jnp.dot(
                part.astype(jnp.bfloat16),
                colk_ref[k * width : k * width + margin_side, :],
                preferred_element_type=jnp.float32,
            )
            total = term if total is None else total + term
        total = total.astype(jnp.bfloat16)
        start = 0
        for out_ref in outs:
            out_ref[skip + n] = total[start : start + out_ref.shape[1]]
            start += out_ref.shape[1]


def match_blocks(first, count, size, loaded, rows, block_side, after, into=()):
    raw = loaded[-1]
    basis_count = loaded[0].shape[0]
    skip = size - count if into else 0
    flops = 2 * count * basis_count * block_side * raw.shape[0] * (raw.shape[0] + block_side)
    return pl.pallas_call(
        functools.partial(match_kernel, first, count, skip, not into),
        out_shape=[jax.ShapeDtypeStruct((size, height, block_side), jnp.bfloat16) for height in rows],
        in_specs=[pl.BlockSpec(memory_space=pl.ANY)] + [pl.BlockSpec(memory_space=VMEM)] * (len(loaded) + len(into)),
        out_specs=[pl.BlockSpec(memory_space=VMEM)] * len(rows),
        input_output_aliases={1 + len(loaded) + i: i for i in range(len(into))},
        compiler_params=pltpu.CompilerParams(vmem_limit_bytes=8 << 20),
        cost_estimate=pl.CostEstimate(flops=4 * flops, bytes_accessed=2 << 20, transcendentals=0),
        name="match_blocks",
    )(after, *loaded, *into)


def bin_kernel(stepped, bins_ref, scale_ref, after_ref, *rest):
    blocks_refs, (out_ref, acc_ref) = rest[:-2], rest[-2:]
    parts = len(blocks_refs) // 2
    step = acc_ref.shape[0]
    acc_ref[...] = jnp.zeros_like(acc_ref)
    for index, blocks_ref in enumerate(blocks_refs):
        line, part = index // parts, index % parts
        start = sum(ref.shape[0] for ref in blocks_refs[:part])
        for n in range(blocks_ref.shape[0]):
            slot = bins_ref[line, start + n]
            if stepped:
                slot = slot - pl.program_id(0) * step

            @pl.when((slot >= 0) & (slot < step) if stepped else slot >= 0)
            def _(blocks_ref=blocks_ref, n=n, slot=slot, line=line, place=start + n):
                acc_ref[slot] += scale_ref[line, place] * blocks_ref[n].astype(jnp.float32)

    out_ref[...] = acc_ref[...].astype(out_ref.dtype)


def bin_blocks(bins, scale, blocks, size, name, after):
    shape = blocks[0].shape[1:]
    step = min(size, 64)
    stepped = step < size
    moved = 2 * sum(part.size for part in blocks) + 2 * size * shape[0] * shape[1]
    if stepped:
        grid = (size // step,)
        block_specs = [pl.BlockSpec(part.shape, lambda g: (0, 0, 0)) for part in blocks]
        out_spec = pl.BlockSpec((step,) + shape, lambda g: (g, 0, 0))
    else:
        grid = ()
        block_specs = [pl.BlockSpec(memory_space=VMEM)] * len(blocks)
        out_spec = pl.BlockSpec(memory_space=VMEM)
    return pl.pallas_call(
        functools.partial(bin_kernel, stepped),
        grid=grid,
        out_shape=jax.ShapeDtypeStruct((size,) + shape, jnp.bfloat16),
        in_specs=[pl.BlockSpec(memory_space=SMEM), pl.BlockSpec(memory_space=SMEM), pl.BlockSpec(memory_space=pl.ANY)]
        + block_specs,
        out_specs=out_spec,
        scratch_shapes=[VMEM((step,) + shape, jnp.float32)],
        compiler_params=pltpu.CompilerParams(vmem_limit_bytes=20 << 20),
        cost_estimate=pl.CostEstimate(flops=2 * moved, bytes_accessed=moved, transcendentals=0),
        name=name,
    )(bins, scale, after, *blocks)


def filters_kernel(edge, taps_ref, rows_ref, cols_ref):
    side, rows_in = rows_ref.shape
    radius = (taps_ref.shape[1] - 1) // 2
    taps = taps_ref[...]
    width = up(rows_in + 1, 128)
    rows_ref[...] = banded(lanes_at(taps, edge - radius, width), side, width)[:, :rows_in].astype(jnp.bfloat16)
    cols_ref[...] = banded(lanes_at(taps, side - radius, 3 * side), side, 3 * side).T.astype(jnp.bfloat16)


def filters(taps, side, edge):
    return pl.pallas_call(
        functools.partial(filters_kernel, edge),
        out_shape=[
            jax.ShapeDtypeStruct((side, side + 2 * edge), jnp.bfloat16),
            jax.ShapeDtypeStruct((3 * side, side), jnp.bfloat16),
        ],
        in_specs=[pl.BlockSpec(memory_space=VMEM)],
        out_specs=[pl.BlockSpec(memory_space=VMEM)] * 2,
        compiler_params=pltpu.CompilerParams(vmem_limit_bytes=12 << 20),
        cost_estimate=pl.CostEstimate(flops=1 << 20, bytes_accessed=1 << 20, transcendentals=0),
        name="filters",
    )(taps)


def smooth_kernel(even_ref, row_filter_ref, mid_ref, beyond_ref, out_ref):
    cells, side, unused = mid_ref.shape
    edge = beyond_ref.shape[1]
    above, below = row_filter_ref[:, :edge], row_filter_ref[:, edge + side :]
    outer = jnp.where(even_ref[0] != 0, above.astype(jnp.float32), below.astype(jnp.float32)).astype(jnp.bfloat16)
    for c in range(cells):
        out_ref[c] = jnp.dot(
            row_filter_ref[:, edge : edge + side], mid_ref[c], preferred_element_type=jnp.float32
        ) + jnp.dot(outer, beyond_ref[c], preferred_element_type=jnp.float32)


def smooth(even, row_filter, mid, beyond):
    return pl.pallas_call(
        smooth_kernel,
        out_shape=jax.ShapeDtypeStruct(mid.shape, jnp.float32),
        in_specs=[pl.BlockSpec(memory_space=SMEM)] + [pl.BlockSpec(memory_space=VMEM)] * 3,
        out_specs=pl.BlockSpec(memory_space=VMEM),
        compiler_params=pltpu.CompilerParams(vmem_limit_bytes=12 << 20),
        cost_estimate=pl.CostEstimate(flops=1 << 26, bytes_accessed=1 << 20, transcendentals=0),
        name="smooth",
    )(even, row_filter, mid, beyond)


def detect_kernel(even_ref, row_filter_ref, col_filter_ref, partial_ref, paired_ref, out_ref):
    cells, side, unused = partial_ref.shape
    edge = paired_ref.shape[1]
    above, below = row_filter_ref[:, :edge], row_filter_ref[:, edge + side :]
    outer = jnp.where(even_ref[0] != 0, below.astype(jnp.float32), above.astype(jnp.float32)).astype(jnp.bfloat16)
    zero = jnp.zeros((side, side), jnp.bfloat16)
    smoothed = [zero]
    for c in range(cells):
        rows = partial_ref[c] + jnp.dot(outer, paired_ref[c], preferred_element_type=jnp.float32)
        smoothed.append(rows.astype(jnp.bfloat16))
    smoothed.append(zero)
    for c in range(cells):
        window = jnp.concatenate(smoothed[c : c + 3], axis=1)
        out_ref[:, c * side : (c + 1) * side] = jnp.dot(
            window, col_filter_ref[...], preferred_element_type=jnp.float32
        )


def detect(even, row_filter, col_filter, partial, paired):
    cells, side, unused = partial.shape
    return pl.pallas_call(
        detect_kernel,
        out_shape=jax.ShapeDtypeStruct((side, cells * side), jnp.float32),
        in_specs=[pl.BlockSpec(memory_space=SMEM)] + [pl.BlockSpec(memory_space=VMEM)] * 4,
        out_specs=pl.BlockSpec(memory_space=VMEM),
        compiler_params=pltpu.CompilerParams(vmem_limit_bytes=12 << 20),
        name="detect",
    )(even, row_filter, col_filter, partial, paired)


def halves(parts, send):
    total = None
    for part in parts:
        half = part.shape[0] // 2
        piece = (part[half:] if send else part[:half]).astype(jnp.float32)
        total = piece if total is None else total + piece
    return total


def first_halves(parts):
    return [part[: part.shape[0] // 2] for part in parts]


def local(
    raw_blocks,
    patch_of_block,
    cell_of_block,
    band_of_block,
    block_weight,
    basis_coef,
    row_basis,
    col_basis,
    band_gain,
    filter_taps,
):
    sky_count = lax.axis_size("sky")
    band_count = lax.axis_size("band")
    sky_bits = sky_count.bit_length() - 1
    band_bits = band_count.bit_length() - 1
    margin_side = raw_blocks.shape[0]
    block_count = raw_blocks.shape[1] // margin_side
    radius = (filter_taps.shape[0] - 1) // 2
    block_side = margin_side - 2 * radius
    sky_here = lax.axis_index("sky")
    band_here = lax.axis_index("band")

    def swap(array, bit):
        axis, count, bit = ("band", band_count, bit) if bit < band_bits else ("sky", sky_count, bit - band_bits)
        return lax.ppermute(array, axis, [(i, i ^ (1 << bit)) for i in range(count)])

    band_bit, sky_bit, next_bit = 1, band_bits, band_bits + 1
    orders = [[band_bit, next_bit, sky_bit], [sky_bit, band_bit, next_bit]]
    later = list(range(2, band_bits)) + list(range(band_bits + 2, band_bits + sky_bits))
    heights = [block_side // len(orders)] * len(orders)

    own_facts, *loaded = load(
        patch_of_block.reshape(1, -1),
        cell_of_block.reshape(1, -1),
        band_of_block.reshape(1, -1),
        block_weight,
        row_basis,
        col_basis,
        basis_coef.T,
        raw_blocks,
        block_side,
    )
    facts = jnp.concatenate(
        [own_facts]
        + [lax.ppermute(own_facts, "band", [(i, i ^ off) for i in range(band_count)]) for off in range(1, band_count)]
    )
    cut, early = block_count * 5 // 8, block_count * 3 // 8
    own, others = [[], []], [[], []]
    begun = match_blocks(0, early, cut, loaded, heights, block_side, own_facts)
    for part in range(max(2, sky_bits)):
        got = swap(facts, band_bits + part) if part < sky_bits else None
        if part == 0:
            found = match_blocks(early, cut - early, cut, loaded, heights, block_side, facts, begun)
        elif part == 1:
            found = match_blocks(cut, block_count - cut, block_count - cut, loaded, heights, block_side, facts)
        if part < 2:
            for group, order in enumerate(orders):
                own[group].append(found[group])
                others[group].append(swap(found[group], order[0]))
        if got is not None:
            facts = jnp.concatenate([facts, got])

    near = jnp.stack([facts[0]] + [facts[1 << order[0]] for order in orders])
    near_key, near_weight = near[:, 0], near[:, 1]
    same = near_key[:, :, None, None] == facts[None, None, :, 0]
    weight_sum = jnp.sum(jnp.where(same, facts[None, None, :, 1], 0.0), axis=(2, 3))
    near_key = near_key.astype(jnp.int32)
    cell = near_key % CELLS
    band = near_key // CELLS % BANDS
    gain = jnp.sum(jnp.where(band[..., None] == jnp.arange(BANDS), band_gain, 0.0), axis=2)
    scale = gain * near_weight / jnp.maximum(weight_sum, 1.0)

    owner_off = (near_key // (CELLS * BANDS) ^ sky_here) << band_bits | (cell // CC ^ band_here)
    size = (1 << (len(orders[0]) + len(later) - 1)) * CC
    half = size // 2
    blocks, bins, scales = [], [], []
    for group, order in enumerate(orders):
        blocks.append(own[group] + others[group])
        scales.append(jnp.stack([scale[0], scale[group + 1]]))
        off = jnp.stack([owner_off[0], owner_off[group + 1]])
        place = jnp.zeros_like(off)
        for bit in [0] + order[1:] + later:
            place = place * 2 + (off >> bit & 1)
        place = place * CC + jnp.stack([cell[0], cell[group + 1]]) % CC
        place = jnp.where(off >> order[0] & 1 == 0, place, -1)
        bins.append(
            [
                jnp.where((place >= low) & (place < low + count), place - low, -1)
                for low, count in ((size, size), (half, half), (0, half))
            ]
        )
    from_pair = [
        swap(bin_blocks(lines[0], factor, parts, size, "bins_for_pair", others[1 - group][-1]), 0)
        for group, (lines, factor, parts) in enumerate(zip(bins, scales, blocks))
    ]
    edge = up(radius, 16)
    taps = filter_taps.astype(jnp.bfloat16).astype(jnp.float32)[None]
    row_filter, col_filter = filters(taps, block_side, edge)
    groups = []
    for lines, factor, parts, order, mine in zip(bins, scales, blocks, orders, from_pair):
        known = factor if mine is from_pair[1] else from_pair[1]
        sent = bin_blocks(lines[1], factor, parts, half, "bins_for_next", known)
        back = swap((sent.astype(jnp.float32) + mine[half:].astype(jnp.float32)).astype(jnp.bfloat16), order[1])
        kept = bin_blocks(lines[2], factor, parts, half, "bins_kept", row_filter)
        groups.append([kept, mine[:half], back])
    got = [swap(halves(parts, True).astype(jnp.bfloat16), order[2]) for parts, order in zip(groups, orders)]
    groups = [first_halves(parts) + [part] for parts, part in zip(groups, got)]
    joined = []
    for bit in later:
        outgoing = jnp.concatenate([halves(parts, True) for parts in groups], axis=1)
        for part in joined:
            outgoing = outgoing + part[part.shape[0] // 2 :].astype(jnp.float32)
        got = swap(outgoing.astype(jnp.bfloat16), bit)
        groups = [first_halves(parts) for parts in groups]
        joined = first_halves(joined) + [got]

    def full(parts):
        return functools.reduce(jnp.add, [part.astype(jnp.float32) for part in parts])

    combined = jnp.concatenate([full(parts) for parts in groups], axis=1)
    if joined:
        combined = combined + full(joined)
    combined = combined.astype(jnp.bfloat16)

    top, bottom = combined[:, :edge], combined[:, block_side - edge :]
    even = band_here & 1 == 0
    inner = [(i, i + 1) for i in range(1, band_count - 1, 2)]
    beyond = lax.ppermute(jnp.where(even, top, bottom), "band", inner + [(i, j) for j, i in inner])
    paired = swap(jnp.where(even, bottom, top), 0)
    side = even.astype(jnp.int32)[None]
    partial = smooth(side, row_filter, combined, beyond)
    return detect(side, row_filter, col_filter, partial, paired)[None]


def solution(mesh):
    return jax.shard_map(
        local,
        mesh=mesh,
        in_specs=(
            P(None, ("sky", "band")),
            P(("sky", "band"), None),
            P(("sky", "band")),
            P(("sky", "band")),
            P(("sky", "band")),
            P(("sky", "band"), None),
            P(),
            P(),
            P(),
            P(),
        ),
        out_specs=P("sky", "band", None),
        check_vma=False,
    )
```

```python
import functools

import jax
import jax.numpy as jnp
from jax import lax
from jax.experimental import pallas as pl
from jax.experimental.pallas import tpu as pltpu
from jax.sharding import PartitionSpec as P

BANDS = 6
CR = 4
CC = 4
CELLS = 16
VMEM = pltpu.VMEM
SMEM = pltpu.SMEM


def up(value, unit):
    return -(-value // unit) * unit


def banded(row, rows, width):
    tile = pltpu.roll(jnp.broadcast_to(row, (8, width)), 0, 1, stride=1, stride_axis=0)
    return jnp.concatenate([tile if i == 0 else pltpu.roll(tile, 8 * i, 1) for i in range(rows // 8)], axis=0)


def lanes_at(row, start, width):
    parts = [row, jnp.zeros((1, width - start - row.shape[1]), row.dtype)]
    if start:
        parts.insert(0, jnp.zeros((1, start), row.dtype))
    return jnp.concatenate(parts, axis=1)


def load_kernel(groups, *refs):
    sources, (facts_ref, coef_ref, rowk_ref, colk_ref, raw_ref) = refs[:8], refs[8:13]
    patch_ref, cell_ref, band_ref, weight_ref, row_ref, col_ref, coef_in = targets = refs[13:20]
    sems = refs[20]
    copies = [
        pltpu.make_async_copy(source, target, sems.at[i])
        for i, (source, target) in enumerate(zip(sources, targets + (raw_ref,)))
    ]
    for copy in copies:
        copy.start()
    for copy in copies[:-1]:
        copy.wait()
    key = (patch_ref[...] * BANDS + band_ref[...]) * CELLS + cell_ref[...]
    facts_ref[0, 0:1, :] = key.astype(jnp.float32)
    facts_ref[0, 1:2, :] = weight_ref[...].astype(jnp.float32).reshape(1, -1)
    coef_ref[...] = coef_in[...].astype(jnp.float32)
    basis_count, margin_side = row_ref.shape[0], raw_ref.shape[0]
    block_side = rowk_ref.shape[0] // basis_count
    width = colk_ref.shape[0] // basis_count
    for k in range(basis_count):
        rows = banded(lanes_at(row_ref[k : k + 1, :], 0, width), block_side, width)
        rows = rows[:, :margin_side].astype(jnp.bfloat16)
        height = block_side // groups
        for group in range(groups):
            place = (group * basis_count + k) * height
            rowk_ref[place : place + height, :] = rows[group * height : (group + 1) * height]
        cols = banded(lanes_at(col_ref[k : k + 1, :], 0, width), block_side, width)
        colk_ref[k * width : (k + 1) * width, :] = cols.T.astype(jnp.bfloat16)
    copies[-1].wait()


def load(patch, cell, band, weight, row_basis, col_basis, coef, raw, block_side, groups):
    basis_count = row_basis.shape[0]
    margin_side = raw.shape[0]
    width = up(margin_side, 128)
    operands = (patch, cell, band, weight, row_basis, col_basis, coef, raw)
    out_shape = [
        jax.ShapeDtypeStruct((1, 2, patch.shape[1]), jnp.float32),
        jax.ShapeDtypeStruct(coef.shape, jnp.float32),
        jax.ShapeDtypeStruct((basis_count * block_side, margin_side), jnp.bfloat16),
        jax.ShapeDtypeStruct((basis_count * width, block_side), jnp.bfloat16),
        jax.ShapeDtypeStruct(raw.shape, raw.dtype),
    ]
    return pl.pallas_call(
        functools.partial(load_kernel, groups),
        out_shape=out_shape,
        in_specs=[pl.BlockSpec(memory_space=pltpu.HBM)] * len(operands),
        out_specs=[pl.BlockSpec(memory_space=VMEM)] * len(out_shape),
        scratch_shapes=[VMEM(value.shape, value.dtype) for value in operands[:-1]]
        + [pltpu.SemaphoreType.DMA((len(operands),))],
        compiler_params=pltpu.CompilerParams(vmem_limit_bytes=12 << 20),
        cost_estimate=pl.CostEstimate(flops=1 << 20, bytes_accessed=4 << 20, transcendentals=0),
        name="load",
    )(*(pltpu.with_memory_space_constraint(value, pltpu.HBM) for value in operands))


def match_kernel(group, after_ref, coef_ref, rowk_ref, colk_ref, raw_ref, out_ref):
    margin_side = raw_ref.shape[0]
    basis_count = coef_ref.shape[0]
    count, height, unused = out_ref.shape
    width = colk_ref.shape[0] // basis_count
    rows = rowk_ref[group * basis_count * height : (group + 1) * basis_count * height, :]
    for n in range(count):
        block = raw_ref[:, n * margin_side : (n + 1) * margin_side]
        sectioned = jnp.dot(rows, block, preferred_element_type=jnp.float32)
        total = None
        for k in range(basis_count):
            part = sectioned[k * height : (k + 1) * height] * coef_ref[k : k + 1, n : n + 1]
            term = jnp.dot(
                part.astype(jnp.bfloat16),
                colk_ref[k * width : k * width + margin_side, :],
                preferred_element_type=jnp.float32,
            )
            total = term if total is None else total + term
        out_ref[n] = total.astype(jnp.bfloat16)


def match_blocks(group, height, loaded, after):
    coef, unused, cols, raw = loaded
    basis_count, count = coef.shape
    flops = 2 * count * basis_count * height * raw.shape[0] * (raw.shape[0] + cols.shape[1])
    return pl.pallas_call(
        functools.partial(match_kernel, group),
        out_shape=jax.ShapeDtypeStruct((count, height, cols.shape[1]), jnp.bfloat16),
        in_specs=[pl.BlockSpec(memory_space=pl.ANY)] + [pl.BlockSpec(memory_space=VMEM)] * len(loaded),
        out_specs=pl.BlockSpec(memory_space=VMEM),
        compiler_params=pltpu.CompilerParams(vmem_limit_bytes=8 << 20),
        cost_estimate=pl.CostEstimate(flops=4 * flops, bytes_accessed=2 << 20, transcendentals=0),
        name="match_blocks",
    )(after, *loaded)


def bin_kernel(stepped, bins_ref, scale_ref, after_ref, *rest):
    blocks_refs, (out_ref, acc_ref) = rest[:-2], rest[-2:]
    parts = len(blocks_refs) // 2
    step = acc_ref.shape[0]
    acc_ref[...] = jnp.zeros_like(acc_ref)
    for index, blocks_ref in enumerate(blocks_refs):
        line, part = index // parts, index % parts
        start = sum(ref.shape[0] for ref in blocks_refs[:part])
        for n in range(blocks_ref.shape[0]):
            slot = bins_ref[line, start + n]
            if stepped:
                slot = slot - pl.program_id(0) * step

            @pl.when((slot >= 0) & (slot < step) if stepped else slot >= 0)
            def _(blocks_ref=blocks_ref, n=n, slot=slot, line=line, place=start + n):
                acc_ref[slot] += scale_ref[line, place] * blocks_ref[n].astype(jnp.float32)

    out_ref[...] = acc_ref[...].astype(out_ref.dtype)


def bin_blocks(bins, scale, blocks, size, name, after):
    shape = blocks[0].shape[1:]
    step = min(size, 64)
    stepped = step < size
    moved = 2 * sum(part.size for part in blocks) + 2 * size * shape[0] * shape[1]
    if stepped:
        grid = (size // step,)
        block_specs = [pl.BlockSpec(part.shape, lambda g: (0, 0, 0)) for part in blocks]
        out_spec = pl.BlockSpec((step,) + shape, lambda g: (g, 0, 0))
    else:
        grid = ()
        block_specs = [pl.BlockSpec(memory_space=VMEM)] * len(blocks)
        out_spec = pl.BlockSpec(memory_space=VMEM)
    return pl.pallas_call(
        functools.partial(bin_kernel, stepped),
        grid=grid,
        out_shape=jax.ShapeDtypeStruct((size,) + shape, jnp.bfloat16),
        in_specs=[pl.BlockSpec(memory_space=SMEM), pl.BlockSpec(memory_space=SMEM), pl.BlockSpec(memory_space=pl.ANY)]
        + block_specs,
        out_specs=out_spec,
        scratch_shapes=[VMEM((step,) + shape, jnp.float32)],
        compiler_params=pltpu.CompilerParams(vmem_limit_bytes=20 << 20),
        cost_estimate=pl.CostEstimate(flops=2 * moved, bytes_accessed=moved, transcendentals=0),
        name=name,
    )(bins, scale, after, *blocks)


def filters_kernel(edge, taps_ref, rows_ref, cols_ref):
    side, rows_in = rows_ref.shape
    radius = (taps_ref.shape[1] - 1) // 2
    taps = taps_ref[...]
    width = up(rows_in + 1, 128)
    rows_ref[...] = banded(lanes_at(taps, edge - radius, width), side, width)[:, :rows_in].astype(jnp.bfloat16)
    cols_ref[...] = banded(lanes_at(taps, side - radius, 3 * side), side, 3 * side).T.astype(jnp.bfloat16)


def filters(taps, side, edge):
    return pl.pallas_call(
        functools.partial(filters_kernel, edge),
        out_shape=[
            jax.ShapeDtypeStruct((side, side + 2 * edge), jnp.bfloat16),
            jax.ShapeDtypeStruct((3 * side, side), jnp.bfloat16),
        ],
        in_specs=[pl.BlockSpec(memory_space=VMEM)],
        out_specs=[pl.BlockSpec(memory_space=VMEM)] * 2,
        compiler_params=pltpu.CompilerParams(vmem_limit_bytes=12 << 20),
        cost_estimate=pl.CostEstimate(flops=1 << 20, bytes_accessed=1 << 20, transcendentals=0),
        name="filters",
    )(taps)


def smooth_kernel(even_ref, row_filter_ref, mid_ref, beyond_ref, out_ref):
    cells, side, unused = mid_ref.shape
    edge = beyond_ref.shape[1]
    above, below = row_filter_ref[:, :edge], row_filter_ref[:, edge + side :]
    outer = jnp.where(even_ref[0] != 0, above.astype(jnp.float32), below.astype(jnp.float32)).astype(jnp.bfloat16)
    for c in range(cells):
        out_ref[c] = jnp.dot(
            row_filter_ref[:, edge : edge + side], mid_ref[c], preferred_element_type=jnp.float32
        ) + jnp.dot(outer, beyond_ref[c], preferred_element_type=jnp.float32)


def smooth(even, row_filter, mid, beyond):
    return pl.pallas_call(
        smooth_kernel,
        out_shape=jax.ShapeDtypeStruct(mid.shape, jnp.float32),
        in_specs=[pl.BlockSpec(memory_space=SMEM)] + [pl.BlockSpec(memory_space=VMEM)] * 3,
        out_specs=pl.BlockSpec(memory_space=VMEM),
        compiler_params=pltpu.CompilerParams(vmem_limit_bytes=12 << 20),
        cost_estimate=pl.CostEstimate(flops=1 << 26, bytes_accessed=1 << 20, transcendentals=0),
        name="smooth",
    )(even, row_filter, mid, beyond)


def detect_kernel(even_ref, row_filter_ref, col_filter_ref, partial_ref, paired_ref, out_ref):
    cells, side, unused = partial_ref.shape
    edge = paired_ref.shape[1]
    above, below = row_filter_ref[:, :edge], row_filter_ref[:, edge + side :]
    outer = jnp.where(even_ref[0] != 0, below.astype(jnp.float32), above.astype(jnp.float32)).astype(jnp.bfloat16)
    zero = jnp.zeros((side, side), jnp.bfloat16)
    smoothed = [zero]
    for c in range(cells):
        rows = partial_ref[c] + jnp.dot(outer, paired_ref[c], preferred_element_type=jnp.float32)
        smoothed.append(rows.astype(jnp.bfloat16))
    smoothed.append(zero)
    for c in range(cells):
        window = jnp.concatenate(smoothed[c : c + 3], axis=1)
        out_ref[:, c * side : (c + 1) * side] = jnp.dot(
            window, col_filter_ref[...], preferred_element_type=jnp.float32
        )


def detect(even, row_filter, col_filter, partial, paired):
    cells, side, unused = partial.shape
    return pl.pallas_call(
        detect_kernel,
        out_shape=jax.ShapeDtypeStruct((side, cells * side), jnp.float32),
        in_specs=[pl.BlockSpec(memory_space=SMEM)] + [pl.BlockSpec(memory_space=VMEM)] * 4,
        out_specs=pl.BlockSpec(memory_space=VMEM),
        compiler_params=pltpu.CompilerParams(vmem_limit_bytes=12 << 20),
        name="detect",
    )(even, row_filter, col_filter, partial, paired)


def halves(parts, send):
    total = None
    for part in parts:
        half = part.shape[0] // 2
        piece = (part[half:] if send else part[:half]).astype(jnp.float32)
        total = piece if total is None else total + piece
    return total


def first_halves(parts):
    return [part[: part.shape[0] // 2] for part in parts]


def local(
    raw_blocks,
    patch_of_block,
    cell_of_block,
    band_of_block,
    block_weight,
    basis_coef,
    row_basis,
    col_basis,
    band_gain,
    filter_taps,
):
    sky_count = lax.axis_size("sky")
    band_count = lax.axis_size("band")
    sky_bits = sky_count.bit_length() - 1
    band_bits = band_count.bit_length() - 1
    margin_side = raw_blocks.shape[0]
    block_count = raw_blocks.shape[1] // margin_side
    radius = (filter_taps.shape[0] - 1) // 2
    block_side = margin_side - 2 * radius
    sky_here = lax.axis_index("sky")
    band_here = lax.axis_index("band")

    def swap(array, bit):
        axis, count, bit = ("band", band_count, bit) if bit < band_bits else ("sky", sky_count, bit - band_bits)
        return lax.ppermute(array, axis, [(i, i ^ (1 << bit)) for i in range(count)])

    band_bit, sky_bit, next_bit = 1, band_bits, band_bits + 1
    orders = [[band_bit, next_bit, sky_bit], [sky_bit, band_bit, next_bit]]
    later = list(range(2, band_bits)) + list(range(band_bits + 2, band_bits + sky_bits))

    own_facts, *loaded = load(
        patch_of_block.reshape(1, -1),
        cell_of_block.reshape(1, -1),
        band_of_block.reshape(1, -1),
        block_weight,
        row_basis,
        col_basis,
        basis_coef.T,
        raw_blocks,
        block_side,
        len(orders),
    )
    facts = chip_facts = jnp.concatenate(
        [own_facts]
        + [lax.ppermute(own_facts, "band", [(i, i ^ off) for i in range(band_count)]) for off in range(1, band_count)]
    )
    height = block_side // len(orders)
    own, others = [], []
    for part in range(max(len(orders), sky_bits)):
        got = swap(facts, band_bits + part) if part < sky_bits else None
        if part < len(orders):
            found = match_blocks(part, height, loaded, own_facts if part == 0 else chip_facts)
            own.append([found])
            others.append([swap(found, orders[part][0])])
        if got is not None:
            facts = jnp.concatenate([facts, got])

    near = jnp.stack([facts[0]] + [facts[1 << order[0]] for order in orders])
    near_key, near_weight = near[:, 0], near[:, 1]
    same = near_key[:, :, None, None] == facts[None, None, :, 0]
    weight_sum = jnp.sum(jnp.where(same, facts[None, None, :, 1], 0.0), axis=(2, 3))
    near_key = near_key.astype(jnp.int32)
    cell = near_key % CELLS
    band = near_key // CELLS % BANDS
    gain = jnp.sum(jnp.where(band[..., None] == jnp.arange(BANDS), band_gain, 0.0), axis=2)
    scale = gain * near_weight / jnp.maximum(weight_sum, 1.0)

    owner_off = (near_key // (CELLS * BANDS) ^ sky_here) << band_bits | (cell // CC ^ band_here)
    size = (1 << (len(orders[0]) + len(later) - 1)) * CC
    half = size // 2
    blocks, bins, scales = [], [], []
    for group, order in enumerate(orders):
        blocks.append(own[group] + others[group])
        scales.append(jnp.stack([scale[0], scale[group + 1]]))
        off = jnp.stack([owner_off[0], owner_off[group + 1]])
        place = jnp.zeros_like(off)
        for bit in [0] + order[1:] + later:
            place = place * 2 + (off >> bit & 1)
        place = place * CC + jnp.stack([cell[0], cell[group + 1]]) % CC
        place = jnp.where(off >> order[0] & 1 == 0, place, -1)
        bins.append(
            [
                jnp.where((place >= low) & (place < low + count), place - low, -1)
                for low, count in ((size, size), (half, half), (0, half))
            ]
        )
    from_pair = [
        swap(bin_blocks(lines[0], factor, parts, size, "bins_for_pair", others[1 - group][-1]), 0)
        for group, (lines, factor, parts) in enumerate(zip(bins, scales, blocks))
    ]
    edge = up(radius, 16)
    taps = filter_taps.astype(jnp.bfloat16).astype(jnp.float32)[None]
    row_filter, col_filter = filters(taps, block_side, edge)
    groups = []
    for lines, factor, parts, order, mine in zip(bins, scales, blocks, orders, from_pair):
        known = factor if mine is from_pair[1] else from_pair[1]
        sent = bin_blocks(lines[1], factor, parts, half, "bins_for_next", known)
        back = swap((sent.astype(jnp.float32) + mine[half:].astype(jnp.float32)).astype(jnp.bfloat16), order[1])
        kept = bin_blocks(lines[2], factor, parts, half, "bins_kept", row_filter)
        groups.append([kept, mine[:half], back])
    got = [swap(halves(parts, True).astype(jnp.bfloat16), order[2]) for parts, order in zip(groups, orders)]
    groups = [first_halves(parts) + [part] for parts, part in zip(groups, got)]
    joined = []
    for bit in later:
        outgoing = jnp.concatenate([halves(parts, True) for parts in groups], axis=1)
        for part in joined:
            outgoing = outgoing + part[part.shape[0] // 2 :].astype(jnp.float32)
        got = swap(outgoing.astype(jnp.bfloat16), bit)
        groups = [first_halves(parts) for parts in groups]
        joined = first_halves(joined) + [got]

    def full(parts):
        return functools.reduce(jnp.add, [part.astype(jnp.float32) for part in parts])

    combined = jnp.concatenate([full(parts) for parts in groups], axis=1)
    if joined:
        combined = combined + full(joined)
    combined = combined.astype(jnp.bfloat16)

    top, bottom = combined[:, :edge], combined[:, block_side - edge :]
    even = band_here & 1 == 0
    inner = [(i, i + 1) for i in range(1, band_count - 1, 2)]
    beyond = lax.ppermute(jnp.where(even, top, bottom), "band", inner + [(i, j) for j, i in inner])
    paired = swap(jnp.where(even, bottom, top), 0)
    side = even.astype(jnp.int32)[None]
    partial = smooth(side, row_filter, combined, beyond)
    return detect(side, row_filter, col_filter, partial, paired)[None]


def solution(mesh):
    return jax.shard_map(
        local,
        mesh=mesh,
        in_specs=(
            P(None, ("sky", "band")),
            P(("sky", "band"), None),
            P(("sky", "band")),
            P(("sky", "band")),
            P(("sky", "band")),
            P(("sky", "band"), None),
            P(),
            P(),
            P(),
            P(),
        ),
        out_specs=P("sky", "band", None),
        check_vma=False,
    )
```

```python
import functools

import jax
import jax.numpy as jnp
from jax import lax
from jax.experimental import pallas as pl
from jax.experimental.pallas import tpu as pltpu
from jax.sharding import PartitionSpec as P

BANDS = 6
CR = 4
CC = 4
CELLS = 16
VMEM = pltpu.VMEM
SMEM = pltpu.SMEM


def up(value, unit):
    return -(-value // unit) * unit


def banded(row, rows, width):
    tile = pltpu.roll(jnp.broadcast_to(row, (8, width)), 0, 1, stride=1, stride_axis=0)
    return jnp.concatenate([tile if i == 0 else pltpu.roll(tile, 8 * i, 1) for i in range(rows // 8)], axis=0)


def lanes_at(row, start, width):
    parts = [row, jnp.zeros((1, width - start - row.shape[1]), row.dtype)]
    if start:
        parts.insert(0, jnp.zeros((1, start), row.dtype))
    return jnp.concatenate(parts, axis=1)


def load_kernel(*refs):
    sources, (facts_ref, coef_ref, rowk_ref, colk_ref, raw_ref) = refs[:8], refs[8:13]
    patch_ref, cell_ref, band_ref, weight_ref, row_ref, col_ref, coef_in = targets = refs[13:20]
    sems = refs[20]
    copies = [
        pltpu.make_async_copy(source, target, sems.at[i])
        for i, (source, target) in enumerate(zip(sources, targets + (raw_ref,)))
    ]
    for copy in copies:
        copy.start()
    for copy in copies[:-1]:
        copy.wait()
    key = (patch_ref[...] * BANDS + band_ref[...]) * CELLS + cell_ref[...]
    facts_ref[0, 0:1, :] = key.astype(jnp.float32)
    facts_ref[0, 1:2, :] = weight_ref[...].astype(jnp.float32).reshape(1, -1)
    coef_ref[...] = coef_in[...].astype(jnp.float32)
    basis_count, margin_side = row_ref.shape[0], raw_ref.shape[0]
    block_side = rowk_ref.shape[0] // basis_count
    width = colk_ref.shape[0] // basis_count
    for k in range(basis_count):
        rows = banded(lanes_at(row_ref[k : k + 1, :], 0, width), block_side, width)
        rowk_ref[k * block_side : (k + 1) * block_side, :] = rows[:, :margin_side].astype(jnp.bfloat16)
        cols = banded(lanes_at(col_ref[k : k + 1, :], 0, width), block_side, width)
        colk_ref[k * width : (k + 1) * width, :] = cols.T.astype(jnp.bfloat16)
    copies[-1].wait()


def load(patch, cell, band, weight, row_basis, col_basis, coef, raw, block_side):
    basis_count = row_basis.shape[0]
    margin_side = raw.shape[0]
    width = up(margin_side, 128)
    operands = (patch, cell, band, weight, row_basis, col_basis, coef, raw)
    out_shape = [
        jax.ShapeDtypeStruct((1, 2, patch.shape[1]), jnp.float32),
        jax.ShapeDtypeStruct(coef.shape, jnp.float32),
        jax.ShapeDtypeStruct((basis_count * block_side, margin_side), jnp.bfloat16),
        jax.ShapeDtypeStruct((basis_count * width, block_side), jnp.bfloat16),
        jax.ShapeDtypeStruct(raw.shape, raw.dtype),
    ]
    return pl.pallas_call(
        load_kernel,
        out_shape=out_shape,
        in_specs=[pl.BlockSpec(memory_space=pltpu.HBM)] * len(operands),
        out_specs=[pl.BlockSpec(memory_space=VMEM)] * len(out_shape),
        scratch_shapes=[VMEM(value.shape, value.dtype) for value in operands[:-1]]
        + [pltpu.SemaphoreType.DMA((len(operands),))],
        compiler_params=pltpu.CompilerParams(vmem_limit_bytes=12 << 20),
        cost_estimate=pl.CostEstimate(flops=1 << 20, bytes_accessed=4 << 20, transcendentals=0),
        name="load",
    )(*(pltpu.with_memory_space_constraint(value, pltpu.HBM) for value in operands))


def match_kernel(first, count, skip, fresh, after_ref, coef_ref, rowk_ref, colk_ref, raw_ref, *outs):
    margin_side = raw_ref.shape[0]
    basis_count = coef_ref.shape[0]
    outs = outs if fresh else outs[len(outs) // 2 :]
    block_side = outs[0].shape[2]
    width = colk_ref.shape[0] // basis_count
    for n in range(count):
        here = first + n
        block = raw_ref[:, here * margin_side : (here + 1) * margin_side]
        sectioned = jnp.dot(rowk_ref[...], block, preferred_element_type=jnp.float32)
        total = None
        for k in range(basis_count):
            part = sectioned[k * block_side : (k + 1) * block_side] * coef_ref[k : k + 1, here : here + 1]
            term = jnp.dot(
                part.astype(jnp.bfloat16),
                colk_ref[k * width : k * width + margin_side, :],
                preferred_element_type=jnp.float32,
            )
            total = term if total is None else total + term
        total = total.astype(jnp.bfloat16)
        start = 0
        for out_ref in outs:
            out_ref[skip + n] = total[start : start + out_ref.shape[1]]
            start += out_ref.shape[1]


def match_blocks(first, count, size, loaded, rows, block_side, after, into=()):
    raw = loaded[-1]
    basis_count = loaded[0].shape[0]
    skip = size - count if into else 0
    flops = 2 * count * basis_count * block_side * raw.shape[0] * (raw.shape[0] + block_side)
    return pl.pallas_call(
        functools.partial(match_kernel, first, count, skip, not into),
        out_shape=[jax.ShapeDtypeStruct((size, height, block_side), jnp.bfloat16) for height in rows],
        in_specs=[pl.BlockSpec(memory_space=pl.ANY)] + [pl.BlockSpec(memory_space=VMEM)] * (len(loaded) + len(into)),
        out_specs=[pl.BlockSpec(memory_space=VMEM)] * len(rows),
        input_output_aliases={1 + len(loaded) + i: i for i in range(len(into))},
        compiler_params=pltpu.CompilerParams(vmem_limit_bytes=8 << 20),
        cost_estimate=pl.CostEstimate(flops=4 * flops, bytes_accessed=2 << 20, transcendentals=0),
        name="match_blocks",
    )(after, *loaded, *into)


def bin_kernel(stepped, sources, bins_ref, scale_ref, after_ref, *rest):
    blocks_refs, outs, acc_ref = rest[:sources], rest[sources:-1], rest[-1]
    parts = sources // 2
    step = acc_ref.shape[0]
    acc_ref[...] = jnp.zeros_like(acc_ref)
    for index, blocks_ref in enumerate(blocks_refs):
        line, part = index // parts, index % parts
        start = sum(ref.shape[0] for ref in blocks_refs[:part])
        for n in range(blocks_ref.shape[0]):
            slot = bins_ref[line, start + n]
            if stepped:
                slot = slot - pl.program_id(0) * step

            @pl.when((slot >= 0) & (slot < step) if stepped else slot >= 0)
            def _(blocks_ref=blocks_ref, n=n, slot=slot, line=line, place=start + n):
                acc_ref[slot] += scale_ref[line, place] * blocks_ref[n].astype(jnp.float32)

    low = 0
    for out_ref in outs:
        out_ref[...] = acc_ref[low : low + out_ref.shape[0]].astype(out_ref.dtype)
        low += out_ref.shape[0]


def bin_blocks(bins, scale, blocks, sizes, name, after):
    shape = blocks[0].shape[1:]
    size = sum(sizes)
    stepped = size > 64
    step = sizes[-1] if stepped else size
    while step > 64:
        step //= 2
    moved = 2 * sum(part.size for part in blocks) + 2 * size * shape[0] * shape[1]
    given = (size,) if stepped else sizes
    if stepped:
        grid = (size // step,)
        block_specs = [pl.BlockSpec(part.shape, lambda g: (0, 0, 0)) for part in blocks]
        out_specs = [pl.BlockSpec((step,) + shape, lambda g: (g, 0, 0))]
    else:
        grid = ()
        block_specs = [pl.BlockSpec(memory_space=VMEM)] * len(blocks)
        out_specs = [pl.BlockSpec(memory_space=VMEM)] * len(given)
    found = pl.pallas_call(
        functools.partial(bin_kernel, stepped, len(blocks)),
        grid=grid,
        out_shape=[jax.ShapeDtypeStruct((count,) + shape, jnp.bfloat16) for count in given],
        in_specs=[pl.BlockSpec(memory_space=SMEM), pl.BlockSpec(memory_space=SMEM), pl.BlockSpec(memory_space=pl.ANY)]
        + block_specs,
        out_specs=out_specs,
        scratch_shapes=[VMEM((step,) + shape, jnp.float32)],
        compiler_params=pltpu.CompilerParams(vmem_limit_bytes=20 << 20),
        cost_estimate=pl.CostEstimate(flops=2 * moved, bytes_accessed=moved, transcendentals=0),
        name=name,
    )(bins, scale, after, *blocks)
    if stepped:
        starts = [sum(sizes[:i]) for i in range(len(sizes))]
        found = [found[0][low : low + count] for low, count in zip(starts, sizes)]
    return found


def filters_kernel(edge, taps_ref, rows_ref, cols_ref):
    side, rows_in = rows_ref.shape
    radius = (taps_ref.shape[1] - 1) // 2
    taps = taps_ref[...]
    width = up(rows_in + 1, 128)
    rows_ref[...] = banded(lanes_at(taps, edge - radius, width), side, width)[:, :rows_in].astype(jnp.bfloat16)
    cols_ref[...] = banded(lanes_at(taps, side - radius, 3 * side), side, 3 * side).T.astype(jnp.bfloat16)


def filters(taps, side, edge):
    return pl.pallas_call(
        functools.partial(filters_kernel, edge),
        out_shape=[
            jax.ShapeDtypeStruct((side, side + 2 * edge), jnp.bfloat16),
            jax.ShapeDtypeStruct((3 * side, side), jnp.bfloat16),
        ],
        in_specs=[pl.BlockSpec(memory_space=VMEM)],
        out_specs=[pl.BlockSpec(memory_space=VMEM)] * 2,
        compiler_params=pltpu.CompilerParams(vmem_limit_bytes=12 << 20),
        cost_estimate=pl.CostEstimate(flops=1 << 20, bytes_accessed=1 << 20, transcendentals=0),
        name="filters",
    )(taps)


def smooth_kernel(even_ref, row_filter_ref, mid_ref, beyond_ref, out_ref):
    cells, side, unused = mid_ref.shape
    edge = beyond_ref.shape[1]
    above, below = row_filter_ref[:, :edge], row_filter_ref[:, edge + side :]
    outer = jnp.where(even_ref[0] != 0, above.astype(jnp.float32), below.astype(jnp.float32)).astype(jnp.bfloat16)
    for c in range(cells):
        out_ref[c] = jnp.dot(
            row_filter_ref[:, edge : edge + side], mid_ref[c], preferred_element_type=jnp.float32
        ) + jnp.dot(outer, beyond_ref[c], preferred_element_type=jnp.float32)


def smooth(even, row_filter, mid, beyond):
    return pl.pallas_call(
        smooth_kernel,
        out_shape=jax.ShapeDtypeStruct(mid.shape, jnp.float32),
        in_specs=[pl.BlockSpec(memory_space=SMEM)] + [pl.BlockSpec(memory_space=VMEM)] * 3,
        out_specs=pl.BlockSpec(memory_space=VMEM),
        compiler_params=pltpu.CompilerParams(vmem_limit_bytes=12 << 20),
        cost_estimate=pl.CostEstimate(flops=1 << 26, bytes_accessed=1 << 20, transcendentals=0),
        name="smooth",
    )(even, row_filter, mid, beyond)


def detect_kernel(even_ref, row_filter_ref, col_filter_ref, partial_ref, paired_ref, out_ref):
    cells, side, unused = partial_ref.shape
    edge = paired_ref.shape[1]
    above, below = row_filter_ref[:, :edge], row_filter_ref[:, edge + side :]
    outer = jnp.where(even_ref[0] != 0, below.astype(jnp.float32), above.astype(jnp.float32)).astype(jnp.bfloat16)
    zero = jnp.zeros((side, side), jnp.bfloat16)
    smoothed = [zero]
    for c in range(cells):
        rows = partial_ref[c] + jnp.dot(outer, paired_ref[c], preferred_element_type=jnp.float32)
        smoothed.append(rows.astype(jnp.bfloat16))
    smoothed.append(zero)
    for c in range(cells):
        window = jnp.concatenate(smoothed[c : c + 3], axis=1)
        out_ref[:, c * side : (c + 1) * side] = jnp.dot(
            window, col_filter_ref[...], preferred_element_type=jnp.float32
        )


def detect(even, row_filter, col_filter, partial, paired):
    cells, side, unused = partial.shape
    return pl.pallas_call(
        detect_kernel,
        out_shape=jax.ShapeDtypeStruct((side, cells * side), jnp.float32),
        in_specs=[pl.BlockSpec(memory_space=SMEM)] + [pl.BlockSpec(memory_space=VMEM)] * 4,
        out_specs=pl.BlockSpec(memory_space=VMEM),
        compiler_params=pltpu.CompilerParams(vmem_limit_bytes=12 << 20),
        name="detect",
    )(even, row_filter, col_filter, partial, paired)


def halves(parts, send):
    total = None
    for part in parts:
        half = part.shape[0] // 2
        piece = (part[half:] if send else part[:half]).astype(jnp.float32)
        total = piece if total is None else total + piece
    return total


def first_halves(parts):
    return [part[: part.shape[0] // 2] for part in parts]


def local(
    raw_blocks,
    patch_of_block,
    cell_of_block,
    band_of_block,
    block_weight,
    basis_coef,
    row_basis,
    col_basis,
    band_gain,
    filter_taps,
):
    sky_count = lax.axis_size("sky")
    band_count = lax.axis_size("band")
    sky_bits = sky_count.bit_length() - 1
    band_bits = band_count.bit_length() - 1
    margin_side = raw_blocks.shape[0]
    block_count = raw_blocks.shape[1] // margin_side
    radius = (filter_taps.shape[0] - 1) // 2
    block_side = margin_side - 2 * radius
    sky_here = lax.axis_index("sky")
    band_here = lax.axis_index("band")

    def swap(array, bit):
        axis, count, bit = ("band", band_count, bit) if bit < band_bits else ("sky", sky_count, bit - band_bits)
        return lax.ppermute(array, axis, [(i, i ^ (1 << bit)) for i in range(count)])

    band_bit, sky_bit, next_bit = 1, band_bits, band_bits + 1
    orders = [[band_bit, next_bit, sky_bit], [sky_bit, band_bit, next_bit]]
    later = list(range(2, band_bits)) + list(range(band_bits + 2, band_bits + sky_bits))
    heights = [block_side // len(orders)] * len(orders)

    own_facts, *loaded = load(
        patch_of_block.reshape(1, -1),
        cell_of_block.reshape(1, -1),
        band_of_block.reshape(1, -1),
        block_weight,
        row_basis,
        col_basis,
        basis_coef.T,
        raw_blocks,
        block_side,
    )
    facts = jnp.concatenate(
        [own_facts]
        + [lax.ppermute(own_facts, "band", [(i, i ^ off) for i in range(band_count)]) for off in range(1, band_count)]
    )
    cut, early = block_count * 5 // 8, block_count * 3 // 8
    own, others = [[], []], [[], []]
    begun = match_blocks(0, early, cut, loaded, heights, block_side, own_facts)
    for part in range(max(2, sky_bits)):
        got = swap(facts, band_bits + part) if part < sky_bits else None
        if part == 0:
            found = match_blocks(early, cut - early, cut, loaded, heights, block_side, facts, begun)
        elif part == 1:
            found = match_blocks(cut, block_count - cut, block_count - cut, loaded, heights, block_side, facts)
        if part < 2:
            for group, order in enumerate(orders):
                own[group].append(found[group])
                others[group].append(swap(found[group], order[0]))
        if got is not None:
            facts = jnp.concatenate([facts, got])

    near = jnp.stack([facts[0]] + [facts[1 << order[0]] for order in orders])
    near_key, near_weight = near[:, 0], near[:, 1]
    same = near_key[:, :, None, None] == facts[None, None, :, 0]
    weight_sum = jnp.sum(jnp.where(same, facts[None, None, :, 1], 0.0), axis=(2, 3))
    near_key = near_key.astype(jnp.int32)
    cell = near_key % CELLS
    band = near_key // CELLS % BANDS
    gain = jnp.sum(jnp.where(band[..., None] == jnp.arange(BANDS), band_gain, 0.0), axis=2)
    scale = gain * near_weight / jnp.maximum(weight_sum, 1.0)

    owner_off = (near_key // (CELLS * BANDS) ^ sky_here) << band_bits | (cell // CC ^ band_here)
    size = (1 << (len(orders[0]) + len(later) - 1)) * CC
    half = size // 2
    blocks, bins, scales = [], [], []
    for group, order in enumerate(orders):
        blocks.append(own[group] + others[group])
        scales.append(jnp.stack([scale[0], scale[group + 1]]))
        off = jnp.stack([owner_off[0], owner_off[group + 1]])
        place = jnp.zeros_like(off)
        for bit in [0] + order[1:] + later:
            place = place * 2 + (off >> bit & 1)
        place = place * CC + jnp.stack([cell[0], cell[group + 1]]) % CC
        place = jnp.where(off >> order[0] & 1 == 0, place, -1)
        leaving = jnp.where(place >= size, place - size, jnp.where(place >= half, place - half + size, -1))
        bins.append([leaving, jnp.where(place < half, place, -1)])
    from_pair, sent = [], []
    for group, (lines, factor, parts) in enumerate(zip(bins, scales, blocks)):
        for_pair, for_next = bin_blocks(lines[0], factor, parts, (size, half), "bins_sent", others[1 - group][-1])
        from_pair.append(swap(for_pair, 0))
        sent.append(for_next)
    edge = up(radius, 16)
    taps = filter_taps.astype(jnp.bfloat16).astype(jnp.float32)[None]
    row_filter, col_filter = filters(taps, block_side, edge)
    groups = []
    for lines, factor, parts, order, mine, going in zip(bins, scales, blocks, orders, from_pair, sent):
        back = swap((going.astype(jnp.float32) + mine[half:].astype(jnp.float32)).astype(jnp.bfloat16), order[1])
        (kept,) = bin_blocks(lines[1], factor, parts, (half,), "bins_kept", row_filter)
        groups.append([kept, mine[:half], back])
    got = [swap(halves(parts, True).astype(jnp.bfloat16), order[2]) for parts, order in zip(groups, orders)]
    groups = [first_halves(parts) + [part] for parts, part in zip(groups, got)]
    joined = []
    for bit in later:
        outgoing = jnp.concatenate([halves(parts, True) for parts in groups], axis=1)
        for part in joined:
            outgoing = outgoing + part[part.shape[0] // 2 :].astype(jnp.float32)
        got = swap(outgoing.astype(jnp.bfloat16), bit)
        groups = [first_halves(parts) for parts in groups]
        joined = first_halves(joined) + [got]

    def full(parts):
        return functools.reduce(jnp.add, [part.astype(jnp.float32) for part in parts])

    combined = jnp.concatenate([full(parts) for parts in groups], axis=1)
    if joined:
        combined = combined + full(joined)
    combined = combined.astype(jnp.bfloat16)

    top, bottom = combined[:, :edge], combined[:, block_side - edge :]
    even = band_here & 1 == 0
    inner = [(i, i + 1) for i in range(1, band_count - 1, 2)]
    beyond = lax.ppermute(jnp.where(even, top, bottom), "band", inner + [(i, j) for j, i in inner])
    paired = swap(jnp.where(even, bottom, top), 0)
    side = even.astype(jnp.int32)[None]
    partial = smooth(side, row_filter, combined, beyond)
    return detect(side, row_filter, col_filter, partial, paired)[None]


def solution(mesh):
    return jax.shard_map(
        local,
        mesh=mesh,
        in_specs=(
            P(None, ("sky", "band")),
            P(("sky", "band"), None),
            P(("sky", "band")),
            P(("sky", "band")),
            P(("sky", "band")),
            P(("sky", "band"), None),
            P(),
            P(),
            P(),
            P(),
        ),
        out_specs=P("sky", "band", None),
        check_vma=False,
    )
```

```python
import functools

import jax
import jax.numpy as jnp
from jax import lax
from jax.experimental import pallas as pl
from jax.experimental.pallas import tpu as pltpu
from jax.sharding import PartitionSpec as P

BANDS = 6
CR = 4
CC = 4
CELLS = 16
VMEM = pltpu.VMEM
SMEM = pltpu.SMEM


def up(value, unit):
    return -(-value // unit) * unit


def banded(row, rows, width):
    tile = pltpu.roll(jnp.broadcast_to(row, (8, width)), 0, 1, stride=1, stride_axis=0)
    return jnp.concatenate([tile if i == 0 else pltpu.roll(tile, 8 * i, 1) for i in range(rows // 8)], axis=0)


def lanes_at(row, start, width):
    parts = [row, jnp.zeros((1, width - start - row.shape[1]), row.dtype)]
    if start:
        parts.insert(0, jnp.zeros((1, start), row.dtype))
    return jnp.concatenate(parts, axis=1)


def load_kernel(*refs):
    sources, (facts_ref, coef_ref, rowk_ref, colk_ref, raw_ref) = refs[:8], refs[8:13]
    patch_ref, cell_ref, band_ref, weight_ref, row_ref, col_ref, coef_in = targets = refs[13:20]
    sems = refs[20]
    copies = [
        pltpu.make_async_copy(source, target, sems.at[i])
        for i, (source, target) in enumerate(zip(sources, targets + (raw_ref,)))
    ]
    for copy in copies:
        copy.start()
    for copy in copies[:-1]:
        copy.wait()
    key = (patch_ref[...] * BANDS + band_ref[...]) * CELLS + cell_ref[...]
    facts_ref[0, 0:1, :] = key.astype(jnp.float32)
    facts_ref[0, 1:2, :] = weight_ref[...].astype(jnp.float32).reshape(1, -1)
    coef_ref[...] = coef_in[...].astype(jnp.float32)
    basis_count, margin_side = row_ref.shape[0], raw_ref.shape[0]
    block_side = rowk_ref.shape[0] // basis_count
    width = colk_ref.shape[0] // basis_count
    for k in range(basis_count):
        rows = banded(lanes_at(row_ref[k : k + 1, :], 0, width), block_side, width)
        rowk_ref[k * block_side : (k + 1) * block_side, :] = rows[:, :margin_side].astype(jnp.bfloat16)
        cols = banded(lanes_at(col_ref[k : k + 1, :], 0, width), block_side, width)
        colk_ref[k * width : (k + 1) * width, :] = cols.T.astype(jnp.bfloat16)
    copies[-1].wait()


def load(patch, cell, band, weight, row_basis, col_basis, coef, raw, block_side):
    basis_count = row_basis.shape[0]
    margin_side = raw.shape[0]
    width = up(margin_side, 128)
    operands = (patch, cell, band, weight, row_basis, col_basis, coef, raw)
    out_shape = [
        jax.ShapeDtypeStruct((1, 2, patch.shape[1]), jnp.float32),
        jax.ShapeDtypeStruct(coef.shape, jnp.float32),
        jax.ShapeDtypeStruct((basis_count * block_side, margin_side), jnp.bfloat16),
        jax.ShapeDtypeStruct((basis_count * width, block_side), jnp.bfloat16),
        jax.ShapeDtypeStruct(raw.shape, raw.dtype),
    ]
    return pl.pallas_call(
        load_kernel,
        out_shape=out_shape,
        in_specs=[pl.BlockSpec(memory_space=pltpu.HBM)] * len(operands),
        out_specs=[pl.BlockSpec(memory_space=VMEM)] * len(out_shape),
        scratch_shapes=[VMEM(value.shape, value.dtype) for value in operands[:-1]]
        + [pltpu.SemaphoreType.DMA((len(operands),))],
        compiler_params=pltpu.CompilerParams(vmem_limit_bytes=12 << 20),
        cost_estimate=pl.CostEstimate(flops=1 << 20, bytes_accessed=4 << 20, transcendentals=0),
        name="load",
    )(*(pltpu.with_memory_space_constraint(value, pltpu.HBM) for value in operands))


def match_kernel(first, count, skip, fresh, after_ref, coef_ref, rowk_ref, colk_ref, raw_ref, *outs):
    margin_side = raw_ref.shape[0]
    basis_count = coef_ref.shape[0]
    outs = outs if fresh else outs[len(outs) // 2 :]
    block_side = outs[0].shape[2]
    width = colk_ref.shape[0] // basis_count
    for n in range(count):
        here = first + n
        block = raw_ref[:, here * margin_side : (here + 1) * margin_side]
        sectioned = jnp.dot(rowk_ref[...], block, preferred_element_type=jnp.float32)
        total = None
        for k in range(basis_count):
            part = sectioned[k * block_side : (k + 1) * block_side] * coef_ref[k : k + 1, here : here + 1]
            term = jnp.dot(
                part.astype(jnp.bfloat16),
                colk_ref[k * width : k * width + margin_side, :],
                preferred_element_type=jnp.float32,
            )
            total = term if total is None else total + term
        total = total.astype(jnp.bfloat16)
        start = 0
        for out_ref in outs:
            out_ref[skip + n] = total[start : start + out_ref.shape[1]]
            start += out_ref.shape[1]


def match_blocks(first, count, size, loaded, rows, block_side, after, into=()):
    raw = loaded[-1]
    basis_count = loaded[0].shape[0]
    skip = size - count if into else 0
    flops = 2 * count * basis_count * block_side * raw.shape[0] * (raw.shape[0] + block_side)
    return pl.pallas_call(
        functools.partial(match_kernel, first, count, skip, not into),
        out_shape=[jax.ShapeDtypeStruct((size, height, block_side), jnp.bfloat16) for height in rows],
        in_specs=[pl.BlockSpec(memory_space=pl.ANY)] + [pl.BlockSpec(memory_space=VMEM)] * (len(loaded) + len(into)),
        out_specs=[pl.BlockSpec(memory_space=VMEM)] * len(rows),
        input_output_aliases={1 + len(loaded) + i: i for i in range(len(into))},
        compiler_params=pltpu.CompilerParams(vmem_limit_bytes=8 << 20),
        cost_estimate=pl.CostEstimate(flops=4 * flops, bytes_accessed=2 << 20, transcendentals=0),
        name="match_blocks",
    )(after, *loaded, *into)


def bin_kernel(stepped, sources, bins_ref, scale_ref, after_ref, *rest):
    blocks_refs, outs, acc_ref = rest[:sources], rest[sources:-1], rest[-1]
    parts = sources // 2
    step = acc_ref.shape[0]
    acc_ref[...] = jnp.zeros_like(acc_ref)
    for index, blocks_ref in enumerate(blocks_refs):
        line, part = index // parts, index % parts
        start = sum(ref.shape[0] for ref in blocks_refs[:part])
        for n in range(blocks_ref.shape[0]):
            slot = bins_ref[line, start + n]
            if stepped:
                slot = slot - pl.program_id(0) * step

            @pl.when((slot >= 0) & (slot < step) if stepped else slot >= 0)
            def _(blocks_ref=blocks_ref, n=n, slot=slot, line=line, place=start + n):
                acc_ref[slot] += scale_ref[line, place] * blocks_ref[n].astype(jnp.float32)

    low = 0
    for out_ref in outs:
        out_ref[...] = acc_ref[low : low + out_ref.shape[0]].astype(out_ref.dtype)
        low += out_ref.shape[0]


def bin_blocks(bins, scale, blocks, sizes, name, after):
    shape = blocks[0].shape[1:]
    size = sum(sizes)
    stepped = size > 64
    step = sizes[-1] if stepped else size
    while step > 64:
        step //= 2
    moved = 2 * sum(part.size for part in blocks) + 2 * size * shape[0] * shape[1]
    given = (size,) if stepped else sizes
    if stepped:
        grid = (size // step,)
        block_specs = [pl.BlockSpec(part.shape, lambda g: (0, 0, 0)) for part in blocks]
        out_specs = [pl.BlockSpec((step,) + shape, lambda g: (g, 0, 0))]
    else:
        grid = ()
        block_specs = [pl.BlockSpec(memory_space=VMEM)] * len(blocks)
        out_specs = [pl.BlockSpec(memory_space=VMEM)] * len(given)
    found = pl.pallas_call(
        functools.partial(bin_kernel, stepped, len(blocks)),
        grid=grid,
        out_shape=[jax.ShapeDtypeStruct((count,) + shape, jnp.bfloat16) for count in given],
        in_specs=[pl.BlockSpec(memory_space=SMEM), pl.BlockSpec(memory_space=SMEM), pl.BlockSpec(memory_space=pl.ANY)]
        + block_specs,
        out_specs=out_specs,
        scratch_shapes=[VMEM((step,) + shape, jnp.float32)],
        compiler_params=pltpu.CompilerParams(vmem_limit_bytes=20 << 20),
        cost_estimate=pl.CostEstimate(flops=2 * moved, bytes_accessed=moved, transcendentals=0),
        name=name,
    )(bins, scale, after, *blocks)
    if stepped:
        starts = [sum(sizes[:i]) for i in range(len(sizes))]
        found = [found[0][low : low + count] for low, count in zip(starts, sizes)]
    return found


def filters_kernel(edge, taps_ref, rows_ref, cols_ref):
    side, rows_in = rows_ref.shape
    radius = (taps_ref.shape[1] - 1) // 2
    taps = taps_ref[...]
    width = up(rows_in + 1, 128)
    rows_ref[...] = banded(lanes_at(taps, edge - radius, width), side, width)[:, :rows_in].astype(jnp.bfloat16)
    cols_ref[...] = banded(lanes_at(taps, side - radius, 3 * side), side, 3 * side).T.astype(jnp.bfloat16)


def filters(taps, side, edge):
    return pl.pallas_call(
        functools.partial(filters_kernel, edge),
        out_shape=[
            jax.ShapeDtypeStruct((side, side + 2 * edge), jnp.bfloat16),
            jax.ShapeDtypeStruct((3 * side, side), jnp.bfloat16),
        ],
        in_specs=[pl.BlockSpec(memory_space=VMEM)],
        out_specs=[pl.BlockSpec(memory_space=VMEM)] * 2,
        compiler_params=pltpu.CompilerParams(vmem_limit_bytes=12 << 20),
        cost_estimate=pl.CostEstimate(flops=1 << 20, bytes_accessed=1 << 20, transcendentals=0),
        name="filters",
    )(taps)


def smooth_kernel(even_ref, row_filter_ref, mid_ref, beyond_ref, out_ref):
    cells, side, unused = mid_ref.shape
    edge = beyond_ref.shape[1]
    above, below = row_filter_ref[:, :edge], row_filter_ref[:, edge + side :]
    outer = jnp.where(even_ref[0] != 0, above.astype(jnp.float32), below.astype(jnp.float32)).astype(jnp.bfloat16)
    for c in range(cells):
        out_ref[c] = jnp.dot(
            row_filter_ref[:, edge : edge + side], mid_ref[c], preferred_element_type=jnp.float32
        ) + jnp.dot(outer, beyond_ref[c], preferred_element_type=jnp.float32)


def smooth(even, row_filter, mid, beyond):
    return pl.pallas_call(
        smooth_kernel,
        out_shape=jax.ShapeDtypeStruct(mid.shape, jnp.float32),
        in_specs=[pl.BlockSpec(memory_space=SMEM)] + [pl.BlockSpec(memory_space=VMEM)] * 3,
        out_specs=pl.BlockSpec(memory_space=VMEM),
        compiler_params=pltpu.CompilerParams(vmem_limit_bytes=12 << 20),
        cost_estimate=pl.CostEstimate(flops=1 << 26, bytes_accessed=1 << 20, transcendentals=0),
        name="smooth",
    )(even, row_filter, mid, beyond)


def detect_kernel(even_ref, row_filter_ref, col_filter_ref, partial_ref, paired_ref, out_ref):
    cells, side, unused = partial_ref.shape
    edge = paired_ref.shape[1]
    above, below = row_filter_ref[:, :edge], row_filter_ref[:, edge + side :]
    outer = jnp.where(even_ref[0] != 0, below.astype(jnp.float32), above.astype(jnp.float32)).astype(jnp.bfloat16)
    zero = jnp.zeros((side, side), jnp.bfloat16)
    smoothed = [zero]
    for c in range(cells):
        rows = partial_ref[c] + jnp.dot(outer, paired_ref[c], preferred_element_type=jnp.float32)
        smoothed.append(rows.astype(jnp.bfloat16))
    smoothed.append(zero)
    for c in range(cells):
        window = jnp.concatenate(smoothed[c : c + 3], axis=1)
        out_ref[:, c * side : (c + 1) * side] = jnp.dot(
            window, col_filter_ref[...], preferred_element_type=jnp.float32
        )


def detect(even, row_filter, col_filter, partial, paired):
    cells, side, unused = partial.shape
    return pl.pallas_call(
        detect_kernel,
        out_shape=jax.ShapeDtypeStruct((side, cells * side), jnp.float32),
        in_specs=[pl.BlockSpec(memory_space=SMEM)] + [pl.BlockSpec(memory_space=VMEM)] * 4,
        out_specs=pl.BlockSpec(memory_space=VMEM),
        compiler_params=pltpu.CompilerParams(vmem_limit_bytes=12 << 20),
        name="detect",
    )(even, row_filter, col_filter, partial, paired)


def halves(parts, send):
    total = None
    for part in parts:
        half = part.shape[0] // 2
        piece = (part[half:] if send else part[:half]).astype(jnp.float32)
        total = piece if total is None else total + piece
    return total


def first_halves(parts):
    return [part[: part.shape[0] // 2] for part in parts]


def local(
    raw_blocks,
    patch_of_block,
    cell_of_block,
    band_of_block,
    block_weight,
    basis_coef,
    row_basis,
    col_basis,
    band_gain,
    filter_taps,
):
    sky_count = lax.axis_size("sky")
    band_count = lax.axis_size("band")
    sky_bits = sky_count.bit_length() - 1
    band_bits = band_count.bit_length() - 1
    margin_side = raw_blocks.shape[0]
    block_count = raw_blocks.shape[1] // margin_side
    radius = (filter_taps.shape[0] - 1) // 2
    block_side = margin_side - 2 * radius
    sky_here = lax.axis_index("sky")
    band_here = lax.axis_index("band")

    def swap(array, bit):
        axis, count, bit = ("band", band_count, bit) if bit < band_bits else ("sky", sky_count, bit - band_bits)
        return lax.ppermute(array, axis, [(i, i ^ (1 << bit)) for i in range(count)])

    band_bit, sky_bit, next_bit = 1, band_bits, band_bits + 1
    orders = [[band_bit, next_bit, sky_bit], [sky_bit, band_bit, next_bit]]
    later = list(range(2, band_bits)) + list(range(band_bits + 2, band_bits + sky_bits))
    heights = [block_side // len(orders)] * len(orders)

    own_facts, *loaded = load(
        patch_of_block.reshape(1, -1),
        cell_of_block.reshape(1, -1),
        band_of_block.reshape(1, -1),
        block_weight,
        row_basis,
        col_basis,
        basis_coef.T,
        raw_blocks,
        block_side,
    )
    facts = jnp.concatenate(
        [own_facts]
        + [lax.ppermute(own_facts, "band", [(i, i ^ off) for i in range(band_count)]) for off in range(1, band_count)]
    )
    cut, early = block_count // 2, block_count * 5 // 16
    own, others = [[], []], [[], []]
    begun = match_blocks(0, early, cut, loaded, heights, block_side, own_facts)
    for part in range(max(2, sky_bits)):
        got = swap(facts, band_bits + part) if part < sky_bits else None
        if part == 0:
            found = match_blocks(early, cut - early, cut, loaded, heights, block_side, facts, begun)
        elif part == 1:
            found = match_blocks(cut, block_count - cut, block_count - cut, loaded, heights, block_side, facts)
        if part < 2:
            for group, order in enumerate(orders):
                own[group].append(found[group])
                others[group].append(swap(found[group], order[0]))
        if got is not None:
            facts = jnp.concatenate([facts, got])

    near = jnp.stack([facts[0]] + [facts[1 << order[0]] for order in orders])
    near_key, near_weight = near[:, 0], near[:, 1]
    same = near_key[:, :, None, None] == facts[None, None, :, 0]
    weight_sum = jnp.sum(jnp.where(same, facts[None, None, :, 1], 0.0), axis=(2, 3))
    near_key = near_key.astype(jnp.int32)
    cell = near_key % CELLS
    band = near_key // CELLS % BANDS
    gain = jnp.sum(jnp.where(band[..., None] == jnp.arange(BANDS), band_gain, 0.0), axis=2)
    scale = gain * near_weight / jnp.maximum(weight_sum, 1.0)

    owner_off = (near_key // (CELLS * BANDS) ^ sky_here) << band_bits | (cell // CC ^ band_here)
    size = (1 << (len(orders[0]) + len(later) - 1)) * CC
    half = size // 2
    blocks, bins, scales = [], [], []
    for group, order in enumerate(orders):
        blocks.append(own[group] + others[group])
        scales.append(jnp.stack([scale[0], scale[group + 1]]))
        off = jnp.stack([owner_off[0], owner_off[group + 1]])
        place = jnp.zeros_like(off)
        for bit in [0] + order[1:] + later:
            place = place * 2 + (off >> bit & 1)
        place = place * CC + jnp.stack([cell[0], cell[group + 1]]) % CC
        place = jnp.where(off >> order[0] & 1 == 0, place, -1)
        leaving = jnp.where(place >= size, place - size, jnp.where(place >= half, place - half + size, -1))
        bins.append([leaving, jnp.where(place < half, place, -1)])
    from_pair, sent = [], []
    for group, (lines, factor, parts) in enumerate(zip(bins, scales, blocks)):
        for_pair, for_next = bin_blocks(lines[0], factor, parts, (size, half), "bins_sent", others[1 - group][-1])
        from_pair.append(swap(for_pair, 0))
        sent.append(for_next)
    edge = up(radius, 16)
    taps = filter_taps.astype(jnp.bfloat16).astype(jnp.float32)[None]
    row_filter, col_filter = filters(taps, block_side, edge)
    groups = []
    for lines, factor, parts, order, mine, going in zip(bins, scales, blocks, orders, from_pair, sent):
        back = swap((going.astype(jnp.float32) + mine[half:].astype(jnp.float32)).astype(jnp.bfloat16), order[1])
        (kept,) = bin_blocks(lines[1], factor, parts, (half,), "bins_kept", row_filter)
        groups.append([kept, mine[:half], back])
    got = [swap(halves(parts, True).astype(jnp.bfloat16), order[2]) for parts, order in zip(groups, orders)]
    groups = [first_halves(parts) + [part] for parts, part in zip(groups, got)]
    joined = []
    for bit in later:
        outgoing = jnp.concatenate([halves(parts, True) for parts in groups], axis=1)
        for part in joined:
            outgoing = outgoing + part[part.shape[0] // 2 :].astype(jnp.float32)
        got = swap(outgoing.astype(jnp.bfloat16), bit)
        groups = [first_halves(parts) for parts in groups]
        joined = first_halves(joined) + [got]

    def full(parts):
        return functools.reduce(jnp.add, [part.astype(jnp.float32) for part in parts])

    combined = jnp.concatenate([full(parts) for parts in groups], axis=1)
    if joined:
        combined = combined + full(joined)
    combined = combined.astype(jnp.bfloat16)

    top, bottom = combined[:, :edge], combined[:, block_side - edge :]
    even = band_here & 1 == 0
    inner = [(i, i + 1) for i in range(1, band_count - 1, 2)]
    beyond = lax.ppermute(jnp.where(even, top, bottom), "band", inner + [(i, j) for j, i in inner])
    paired = swap(jnp.where(even, bottom, top), 0)
    side = even.astype(jnp.int32)[None]
    partial = smooth(side, row_filter, combined, beyond)
    return detect(side, row_filter, col_filter, partial, paired)[None]


def solution(mesh):
    return jax.shard_map(
        local,
        mesh=mesh,
        in_specs=(
            P(None, ("sky", "band")),
            P(("sky", "band"), None),
            P(("sky", "band")),
            P(("sky", "band")),
            P(("sky", "band")),
            P(("sky", "band"), None),
            P(),
            P(),
            P(),
            P(),
        ),
        out_specs=P("sky", "band", None),
        check_vma=False,
    )
```

```python
import functools

import jax
import jax.numpy as jnp
from jax import lax
from jax.experimental import pallas as pl
from jax.experimental.pallas import tpu as pltpu
from jax.sharding import PartitionSpec as P

BANDS = 6
CR = 4
CC = 4
CELLS = 16
VMEM = pltpu.VMEM
SMEM = pltpu.SMEM


def up(value, unit):
    return -(-value // unit) * unit


def banded(row, rows, width):
    tile = pltpu.roll(jnp.broadcast_to(row, (8, width)), 0, 1, stride=1, stride_axis=0)
    return jnp.concatenate([tile if i == 0 else pltpu.roll(tile, 8 * i, 1) for i in range(rows // 8)], axis=0)


def lanes_at(row, start, width):
    parts = [row, jnp.zeros((1, width - start - row.shape[1]), row.dtype)]
    if start:
        parts.insert(0, jnp.zeros((1, start), row.dtype))
    return jnp.concatenate(parts, axis=1)


def load_kernel(*refs):
    sources, (facts_ref, coef_ref, rowk_ref, colk_ref, raw_ref) = refs[:8], refs[8:13]
    patch_ref, cell_ref, band_ref, weight_ref, row_ref, col_ref, coef_in = targets = refs[13:20]
    sems = refs[20]
    copies = [
        pltpu.make_async_copy(source, target, sems.at[i])
        for i, (source, target) in enumerate(zip(sources, targets + (raw_ref,)))
    ]
    for copy in copies:
        copy.start()
    for copy in copies[:-1]:
        copy.wait()
    key = (patch_ref[...] * BANDS + band_ref[...]) * CELLS + cell_ref[...]
    facts_ref[0, 0:1, :] = key.astype(jnp.float32)
    facts_ref[0, 1:2, :] = weight_ref[...].astype(jnp.float32).reshape(1, -1)
    coef_ref[...] = coef_in[...].astype(jnp.float32)
    basis_count, margin_side = row_ref.shape[0], raw_ref.shape[0]
    block_side = rowk_ref.shape[0] // basis_count
    width = colk_ref.shape[0] // basis_count
    for k in range(basis_count):
        rows = banded(lanes_at(row_ref[k : k + 1, :], 0, width), block_side, width)
        rowk_ref[k * block_side : (k + 1) * block_side, :] = rows[:, :margin_side].astype(jnp.bfloat16)
        cols = banded(lanes_at(col_ref[k : k + 1, :], 0, width), block_side, width)
        colk_ref[k * width : (k + 1) * width, :] = cols.T.astype(jnp.bfloat16)
    copies[-1].wait()


def load(patch, cell, band, weight, row_basis, col_basis, coef, raw, block_side):
    basis_count = row_basis.shape[0]
    margin_side = raw.shape[0]
    width = up(margin_side, 128)
    operands = (patch, cell, band, weight, row_basis, col_basis, coef, raw)
    out_shape = [
        jax.ShapeDtypeStruct((1, 2, patch.shape[1]), jnp.float32),
        jax.ShapeDtypeStruct(coef.shape, jnp.float32),
        jax.ShapeDtypeStruct((basis_count * block_side, margin_side), jnp.bfloat16),
        jax.ShapeDtypeStruct((basis_count * width, block_side), jnp.bfloat16),
        jax.ShapeDtypeStruct(raw.shape, raw.dtype),
    ]
    return pl.pallas_call(
        load_kernel,
        out_shape=out_shape,
        in_specs=[pl.BlockSpec(memory_space=pltpu.HBM)] * len(operands),
        out_specs=[pl.BlockSpec(memory_space=VMEM)] * len(out_shape),
        scratch_shapes=[VMEM(value.shape, value.dtype) for value in operands[:-1]]
        + [pltpu.SemaphoreType.DMA((len(operands),))],
        compiler_params=pltpu.CompilerParams(vmem_limit_bytes=12 << 20),
        cost_estimate=pl.CostEstimate(flops=1 << 20, bytes_accessed=4 << 20, transcendentals=0),
        name="load",
    )(*(pltpu.with_memory_space_constraint(value, pltpu.HBM) for value in operands))


def match_kernel(first, count, skip, fresh, after_ref, coef_ref, rowk_ref, colk_ref, raw_ref, *outs):
    margin_side = raw_ref.shape[0]
    basis_count = coef_ref.shape[0]
    outs = outs if fresh else outs[len(outs) // 2 :]
    block_side = outs[0].shape[2]
    width = colk_ref.shape[0] // basis_count
    for n in range(count):
        here = first + n
        block = raw_ref[:, here * margin_side : (here + 1) * margin_side]
        sectioned = jnp.dot(rowk_ref[...], block, preferred_element_type=jnp.float32)
        total = None
        for k in range(basis_count):
            part = sectioned[k * block_side : (k + 1) * block_side] * coef_ref[k : k + 1, here : here + 1]
            term = jnp.dot(
                part.astype(jnp.bfloat16),
                colk_ref[k * width : k * width + margin_side, :],
                preferred_element_type=jnp.float32,
            )
            total = term if total is None else total + term
        total = total.astype(jnp.bfloat16)
        start = 0
        for out_ref in outs:
            out_ref[skip + n] = total[start : start + out_ref.shape[1]]
            start += out_ref.shape[1]


def match_blocks(first, count, size, loaded, rows, block_side, after, into=()):
    raw = loaded[-1]
    basis_count = loaded[0].shape[0]
    skip = size - count if into else 0
    flops = 2 * count * basis_count * block_side * raw.shape[0] * (raw.shape[0] + block_side)
    return pl.pallas_call(
        functools.partial(match_kernel, first, count, skip, not into),
        out_shape=[jax.ShapeDtypeStruct((size, height, block_side), jnp.bfloat16) for height in rows],
        in_specs=[pl.BlockSpec(memory_space=pl.ANY)] + [pl.BlockSpec(memory_space=VMEM)] * (len(loaded) + len(into)),
        out_specs=[pl.BlockSpec(memory_space=VMEM)] * len(rows),
        input_output_aliases={1 + len(loaded) + i: i for i in range(len(into))},
        compiler_params=pltpu.CompilerParams(vmem_limit_bytes=8 << 20),
        cost_estimate=pl.CostEstimate(flops=4 * flops, bytes_accessed=2 << 20, transcendentals=0),
        name="match_blocks",
    )(after, *loaded, *into)


def bin_kernel(stepped, sources, bins_ref, scale_ref, after_ref, *rest):
    blocks_refs, outs, acc_ref = rest[:sources], rest[sources:-1], rest[-1]
    parts = sources // 2
    step = acc_ref.shape[0]
    acc_ref[...] = jnp.zeros_like(acc_ref)
    for index, blocks_ref in enumerate(blocks_refs):
        line, part = index // parts, index % parts
        start = sum(ref.shape[0] for ref in blocks_refs[:part])
        for n in range(blocks_ref.shape[0]):
            slot = bins_ref[line, start + n]
            if stepped:
                slot = slot - pl.program_id(0) * step

            @pl.when((slot >= 0) & (slot < step) if stepped else slot >= 0)
            def _(blocks_ref=blocks_ref, n=n, slot=slot, line=line, place=start + n):
                acc_ref[slot] += scale_ref[line, place] * blocks_ref[n].astype(jnp.float32)

    low = 0
    for out_ref in outs:
        out_ref[...] = acc_ref[low : low + out_ref.shape[0]].astype(out_ref.dtype)
        low += out_ref.shape[0]


def bin_blocks(bins, scale, blocks, sizes, name, after):
    shape = blocks[0].shape[1:]
    size = sum(sizes)
    stepped = size > 64
    step = sizes[-1] if stepped else size
    while step > 64:
        step //= 2
    moved = 2 * sum(part.size for part in blocks) + 2 * size * shape[0] * shape[1]
    given = (size,) if stepped else sizes
    if stepped:
        grid = (size // step,)
        block_specs = [pl.BlockSpec(part.shape, lambda g: (0, 0, 0)) for part in blocks]
        out_specs = [pl.BlockSpec((step,) + shape, lambda g: (g, 0, 0))]
    else:
        grid = ()
        block_specs = [pl.BlockSpec(memory_space=VMEM)] * len(blocks)
        out_specs = [pl.BlockSpec(memory_space=VMEM)] * len(given)
    found = pl.pallas_call(
        functools.partial(bin_kernel, stepped, len(blocks)),
        grid=grid,
        out_shape=[jax.ShapeDtypeStruct((count,) + shape, jnp.bfloat16) for count in given],
        in_specs=[pl.BlockSpec(memory_space=SMEM), pl.BlockSpec(memory_space=SMEM), pl.BlockSpec(memory_space=pl.ANY)]
        + block_specs,
        out_specs=out_specs,
        scratch_shapes=[VMEM((step,) + shape, jnp.float32)],
        compiler_params=pltpu.CompilerParams(vmem_limit_bytes=20 << 20),
        cost_estimate=pl.CostEstimate(flops=2 * moved, bytes_accessed=moved, transcendentals=0),
        name=name,
    )(bins, scale, after, *blocks)
    if stepped:
        starts = [sum(sizes[:i]) for i in range(len(sizes))]
        found = [found[0][low : low + count] for low, count in zip(starts, sizes)]
    return found


def filters_kernel(edge, taps_ref, rows_ref, cols_ref):
    side, rows_in = rows_ref.shape
    radius = (taps_ref.shape[1] - 1) // 2
    taps = taps_ref[...]
    width = up(rows_in + 1, 128)
    rows_ref[...] = banded(lanes_at(taps, edge - radius, width), side, width)[:, :rows_in].astype(jnp.bfloat16)
    cols_ref[...] = banded(lanes_at(taps, side - radius, 3 * side), side, 3 * side).T.astype(jnp.bfloat16)


def filters(taps, side, edge):
    return pl.pallas_call(
        functools.partial(filters_kernel, edge),
        out_shape=[
            jax.ShapeDtypeStruct((side, side + 2 * edge), jnp.bfloat16),
            jax.ShapeDtypeStruct((3 * side, side), jnp.bfloat16),
        ],
        in_specs=[pl.BlockSpec(memory_space=VMEM)],
        out_specs=[pl.BlockSpec(memory_space=VMEM)] * 2,
        compiler_params=pltpu.CompilerParams(vmem_limit_bytes=12 << 20),
        cost_estimate=pl.CostEstimate(flops=1 << 20, bytes_accessed=1 << 20, transcendentals=0),
        name="filters",
    )(taps)


def smooth_kernel(even_ref, row_filter_ref, mid_ref, beyond_ref, out_ref):
    cells, side, unused = mid_ref.shape
    edge = beyond_ref.shape[1]
    above, below = row_filter_ref[:, :edge], row_filter_ref[:, edge + side :]
    outer = jnp.where(even_ref[0] != 0, above.astype(jnp.float32), below.astype(jnp.float32)).astype(jnp.bfloat16)
    for c in range(cells):
        out_ref[c] = jnp.dot(
            row_filter_ref[:, edge : edge + side], mid_ref[c], preferred_element_type=jnp.float32
        ) + jnp.dot(outer, beyond_ref[c], preferred_element_type=jnp.float32)


def smooth(even, row_filter, mid, beyond):
    return pl.pallas_call(
        smooth_kernel,
        out_shape=jax.ShapeDtypeStruct(mid.shape, jnp.float32),
        in_specs=[pl.BlockSpec(memory_space=SMEM)] + [pl.BlockSpec(memory_space=VMEM)] * 3,
        out_specs=pl.BlockSpec(memory_space=VMEM),
        compiler_params=pltpu.CompilerParams(vmem_limit_bytes=12 << 20),
        cost_estimate=pl.CostEstimate(flops=1 << 26, bytes_accessed=1 << 20, transcendentals=0),
        name="smooth",
    )(even, row_filter, mid, beyond)


def detect_kernel(even_ref, row_filter_ref, col_filter_ref, partial_ref, paired_ref, out_ref):
    cells, side, unused = partial_ref.shape
    edge = paired_ref.shape[1]
    above, below = row_filter_ref[:, :edge], row_filter_ref[:, edge + side :]
    outer = jnp.where(even_ref[0] != 0, below.astype(jnp.float32), above.astype(jnp.float32)).astype(jnp.bfloat16)
    zero = jnp.zeros((side, side), jnp.bfloat16)
    smoothed = [zero]
    for c in range(cells):
        rows = partial_ref[c] + jnp.dot(outer, paired_ref[c], preferred_element_type=jnp.float32)
        smoothed.append(rows.astype(jnp.bfloat16))
    smoothed.append(zero)
    for c in range(cells):
        window = jnp.concatenate(smoothed[c : c + 3], axis=1)
        out_ref[:, c * side : (c + 1) * side] = jnp.dot(
            window, col_filter_ref[...], preferred_element_type=jnp.float32
        )


def detect(even, row_filter, col_filter, partial, paired):
    cells, side, unused = partial.shape
    return pl.pallas_call(
        detect_kernel,
        out_shape=jax.ShapeDtypeStruct((side, cells * side), jnp.float32),
        in_specs=[pl.BlockSpec(memory_space=SMEM)] + [pl.BlockSpec(memory_space=VMEM)] * 4,
        out_specs=pl.BlockSpec(memory_space=VMEM),
        compiler_params=pltpu.CompilerParams(vmem_limit_bytes=12 << 20),
        name="detect",
    )(even, row_filter, col_filter, partial, paired)


def halves(parts, send):
    total = None
    for part in parts:
        half = part.shape[0] // 2
        piece = (part[half:] if send else part[:half]).astype(jnp.float32)
        total = piece if total is None else total + piece
    return total


def first_halves(parts):
    return [part[: part.shape[0] // 2] for part in parts]


def local(
    raw_blocks,
    patch_of_block,
    cell_of_block,
    band_of_block,
    block_weight,
    basis_coef,
    row_basis,
    col_basis,
    band_gain,
    filter_taps,
):
    sky_count = lax.axis_size("sky")
    band_count = lax.axis_size("band")
    sky_bits = sky_count.bit_length() - 1
    band_bits = band_count.bit_length() - 1
    margin_side = raw_blocks.shape[0]
    block_count = raw_blocks.shape[1] // margin_side
    radius = (filter_taps.shape[0] - 1) // 2
    block_side = margin_side - 2 * radius
    sky_here = lax.axis_index("sky")
    band_here = lax.axis_index("band")

    def swap(array, bit):
        axis, count, bit = ("band", band_count, bit) if bit < band_bits else ("sky", sky_count, bit - band_bits)
        return lax.ppermute(array, axis, [(i, i ^ (1 << bit)) for i in range(count)])

    band_bit, sky_bit, next_bit = 1, band_bits, band_bits + 1
    orders = [[band_bit, next_bit, sky_bit], [sky_bit, band_bit, next_bit]]
    later = list(range(2, band_bits)) + list(range(band_bits + 2, band_bits + sky_bits))
    heights = [block_side // len(orders)] * len(orders)

    own_facts, *loaded = load(
        patch_of_block.reshape(1, -1),
        cell_of_block.reshape(1, -1),
        band_of_block.reshape(1, -1),
        block_weight,
        row_basis,
        col_basis,
        basis_coef.T,
        raw_blocks,
        block_side,
    )
    facts = jnp.concatenate(
        [own_facts]
        + [lax.ppermute(own_facts, "band", [(i, i ^ off) for i in range(band_count)]) for off in range(1, band_count)]
    )
    cut, early = block_count // 2, block_count * 5 // 16
    own, others = [[], []], [[], []]
    begun = match_blocks(0, early, cut, loaded, heights, block_side, own_facts)
    for part in range(max(2, sky_bits)):
        got = swap(facts, band_bits + part) if part < sky_bits else None
        if part == 0:
            found = match_blocks(early, cut - early, cut, loaded, heights, block_side, facts, begun)
        elif part == 1:
            found = match_blocks(cut, block_count - cut, block_count - cut, loaded, heights, block_side, facts)
        if part < 2:
            for group, order in enumerate(orders):
                own[group].append(found[group])
                others[group].append(swap(found[group], order[0]))
        if got is not None and part < sky_bits - 1:
            facts = jnp.concatenate([facts, got])
        elif got is not None:
            last_facts = got

    near = jnp.stack([facts[0]] + [facts[1 << order[0]] for order in orders])
    near_key, near_weight = near[:, 0], near[:, 1]
    weight_sum, wanted = 0.0, near_key
    for part in (facts, last_facts):
        same = wanted[:, :, None, None] == part[None, None, :, 0]
        weight_sum = weight_sum + jnp.sum(jnp.where(same, part[None, None, :, 1], 0.0), axis=(2, 3))
        weight_sum, wanted = lax.optimization_barrier((weight_sum, wanted))
    near_key = near_key.astype(jnp.int32)
    cell = near_key % CELLS
    band = near_key // CELLS % BANDS
    gain = jnp.sum(jnp.where(band[..., None] == jnp.arange(BANDS), band_gain, 0.0), axis=2)
    scale = gain * near_weight / jnp.maximum(weight_sum, 1.0)

    owner_off = (near_key // (CELLS * BANDS) ^ sky_here) << band_bits | (cell // CC ^ band_here)
    size = (1 << (len(orders[0]) + len(later) - 1)) * CC
    half = size // 2
    blocks, bins, scales = [], [], []
    for group, order in enumerate(orders):
        blocks.append(own[group] + others[group])
        scales.append(jnp.stack([scale[0], scale[group + 1]]))
        off = jnp.stack([owner_off[0], owner_off[group + 1]])
        place = jnp.zeros_like(off)
        for bit in [0] + order[1:] + later:
            place = place * 2 + (off >> bit & 1)
        place = place * CC + jnp.stack([cell[0], cell[group + 1]]) % CC
        place = jnp.where(off >> order[0] & 1 == 0, place, -1)
        leaving = jnp.where(place >= size, place - size, jnp.where(place >= half, place - half + size, -1))
        bins.append([leaving, jnp.where(place < half, place, -1)])
    from_pair, sent = [], []
    for group, (lines, factor, parts) in enumerate(zip(bins, scales, blocks)):
        for_pair, for_next = bin_blocks(lines[0], factor, parts, (size, half), "bins_sent", others[1 - group][-1])
        from_pair.append(swap(for_pair, 0))
        sent.append(for_next)
    edge = up(radius, 16)
    taps = filter_taps.astype(jnp.bfloat16).astype(jnp.float32)[None]
    row_filter, col_filter = filters(taps, block_side, edge)
    groups = []
    for lines, factor, parts, order, mine, going in zip(bins, scales, blocks, orders, from_pair, sent):
        back = swap((going.astype(jnp.float32) + mine[half:].astype(jnp.float32)).astype(jnp.bfloat16), order[1])
        (kept,) = bin_blocks(lines[1], factor, parts, (half,), "bins_kept", row_filter)
        groups.append([kept, mine[:half], back])
    got = [swap(halves(parts, True).astype(jnp.bfloat16), order[2]) for parts, order in zip(groups, orders)]
    groups = [first_halves(parts) + [part] for parts, part in zip(groups, got)]
    joined = []
    for bit in later:
        outgoing = jnp.concatenate([halves(parts, True) for parts in groups], axis=1)
        for part in joined:
            outgoing = outgoing + part[part.shape[0] // 2 :].astype(jnp.float32)
        got = swap(outgoing.astype(jnp.bfloat16), bit)
        groups = [first_halves(parts) for parts in groups]
        joined = first_halves(joined) + [got]

    def full(parts):
        return functools.reduce(jnp.add, [part.astype(jnp.float32) for part in parts])

    combined = jnp.concatenate([full(parts) for parts in groups], axis=1)
    if joined:
        combined = combined + full(joined)
    combined = combined.astype(jnp.bfloat16)

    top, bottom = combined[:, :edge], combined[:, block_side - edge :]
    even = band_here & 1 == 0
    inner = [(i, i + 1) for i in range(1, band_count - 1, 2)]
    beyond = lax.ppermute(jnp.where(even, top, bottom), "band", inner + [(i, j) for j, i in inner])
    paired = swap(jnp.where(even, bottom, top), 0)
    side = even.astype(jnp.int32)[None]
    partial = smooth(side, row_filter, combined, beyond)
    return detect(side, row_filter, col_filter, partial, paired)[None]


def solution(mesh):
    return jax.shard_map(
        local,
        mesh=mesh,
        in_specs=(
            P(None, ("sky", "band")),
            P(("sky", "band"), None),
            P(("sky", "band")),
            P(("sky", "band")),
            P(("sky", "band")),
            P(("sky", "band"), None),
            P(),
            P(),
            P(),
            P(),
        ),
        out_specs=P("sky", "band", None),
        check_vma=False,
    )
```

```python
import functools

import jax
import jax.numpy as jnp
from jax import lax
from jax.experimental import pallas as pl
from jax.experimental.pallas import tpu as pltpu
from jax.sharding import PartitionSpec as P

BANDS = 6
CR = 4
CC = 4
CELLS = 16
VMEM = pltpu.VMEM
SMEM = pltpu.SMEM


def up(value, unit):
    return -(-value // unit) * unit


def banded(row, rows, width):
    tile = pltpu.roll(jnp.broadcast_to(row, (8, width)), 0, 1, stride=1, stride_axis=0)
    return jnp.concatenate([tile if i == 0 else pltpu.roll(tile, 8 * i, 1) for i in range(rows // 8)], axis=0)


def lanes_at(row, start, width):
    parts = [row, jnp.zeros((1, width - start - row.shape[1]), row.dtype)]
    if start:
        parts.insert(0, jnp.zeros((1, start), row.dtype))
    return jnp.concatenate(parts, axis=1)


def load_kernel(*refs):
    sources, (facts_ref, coef_ref, rowk_ref, colk_ref, raw_ref) = refs[:8], refs[8:13]
    patch_ref, cell_ref, band_ref, weight_ref, row_ref, col_ref, coef_in = targets = refs[13:20]
    sems = refs[20]
    copies = [
        pltpu.make_async_copy(source, target, sems.at[i])
        for i, (source, target) in enumerate(zip(sources, targets + (raw_ref,)))
    ]
    for copy in copies:
        copy.start()
    for copy in copies[:-1]:
        copy.wait()
    key = (patch_ref[...] * BANDS + band_ref[...]) * CELLS + cell_ref[...]
    facts_ref[0, 0:1, :] = key.astype(jnp.float32)
    facts_ref[0, 1:2, :] = weight_ref[...].astype(jnp.float32).reshape(1, -1)
    coef_ref[...] = coef_in[...].astype(jnp.float32)
    basis_count, margin_side = row_ref.shape[0], raw_ref.shape[0]
    block_side = rowk_ref.shape[0] // basis_count
    width = colk_ref.shape[0] // basis_count
    for k in range(basis_count):
        rows = banded(lanes_at(row_ref[k : k + 1, :], 0, width), block_side, width)
        rowk_ref[k * block_side : (k + 1) * block_side, :] = rows[:, :margin_side].astype(jnp.bfloat16)
        cols = banded(lanes_at(col_ref[k : k + 1, :], 0, width), block_side, width)
        colk_ref[k * width : (k + 1) * width, :] = cols.T.astype(jnp.bfloat16)
    copies[-1].wait()


def load(patch, cell, band, weight, row_basis, col_basis, coef, raw, block_side):
    basis_count = row_basis.shape[0]
    margin_side = raw.shape[0]
    width = up(margin_side, 128)
    operands = (patch, cell, band, weight, row_basis, col_basis, coef, raw)
    out_shape = [
        jax.ShapeDtypeStruct((1, 2, patch.shape[1]), jnp.float32),
        jax.ShapeDtypeStruct(coef.shape, jnp.float32),
        jax.ShapeDtypeStruct((basis_count * block_side, margin_side), jnp.bfloat16),
        jax.ShapeDtypeStruct((basis_count * width, block_side), jnp.bfloat16),
        jax.ShapeDtypeStruct(raw.shape, raw.dtype),
    ]
    return pl.pallas_call(
        load_kernel,
        out_shape=out_shape,
        in_specs=[pl.BlockSpec(memory_space=pltpu.HBM)] * len(operands),
        out_specs=[pl.BlockSpec(memory_space=VMEM)] * len(out_shape),
        scratch_shapes=[VMEM(value.shape, value.dtype) for value in operands[:-1]]
        + [pltpu.SemaphoreType.DMA((len(operands),))],
        compiler_params=pltpu.CompilerParams(vmem_limit_bytes=12 << 20),
        cost_estimate=pl.CostEstimate(flops=1 << 20, bytes_accessed=4 << 20, transcendentals=0),
        name="load",
    )(*(pltpu.with_memory_space_constraint(value, pltpu.HBM) for value in operands))


def match_kernel(first, count, skip, fresh, after_ref, coef_ref, rowk_ref, colk_ref, raw_ref, *outs):
    margin_side = raw_ref.shape[0]
    basis_count = coef_ref.shape[0]
    outs = outs if fresh else outs[len(outs) // 2 :]
    block_side = outs[0].shape[2]
    width = colk_ref.shape[0] // basis_count
    for n in range(count):
        here = first + n
        block = raw_ref[:, here * margin_side : (here + 1) * margin_side]
        sectioned = jnp.dot(rowk_ref[...], block, preferred_element_type=jnp.float32)
        total = None
        for k in range(basis_count):
            part = sectioned[k * block_side : (k + 1) * block_side] * coef_ref[k : k + 1, here : here + 1]
            term = jnp.dot(
                part.astype(jnp.bfloat16),
                colk_ref[k * width : k * width + margin_side, :],
                preferred_element_type=jnp.float32,
            )
            total = term if total is None else total + term
        total = total.astype(jnp.bfloat16)
        start = 0
        for out_ref in outs:
            out_ref[skip + n] = total[start : start + out_ref.shape[1]]
            start += out_ref.shape[1]


def match_blocks(first, count, size, loaded, rows, block_side, after, into=()):
    raw = loaded[-1]
    basis_count = loaded[0].shape[0]
    skip = first if into else 0
    flops = 2 * count * basis_count * block_side * raw.shape[0] * (raw.shape[0] + block_side)
    return pl.pallas_call(
        functools.partial(match_kernel, first, count, skip, not into),
        out_shape=[jax.ShapeDtypeStruct((size, height, block_side), jnp.bfloat16) for height in rows],
        in_specs=[pl.BlockSpec(memory_space=pl.ANY)] + [pl.BlockSpec(memory_space=VMEM)] * (len(loaded) + len(into)),
        out_specs=[pl.BlockSpec(memory_space=VMEM)] * len(rows),
        input_output_aliases={1 + len(loaded) + i: i for i in range(len(into))},
        compiler_params=pltpu.CompilerParams(vmem_limit_bytes=8 << 20),
        cost_estimate=pl.CostEstimate(flops=4 * flops, bytes_accessed=2 << 20, transcendentals=0),
        name="match_blocks",
    )(after, *loaded, *into)


def bin_kernel(stepped, sources, bins_ref, scale_ref, after_ref, *rest):
    blocks_refs, outs, acc_ref = rest[:sources], rest[sources:-1], rest[-1]
    parts = sources // 2
    step = acc_ref.shape[0]
    acc_ref[...] = jnp.zeros_like(acc_ref)
    for index, blocks_ref in enumerate(blocks_refs):
        line, part = index // parts, index % parts
        start = sum(ref.shape[0] for ref in blocks_refs[:part])
        for n in range(blocks_ref.shape[0]):
            slot = bins_ref[line, start + n]
            if stepped:
                slot = slot - pl.program_id(0) * step

            @pl.when((slot >= 0) & (slot < step) if stepped else slot >= 0)
            def _(blocks_ref=blocks_ref, n=n, slot=slot, line=line, place=start + n):
                acc_ref[slot] += scale_ref[line, place] * blocks_ref[n].astype(jnp.float32)

    low = 0
    for out_ref in outs:
        out_ref[...] = acc_ref[low : low + out_ref.shape[0]].astype(out_ref.dtype)
        low += out_ref.shape[0]


def bin_blocks(bins, scale, blocks, sizes, name, after):
    shape = blocks[0].shape[1:]
    size = sum(sizes)
    stepped = size > 64
    step = sizes[-1] if stepped else size
    while step > 64:
        step //= 2
    moved = 2 * sum(part.size for part in blocks) + 2 * size * shape[0] * shape[1]
    given = (size,) if stepped else sizes
    if stepped:
        grid = (size // step,)
        block_specs = [pl.BlockSpec(part.shape, lambda g: (0, 0, 0)) for part in blocks]
        out_specs = [pl.BlockSpec((step,) + shape, lambda g: (g, 0, 0))]
    else:
        grid = ()
        block_specs = [pl.BlockSpec(memory_space=VMEM)] * len(blocks)
        out_specs = [pl.BlockSpec(memory_space=VMEM)] * len(given)
    found = pl.pallas_call(
        functools.partial(bin_kernel, stepped, len(blocks)),
        grid=grid,
        out_shape=[jax.ShapeDtypeStruct((count,) + shape, jnp.bfloat16) for count in given],
        in_specs=[pl.BlockSpec(memory_space=SMEM), pl.BlockSpec(memory_space=SMEM), pl.BlockSpec(memory_space=pl.ANY)]
        + block_specs,
        out_specs=out_specs,
        scratch_shapes=[VMEM((step,) + shape, jnp.float32)],
        compiler_params=pltpu.CompilerParams(vmem_limit_bytes=20 << 20),
        cost_estimate=pl.CostEstimate(flops=2 * moved, bytes_accessed=moved, transcendentals=0),
        name=name,
    )(bins, scale, after, *blocks)
    if stepped:
        starts = [sum(sizes[:i]) for i in range(len(sizes))]
        found = [found[0][low : low + count] for low, count in zip(starts, sizes)]
    return found


def filters_kernel(edge, taps_ref, rows_ref, cols_ref):
    side, rows_in = rows_ref.shape
    radius = (taps_ref.shape[1] - 1) // 2
    taps = taps_ref[...]
    width = up(rows_in + 1, 128)
    rows_ref[...] = banded(lanes_at(taps, edge - radius, width), side, width)[:, :rows_in].astype(jnp.bfloat16)
    cols_ref[...] = banded(lanes_at(taps, side - radius, 3 * side), side, 3 * side).T.astype(jnp.bfloat16)


def filters(taps, side, edge):
    return pl.pallas_call(
        functools.partial(filters_kernel, edge),
        out_shape=[
            jax.ShapeDtypeStruct((side, side + 2 * edge), jnp.bfloat16),
            jax.ShapeDtypeStruct((3 * side, side), jnp.bfloat16),
        ],
        in_specs=[pl.BlockSpec(memory_space=VMEM)],
        out_specs=[pl.BlockSpec(memory_space=VMEM)] * 2,
        compiler_params=pltpu.CompilerParams(vmem_limit_bytes=12 << 20),
        cost_estimate=pl.CostEstimate(flops=1 << 20, bytes_accessed=1 << 20, transcendentals=0),
        name="filters",
    )(taps)


def smooth_kernel(even_ref, row_filter_ref, mid_ref, beyond_ref, out_ref):
    cells, side, unused = mid_ref.shape
    edge = beyond_ref.shape[1]
    above, below = row_filter_ref[:, :edge], row_filter_ref[:, edge + side :]
    outer = jnp.where(even_ref[0] != 0, above.astype(jnp.float32), below.astype(jnp.float32)).astype(jnp.bfloat16)
    for c in range(cells):
        out_ref[c] = jnp.dot(
            row_filter_ref[:, edge : edge + side], mid_ref[c], preferred_element_type=jnp.float32
        ) + jnp.dot(outer, beyond_ref[c], preferred_element_type=jnp.float32)


def smooth(even, row_filter, mid, beyond):
    return pl.pallas_call(
        smooth_kernel,
        out_shape=jax.ShapeDtypeStruct(mid.shape, jnp.float32),
        in_specs=[pl.BlockSpec(memory_space=SMEM)] + [pl.BlockSpec(memory_space=VMEM)] * 3,
        out_specs=pl.BlockSpec(memory_space=VMEM),
        compiler_params=pltpu.CompilerParams(vmem_limit_bytes=12 << 20),
        cost_estimate=pl.CostEstimate(flops=1 << 26, bytes_accessed=1 << 20, transcendentals=0),
        name="smooth",
    )(even, row_filter, mid, beyond)


def detect_kernel(even_ref, row_filter_ref, col_filter_ref, partial_ref, paired_ref, out_ref):
    cells, side, unused = partial_ref.shape
    edge = paired_ref.shape[1]
    above, below = row_filter_ref[:, :edge], row_filter_ref[:, edge + side :]
    outer = jnp.where(even_ref[0] != 0, below.astype(jnp.float32), above.astype(jnp.float32)).astype(jnp.bfloat16)
    zero = jnp.zeros((side, side), jnp.bfloat16)
    smoothed = [zero]
    for c in range(cells):
        rows = partial_ref[c] + jnp.dot(outer, paired_ref[c], preferred_element_type=jnp.float32)
        smoothed.append(rows.astype(jnp.bfloat16))
    smoothed.append(zero)
    for c in range(cells):
        window = jnp.concatenate(smoothed[c : c + 3], axis=1)
        out_ref[:, c * side : (c + 1) * side] = jnp.dot(
            window, col_filter_ref[...], preferred_element_type=jnp.float32
        )


def detect(even, row_filter, col_filter, partial, paired):
    cells, side, unused = partial.shape
    return pl.pallas_call(
        detect_kernel,
        out_shape=jax.ShapeDtypeStruct((side, cells * side), jnp.float32),
        in_specs=[pl.BlockSpec(memory_space=SMEM)] + [pl.BlockSpec(memory_space=VMEM)] * 4,
        out_specs=pl.BlockSpec(memory_space=VMEM),
        compiler_params=pltpu.CompilerParams(vmem_limit_bytes=12 << 20),
        name="detect",
    )(even, row_filter, col_filter, partial, paired)


def halves(parts, send):
    total = None
    for part in parts:
        half = part.shape[0] // 2
        piece = (part[half:] if send else part[:half]).astype(jnp.float32)
        total = piece if total is None else total + piece
    return total


def first_halves(parts):
    return [part[: part.shape[0] // 2] for part in parts]


def local(
    raw_blocks,
    patch_of_block,
    cell_of_block,
    band_of_block,
    block_weight,
    basis_coef,
    row_basis,
    col_basis,
    band_gain,
    filter_taps,
):
    sky_count = lax.axis_size("sky")
    band_count = lax.axis_size("band")
    sky_bits = sky_count.bit_length() - 1
    band_bits = band_count.bit_length() - 1
    margin_side = raw_blocks.shape[0]
    block_count = raw_blocks.shape[1] // margin_side
    radius = (filter_taps.shape[0] - 1) // 2
    block_side = margin_side - 2 * radius
    sky_here = lax.axis_index("sky")
    band_here = lax.axis_index("band")

    def swap(array, bit):
        axis, count, bit = ("band", band_count, bit) if bit < band_bits else ("sky", sky_count, bit - band_bits)
        return lax.ppermute(array, axis, [(i, i ^ (1 << bit)) for i in range(count)])

    band_bit, sky_bit, next_bit = 1, band_bits, band_bits + 1
    orders = [[band_bit, next_bit, sky_bit], [sky_bit, band_bit, next_bit]]
    later = list(range(2, band_bits)) + list(range(band_bits + 2, band_bits + sky_bits))
    heights = [block_side // len(orders)] * len(orders)

    own_facts, *loaded = load(
        patch_of_block.reshape(1, -1),
        cell_of_block.reshape(1, -1),
        band_of_block.reshape(1, -1),
        block_weight,
        row_basis,
        col_basis,
        basis_coef.T,
        raw_blocks,
        block_side,
    )
    cut = block_count // 2
    marks = [cut * i // (band_bits + 1) for i in range(band_bits + 2)]
    own, others = [[], []], [[], []]
    facts, found = own_facts, ()
    for bit in range(band_bits):
        got = swap(facts, bit)
        found = match_blocks(marks[bit], marks[bit + 1] - marks[bit], cut, loaded, heights, block_side, facts, found)
        facts = jnp.concatenate([facts, got])
    for part in range(max(2, sky_bits)):
        got = swap(facts, band_bits + part) if part < sky_bits else None
        if part == 0:
            first, last = marks[-2:]
            found = match_blocks(first, last - first, cut, loaded, heights, block_side, facts, found)
        elif part == 1:
            found = match_blocks(cut, block_count - cut, block_count - cut, loaded, heights, block_side, facts)
        if part < 2:
            for group, order in enumerate(orders):
                own[group].append(found[group])
                others[group].append(swap(found[group], order[0]))
        if got is not None:
            facts = jnp.concatenate([facts, got])

    near = jnp.stack([facts[0]] + [facts[1 << order[0]] for order in orders])
    near_key, near_weight = near[:, 0], near[:, 1]
    same = near_key[:, :, None, None] == facts[None, None, :, 0]
    weight_sum = jnp.sum(jnp.where(same, facts[None, None, :, 1], 0.0), axis=(2, 3))
    near_key = near_key.astype(jnp.int32)
    cell = near_key % CELLS
    band = near_key // CELLS % BANDS
    gain = jnp.sum(jnp.where(band[..., None] == jnp.arange(BANDS), band_gain, 0.0), axis=2)
    scale = gain * near_weight / jnp.maximum(weight_sum, 1.0)

    owner_off = (near_key // (CELLS * BANDS) ^ sky_here) << band_bits | (cell // CC ^ band_here)
    size = (1 << (len(orders[0]) + len(later) - 1)) * CC
    half = size // 2
    blocks, bins, scales = [], [], []
    for group, order in enumerate(orders):
        blocks.append(own[group] + others[group])
        scales.append(jnp.stack([scale[0], scale[group + 1]]))
        off = jnp.stack([owner_off[0], owner_off[group + 1]])
        place = jnp.zeros_like(off)
        for bit in [0] + order[1:] + later:
            place = place * 2 + (off >> bit & 1)
        place = place * CC + jnp.stack([cell[0], cell[group + 1]]) % CC
        place = jnp.where(off >> order[0] & 1 == 0, place, -1)
        leaving = jnp.where(place >= size, place - size, jnp.where(place >= half, place - half + size, -1))
        bins.append([leaving, jnp.where(place < half, place, -1)])
    from_pair, sent = [], []
    for group, (lines, factor, parts) in enumerate(zip(bins, scales, blocks)):
        for_pair, for_next = bin_blocks(lines[0], factor, parts, (size, half), "bins_sent", others[1 - group][-1])
        from_pair.append(swap(for_pair, 0))
        sent.append(for_next)
    edge = up(radius, 16)
    taps = filter_taps.astype(jnp.bfloat16).astype(jnp.float32)[None]
    row_filter, col_filter = filters(taps, block_side, edge)
    groups = []
    for lines, factor, parts, order, mine, going in zip(bins, scales, blocks, orders, from_pair, sent):
        back = swap((going.astype(jnp.float32) + mine[half:].astype(jnp.float32)).astype(jnp.bfloat16), order[1])
        (kept,) = bin_blocks(lines[1], factor, parts, (half,), "bins_kept", row_filter)
        groups.append([kept, mine[:half], back])
    got = [swap(halves(parts, True).astype(jnp.bfloat16), order[2]) for parts, order in zip(groups, orders)]
    groups = [first_halves(parts) + [part] for parts, part in zip(groups, got)]
    joined = []
    for bit in later:
        outgoing = jnp.concatenate([halves(parts, True) for parts in groups], axis=1)
        for part in joined:
            outgoing = outgoing + part[part.shape[0] // 2 :].astype(jnp.float32)
        got = swap(outgoing.astype(jnp.bfloat16), bit)
        groups = [first_halves(parts) for parts in groups]
        joined = first_halves(joined) + [got]

    def full(parts):
        return functools.reduce(jnp.add, [part.astype(jnp.float32) for part in parts])

    combined = jnp.concatenate([full(parts) for parts in groups], axis=1)
    if joined:
        combined = combined + full(joined)
    combined = combined.astype(jnp.bfloat16)

    top, bottom = combined[:, :edge], combined[:, block_side - edge :]
    even = band_here & 1 == 0
    inner = [(i, i + 1) for i in range(1, band_count - 1, 2)]
    beyond = lax.ppermute(jnp.where(even, top, bottom), "band", inner + [(i, j) for j, i in inner])
    paired = swap(jnp.where(even, bottom, top), 0)
    side = even.astype(jnp.int32)[None]
    partial = smooth(side, row_filter, combined, beyond)
    return detect(side, row_filter, col_filter, partial, paired)[None]


def solution(mesh):
    return jax.shard_map(
        local,
        mesh=mesh,
        in_specs=(
            P(None, ("sky", "band")),
            P(("sky", "band"), None),
            P(("sky", "band")),
            P(("sky", "band")),
            P(("sky", "band")),
            P(("sky", "band"), None),
            P(),
            P(),
            P(),
            P(),
        ),
        out_specs=P("sky", "band", None),
        check_vma=False,
    )
```

```python
import functools

import jax
import jax.numpy as jnp
from jax import lax
from jax.experimental import pallas as pl
from jax.experimental.pallas import tpu as pltpu
from jax.sharding import PartitionSpec as P

BANDS = 6
CR = 4
CC = 4
CELLS = 16
VMEM = pltpu.VMEM
SMEM = pltpu.SMEM


def up(value, unit):
    return -(-value // unit) * unit


def banded(row, rows, width):
    tile = pltpu.roll(jnp.broadcast_to(row, (8, width)), 0, 1, stride=1, stride_axis=0)
    return jnp.concatenate([tile if i == 0 else pltpu.roll(tile, 8 * i, 1) for i in range(rows // 8)], axis=0)


def lanes_at(row, start, width):
    parts = [row, jnp.zeros((1, width - start - row.shape[1]), row.dtype)]
    if start:
        parts.insert(0, jnp.zeros((1, start), row.dtype))
    return jnp.concatenate(parts, axis=1)


def load_kernel(*refs):
    sources, (facts_ref, coef_ref, rowk_ref, colk_ref, raw_ref) = refs[:8], refs[8:13]
    patch_ref, cell_ref, band_ref, weight_ref, row_ref, col_ref, coef_in = targets = refs[13:20]
    sems = refs[20]
    copies = [
        pltpu.make_async_copy(source, target, sems.at[i])
        for i, (source, target) in enumerate(zip(sources, targets + (raw_ref,)))
    ]
    for copy in copies:
        copy.start()
    for copy in copies[:-1]:
        copy.wait()
    key = (patch_ref[...] * BANDS + band_ref[...]) * CELLS + cell_ref[...]
    facts_ref[0, 0:1, :] = key.astype(jnp.float32)
    facts_ref[0, 1:2, :] = weight_ref[...].astype(jnp.float32).reshape(1, -1)
    coef_ref[...] = coef_in[...].astype(jnp.float32)
    basis_count, margin_side = row_ref.shape[0], raw_ref.shape[0]
    block_side = rowk_ref.shape[0] // basis_count
    width = colk_ref.shape[0] // basis_count
    for k in range(basis_count):
        rows = banded(lanes_at(row_ref[k : k + 1, :], 0, width), block_side, width)
        rowk_ref[k * block_side : (k + 1) * block_side, :] = rows[:, :margin_side].astype(jnp.bfloat16)
        cols = banded(lanes_at(col_ref[k : k + 1, :], 0, width), block_side, width)
        colk_ref[k * width : (k + 1) * width, :] = cols.T.astype(jnp.bfloat16)
    copies[-1].wait()


def load(patch, cell, band, weight, row_basis, col_basis, coef, raw, block_side):
    basis_count = row_basis.shape[0]
    margin_side = raw.shape[0]
    width = up(margin_side, 128)
    operands = (patch, cell, band, weight, row_basis, col_basis, coef, raw)
    out_shape = [
        jax.ShapeDtypeStruct((1, 2, patch.shape[1]), jnp.float32),
        jax.ShapeDtypeStruct(coef.shape, jnp.float32),
        jax.ShapeDtypeStruct((basis_count * block_side, margin_side), jnp.bfloat16),
        jax.ShapeDtypeStruct((basis_count * width, block_side), jnp.bfloat16),
        jax.ShapeDtypeStruct(raw.shape, raw.dtype),
    ]
    return pl.pallas_call(
        load_kernel,
        out_shape=out_shape,
        in_specs=[pl.BlockSpec(memory_space=pltpu.HBM)] * len(operands),
        out_specs=[pl.BlockSpec(memory_space=VMEM)] * len(out_shape),
        scratch_shapes=[VMEM(value.shape, value.dtype) for value in operands[:-1]]
        + [pltpu.SemaphoreType.DMA((len(operands),))],
        compiler_params=pltpu.CompilerParams(vmem_limit_bytes=12 << 20),
        cost_estimate=pl.CostEstimate(flops=1 << 20, bytes_accessed=4 << 20, transcendentals=0),
        name="load",
    )(*(pltpu.with_memory_space_constraint(value, pltpu.HBM) for value in operands))


def match_kernel(first, count, skip, fresh, after_ref, coef_ref, rowk_ref, colk_ref, raw_ref, *outs):
    margin_side = raw_ref.shape[0]
    basis_count = coef_ref.shape[0]
    outs = outs if fresh else outs[len(outs) // 2 :]
    block_side = outs[0].shape[2]
    width = colk_ref.shape[0] // basis_count
    for n in range(count):
        here = first + n
        block = raw_ref[:, here * margin_side : (here + 1) * margin_side]
        sectioned = jnp.dot(rowk_ref[...], block, preferred_element_type=jnp.float32)
        total = None
        for k in range(basis_count):
            part = sectioned[k * block_side : (k + 1) * block_side] * coef_ref[k : k + 1, here : here + 1]
            term = jnp.dot(
                part.astype(jnp.bfloat16),
                colk_ref[k * width : k * width + margin_side, :],
                preferred_element_type=jnp.float32,
            )
            total = term if total is None else total + term
        total = total.astype(jnp.bfloat16)
        start = 0
        for out_ref in outs:
            out_ref[skip + n] = total[start : start + out_ref.shape[1]]
            start += out_ref.shape[1]


def match_blocks(first, count, size, loaded, rows, block_side, after, into=()):
    raw = loaded[-1]
    basis_count = loaded[0].shape[0]
    skip = size - count if into else 0
    flops = 2 * count * basis_count * block_side * raw.shape[0] * (raw.shape[0] + block_side)
    return pl.pallas_call(
        functools.partial(match_kernel, first, count, skip, not into),
        out_shape=[jax.ShapeDtypeStruct((size, height, block_side), jnp.bfloat16) for height in rows],
        in_specs=[pl.BlockSpec(memory_space=pl.ANY)] + [pl.BlockSpec(memory_space=VMEM)] * (len(loaded) + len(into)),
        out_specs=[pl.BlockSpec(memory_space=VMEM)] * len(rows),
        input_output_aliases={1 + len(loaded) + i: i for i in range(len(into))},
        compiler_params=pltpu.CompilerParams(vmem_limit_bytes=8 << 20),
        cost_estimate=pl.CostEstimate(flops=4 * flops, bytes_accessed=2 << 20, transcendentals=0),
        name="match_blocks",
    )(after, *loaded, *into)


def bin_kernel(stepped, sources, bins_ref, scale_ref, after_ref, *rest):
    blocks_refs, outs, acc_ref = rest[:sources], rest[sources:-1], rest[-1]
    parts = sources // 2
    step = acc_ref.shape[0]
    acc_ref[...] = jnp.zeros_like(acc_ref)
    for index, blocks_ref in enumerate(blocks_refs):
        line, part = index // parts, index % parts
        start = sum(ref.shape[0] for ref in blocks_refs[:part])
        for n in range(blocks_ref.shape[0]):
            slot = bins_ref[line, start + n]
            if stepped:
                slot = slot - pl.program_id(0) * step

            @pl.when((slot >= 0) & (slot < step) if stepped else slot >= 0)
            def _(blocks_ref=blocks_ref, n=n, slot=slot, line=line, place=start + n):
                acc_ref[slot] += scale_ref[line, place] * blocks_ref[n].astype(jnp.float32)

    low = 0
    for out_ref in outs:
        out_ref[...] = acc_ref[low : low + out_ref.shape[0]].astype(out_ref.dtype)
        low += out_ref.shape[0]


def bin_blocks(bins, scale, blocks, sizes, name, after):
    shape = blocks[0].shape[1:]
    size = sum(sizes)
    stepped = size > 64
    step = sizes[-1] if stepped else size
    while step > 64:
        step //= 2
    moved = 2 * sum(part.size for part in blocks) + 2 * size * shape[0] * shape[1]
    given = (size,) if stepped else sizes
    if stepped:
        grid = (size // step,)
        block_specs = [pl.BlockSpec(part.shape, lambda g: (0, 0, 0)) for part in blocks]
        out_specs = [pl.BlockSpec((step,) + shape, lambda g: (g, 0, 0))]
    else:
        grid = ()
        block_specs = [pl.BlockSpec(memory_space=VMEM)] * len(blocks)
        out_specs = [pl.BlockSpec(memory_space=VMEM)] * len(given)
    found = pl.pallas_call(
        functools.partial(bin_kernel, stepped, len(blocks)),
        grid=grid,
        out_shape=[jax.ShapeDtypeStruct((count,) + shape, jnp.bfloat16) for count in given],
        in_specs=[pl.BlockSpec(memory_space=SMEM), pl.BlockSpec(memory_space=SMEM), pl.BlockSpec(memory_space=pl.ANY)]
        + block_specs,
        out_specs=out_specs,
        scratch_shapes=[VMEM((step,) + shape, jnp.float32)],
        compiler_params=pltpu.CompilerParams(vmem_limit_bytes=20 << 20),
        cost_estimate=pl.CostEstimate(flops=2 * moved, bytes_accessed=moved, transcendentals=0),
        name=name,
    )(bins, scale, after, *blocks)
    if stepped:
        starts = [sum(sizes[:i]) for i in range(len(sizes))]
        found = [found[0][low : low + count] for low, count in zip(starts, sizes)]
    return found


def filters_kernel(edge, taps_ref, rows_ref, cols_ref):
    side, rows_in = rows_ref.shape
    radius = (taps_ref.shape[1] - 1) // 2
    taps = taps_ref[...]
    width = up(rows_in + 1, 128)
    rows_ref[...] = banded(lanes_at(taps, edge - radius, width), side, width)[:, :rows_in].astype(jnp.bfloat16)
    cols_ref[...] = banded(lanes_at(taps, side - radius, 3 * side), side, 3 * side).T.astype(jnp.bfloat16)


def filters(taps, side, edge):
    return pl.pallas_call(
        functools.partial(filters_kernel, edge),
        out_shape=[
            jax.ShapeDtypeStruct((side, side + 2 * edge), jnp.bfloat16),
            jax.ShapeDtypeStruct((3 * side, side), jnp.bfloat16),
        ],
        in_specs=[pl.BlockSpec(memory_space=VMEM)],
        out_specs=[pl.BlockSpec(memory_space=VMEM)] * 2,
        compiler_params=pltpu.CompilerParams(vmem_limit_bytes=12 << 20),
        cost_estimate=pl.CostEstimate(flops=1 << 20, bytes_accessed=1 << 20, transcendentals=0),
        name="filters",
    )(taps)


def smooth_kernel(even_ref, row_filter_ref, mid_ref, beyond_ref, out_ref):
    cells, side, unused = mid_ref.shape
    edge = beyond_ref.shape[1]
    above, below = row_filter_ref[:, :edge], row_filter_ref[:, edge + side :]
    outer = jnp.where(even_ref[0] != 0, above.astype(jnp.float32), below.astype(jnp.float32)).astype(jnp.bfloat16)
    for c in range(cells):
        out_ref[c] = jnp.dot(
            row_filter_ref[:, edge : edge + side], mid_ref[c], preferred_element_type=jnp.float32
        ) + jnp.dot(outer, beyond_ref[c], preferred_element_type=jnp.float32)


def smooth(even, row_filter, mid, beyond):
    return pl.pallas_call(
        smooth_kernel,
        out_shape=jax.ShapeDtypeStruct(mid.shape, jnp.float32),
        in_specs=[pl.BlockSpec(memory_space=SMEM)] + [pl.BlockSpec(memory_space=VMEM)] * 3,
        out_specs=pl.BlockSpec(memory_space=VMEM),
        compiler_params=pltpu.CompilerParams(vmem_limit_bytes=12 << 20),
        cost_estimate=pl.CostEstimate(flops=1 << 26, bytes_accessed=1 << 20, transcendentals=0),
        name="smooth",
    )(even, row_filter, mid, beyond)


def detect_kernel(even_ref, row_filter_ref, col_filter_ref, partial_ref, paired_ref, out_ref):
    cells, side, unused = partial_ref.shape
    edge = paired_ref.shape[1]
    above, below = row_filter_ref[:, :edge], row_filter_ref[:, edge + side :]
    outer = jnp.where(even_ref[0] != 0, below.astype(jnp.float32), above.astype(jnp.float32)).astype(jnp.bfloat16)
    zero = jnp.zeros((side, side), jnp.bfloat16)
    smoothed = [zero]
    for c in range(cells):
        rows = partial_ref[c] + jnp.dot(outer, paired_ref[c], preferred_element_type=jnp.float32)
        smoothed.append(rows.astype(jnp.bfloat16))
    smoothed.append(zero)
    for c in range(cells):
        window = jnp.concatenate(smoothed[c : c + 3], axis=1)
        out_ref[:, c * side : (c + 1) * side] = jnp.dot(
            window, col_filter_ref[...], preferred_element_type=jnp.float32
        )


def detect(even, row_filter, col_filter, partial, paired):
    cells, side, unused = partial.shape
    return pl.pallas_call(
        detect_kernel,
        out_shape=jax.ShapeDtypeStruct((side, cells * side), jnp.float32),
        in_specs=[pl.BlockSpec(memory_space=SMEM)] + [pl.BlockSpec(memory_space=VMEM)] * 4,
        out_specs=pl.BlockSpec(memory_space=VMEM),
        compiler_params=pltpu.CompilerParams(vmem_limit_bytes=12 << 20),
        name="detect",
    )(even, row_filter, col_filter, partial, paired)


def halves(parts, send):
    total = None
    for part in parts:
        half = part.shape[0] // 2
        piece = (part[half:] if send else part[:half]).astype(jnp.float32)
        total = piece if total is None else total + piece
    return total


def first_halves(parts):
    return [part[: part.shape[0] // 2] for part in parts]


def local(
    raw_blocks,
    patch_of_block,
    cell_of_block,
    band_of_block,
    block_weight,
    basis_coef,
    row_basis,
    col_basis,
    band_gain,
    filter_taps,
):
    sky_count = lax.axis_size("sky")
    band_count = lax.axis_size("band")
    sky_bits = sky_count.bit_length() - 1
    band_bits = band_count.bit_length() - 1
    margin_side = raw_blocks.shape[0]
    block_count = raw_blocks.shape[1] // margin_side
    radius = (filter_taps.shape[0] - 1) // 2
    block_side = margin_side - 2 * radius
    sky_here = lax.axis_index("sky")
    band_here = lax.axis_index("band")

    def swap(array, bit):
        axis, count, bit = ("band", band_count, bit) if bit < band_bits else ("sky", sky_count, bit - band_bits)
        return lax.ppermute(array, axis, [(i, i ^ (1 << bit)) for i in range(count)])

    band_bit, sky_bit, next_bit = 1, band_bits, band_bits + 1
    orders = [[band_bit, next_bit, sky_bit], [sky_bit, band_bit, next_bit]]
    later = list(range(2, band_bits)) + list(range(band_bits + 2, band_bits + sky_bits))
    heights = [block_side // len(orders)] * len(orders)

    own_facts, *loaded = load(
        patch_of_block.reshape(1, -1),
        cell_of_block.reshape(1, -1),
        band_of_block.reshape(1, -1),
        block_weight,
        row_basis,
        col_basis,
        basis_coef.T,
        raw_blocks,
        block_side,
    )
    facts = jnp.concatenate(
        [own_facts]
        + [lax.ppermute(own_facts, "band", [(i, i ^ off) for i in range(band_count)]) for off in range(1, band_count)]
    )
    cut, early = block_count // 2, block_count // 4
    own, others = [[], []], [[], []]
    begun = match_blocks(0, early, cut, loaded, heights, block_side, own_facts)
    for part in range(max(2, sky_bits)):
        got = swap(facts, band_bits + part) if part < sky_bits else None
        if part == 0:
            found = match_blocks(early, cut - early, cut, loaded, heights, block_side, facts, begun)
        elif part == 1:
            found = match_blocks(cut, block_count - cut, block_count - cut, loaded, heights, block_side, facts)
        if part < 2:
            for group, order in enumerate(orders):
                own[group].append(found[group])
                others[group].append(swap(found[group], order[0]))
        if got is not None:
            facts = jnp.concatenate([facts, got])

    near = jnp.stack([facts[0]] + [facts[1 << order[0]] for order in orders])
    near_key, near_weight = near[:, 0], near[:, 1]
    same = near_key[:, :, None, None] == facts[None, None, :, 0]
    weight_sum = jnp.sum(jnp.where(same, facts[None, None, :, 1], 0.0), axis=(2, 3))
    near_key = near_key.astype(jnp.int32)
    cell = near_key % CELLS
    band = near_key // CELLS % BANDS
    gain = jnp.sum(jnp.where(band[..., None] == jnp.arange(BANDS), band_gain, 0.0), axis=2)
    scale = gain * near_weight / jnp.maximum(weight_sum, 1.0)

    owner_off = (near_key // (CELLS * BANDS) ^ sky_here) << band_bits | (cell // CC ^ band_here)
    size = (1 << (len(orders[0]) + len(later) - 1)) * CC
    half = size // 2
    blocks, bins, scales = [], [], []
    for group, order in enumerate(orders):
        blocks.append(own[group] + others[group])
        scales.append(jnp.stack([scale[0], scale[group + 1]]))
        off = jnp.stack([owner_off[0], owner_off[group + 1]])
        place = jnp.zeros_like(off)
        for bit in [0] + order[1:] + later:
            place = place * 2 + (off >> bit & 1)
        place = place * CC + jnp.stack([cell[0], cell[group + 1]]) % CC
        place = jnp.where(off >> order[0] & 1 == 0, place, -1)
        leaving = jnp.where(place >= size, place - size, jnp.where(place >= half, place - half + size, -1))
        bins.append([leaving, jnp.where(place < half, place, -1)])
    from_pair, sent = [], []
    for group, (lines, factor, parts) in enumerate(zip(bins, scales, blocks)):
        for_pair, for_next = bin_blocks(lines[0], factor, parts, (size, half), "bins_sent", others[1 - group][-1])
        from_pair.append(swap(for_pair, 0))
        sent.append(for_next)
    edge = up(radius, 16)
    taps = filter_taps.astype(jnp.bfloat16).astype(jnp.float32)[None]
    row_filter, col_filter = filters(taps, block_side, edge)
    groups = []
    for lines, factor, parts, order, mine, going in zip(bins, scales, blocks, orders, from_pair, sent):
        back = swap((going.astype(jnp.float32) + mine[half:].astype(jnp.float32)).astype(jnp.bfloat16), order[1])
        (kept,) = bin_blocks(lines[1], factor, parts, (half,), "bins_kept", row_filter)
        groups.append([kept, mine[:half], back])
    got = [swap(halves(parts, True).astype(jnp.bfloat16), order[2]) for parts, order in zip(groups, orders)]
    groups = [first_halves(parts) + [part] for parts, part in zip(groups, got)]
    joined = []
    for bit in later:
        outgoing = jnp.concatenate([halves(parts, True) for parts in groups], axis=1)
        for part in joined:
            outgoing = outgoing + part[part.shape[0] // 2 :].astype(jnp.float32)
        got = swap(outgoing.astype(jnp.bfloat16), bit)
        groups = [first_halves(parts) for parts in groups]
        joined = first_halves(joined) + [got]

    def full(parts):
        return functools.reduce(jnp.add, [part.astype(jnp.float32) for part in parts])

    combined = jnp.concatenate([full(parts) for parts in groups], axis=1)
    if joined:
        combined = combined + full(joined)
    combined = combined.astype(jnp.bfloat16)

    top, bottom = combined[:, :edge], combined[:, block_side - edge :]
    even = band_here & 1 == 0
    inner = [(i, i + 1) for i in range(1, band_count - 1, 2)]
    beyond = lax.ppermute(jnp.where(even, top, bottom), "band", inner + [(i, j) for j, i in inner])
    paired = swap(jnp.where(even, bottom, top), 0)
    side = even.astype(jnp.int32)[None]
    partial = smooth(side, row_filter, combined, beyond)
    return detect(side, row_filter, col_filter, partial, paired)[None]


def solution(mesh):
    return jax.shard_map(
        local,
        mesh=mesh,
        in_specs=(
            P(None, ("sky", "band")),
            P(("sky", "band"), None),
            P(("sky", "band")),
            P(("sky", "band")),
            P(("sky", "band")),
            P(("sky", "band"), None),
            P(),
            P(),
            P(),
            P(),
        ),
        out_specs=P("sky", "band", None),
        check_vma=False,
    )
```
